512 devices in a mesh: dp: 16 (over x, z_lo), tensor: 32 (over z_hi, y, core).
Axes of the slice: x: 4, y: 4, z: 16 (z_hi: 4, z_lo: 4; z = z_hi * 4 + z_lo), core: 2. Of those that a mesh axis runs over, the one named last changes fastest.
Arguments:
- layer_input: bfloat16 [16, 192, 4096], P('dp', None, 'tensor'), may hold values from -15 to 15
- frame_mask: int32 [16, 192], P('dp'), may hold values 0 or 1
- w_qkv: bfloat16 [3, 4096, 4096], P(None, None, 'tensor'), may hold values from -0.09375 to 0.09375
- w_out: bfloat16 [4096, 4096], P('tensor'), may hold values from -0.5 to 0.5
- w_in: bfloat16 [4096, 1024], P('tensor'), may hold values from -0.09375 to 0.09375
- step_embed: bfloat16 [17, 1024], replicated, may hold values from -6 to 6
- depth_gain: bfloat16 [1024], replicated, may hold values from 0.5 to 1.5
- cotangent: bfloat16 [16, 192, 17, 1024], P('dp', 'tensor'), may hold values from -6 to 6
Outputs:
- grad_x: bfloat16 [16, 192, 4096], P('dp', None, 'tensor')
- grad_w_in: bfloat16 [4096, 1024], P('tensor')
- grad_step_embed: float32 [17, 1024], replicated
- grad_gain: float32 [1024], replicated
The draws below stay inside these ranges and needn't reach their ends.
All inputs are finite; a program needn't handle non-finite values. No bound on the sum of `frame_mask` on one device may be relied on, other than what follows from the above.
Results may differ from the reference program's by a relative error of at most 0.03.
Values may be sent and summed in bfloat16 or wider, within the bound.
A program may use at most 64 MiB of HBM per device.

```python
import jax
import jax.numpy as jnp
from jax import lax

D = 4096
HD = 128
DD = 1024
STEPS = 17
FRAMES = 192
H = 32
DIALOGUES = 16
N_TENSOR = 32


def draw_layer_input(key, part):
    key = jax.random.fold_in(key, 11)
    array_shape = (DIALOGUES, FRAMES, D)
    values = jax.random.truncated_normal(key, -4.0, 4.0, array_shape, jnp.float32)
    return values.astype(jnp.bfloat16)


def draw_w_qkv(key, part):
    key = jax.random.fold_in(key, 23)
    factor = D ** (-0.5)
    first_key = jax.random.fold_in(key, 0)
    stacked = jax.random.truncated_normal(first_key, -4.0, 4.0, (3, D, H * HD), jnp.float32)
    return (stacked * factor).astype(jnp.bfloat16)


def plant(values, own_key, smallest, largest):
    longest = values.shape.index(max(values.shape))
    spots = []
    for shift in (0, 1):
        where = [jax.random.randint(jax.random.fold_in(own_key, axis), (), 0, length) for axis, length in enumerate(values.shape)]
        where[longest] = (where[longest] + shift) % values.shape[longest]
        spots.append(tuple(where))
    return values.at[spots[0]].set(smallest).at[spots[1]].set(largest)


def steps_of(key, dims, cuts, least, largest):
    def one(dim, blocks):
        draws = jax.random.uniform(jax.random.fold_in(jax.random.fold_in(key, 6), dim), (blocks,), jnp.float32, least / len(cuts), largest / len(cuts))
        return jnp.repeat(jnp.exp(draws), dims[dim] // blocks).reshape((-1,) + (1,) * (len(dims) - dim - 1))

    loudness = one(*cuts[0])
    for cut in cuts[1:]:
        loudness = loudness * one(*cut)
    return loudness


def gaussian(key, dims, scale, bound, cuts=(), kind=jnp.bfloat16):
    result = scale * jax.random.normal(key, dims, jnp.float32)
    if cuts:
        result = result * steps_of(key, dims, cuts, -0.22, 0.18)
    return jnp.clip(result, -bound, bound).astype(kind)


def setup_inputs(seed: int = 0) -> dict:
    streams_of = jax.random.split(jax.random.key(seed), 9)
    layer_input = draw_layer_input(jax.random.fold_in(streams_of[8], 71), 0)
    frame_mask = plant((jax.random.randint(streams_of[1], (DIALOGUES, FRAMES), 0, 8) < 7).astype(jnp.int32), jax.random.fold_in(streams_of[1], 1), 0, 1)
    w_qkv = draw_w_qkv(jax.random.fold_in(streams_of[8], 71), 0)
    w_out = gaussian(streams_of[3], (H * HD, D), HD ** -0.5, 0.5, ((0, 32),))
    w_in = gaussian(streams_of[4], (D, DD), D ** -0.5, 0.09375, ((0, 32),))
    step_embed = gaussian(streams_of[5], (STEPS, DD), 1.0, 6.0)
    depth_gain = jnp.clip(1.0 + 0.1 * jax.random.normal(streams_of[6], (DD,), jnp.float32), 0.5, 1.5).astype(jnp.bfloat16)
    cotangent = gaussian(streams_of[7], (DIALOGUES, FRAMES, STEPS, DD), 1.0, 6.0, ((0, 16), (1, 32)))
    return {"layer_input": layer_input, "frame_mask": frame_mask, "w_qkv": w_qkv, "w_out": w_out, "w_in": w_in, "step_embed": step_embed, "depth_gain": depth_gain, "cotangent": cotangent}


def permitted(mask):
    length = mask.shape[0]
    rows = jnp.arange(length)[:, None]
    cols = jnp.arange(length)[None, :]
    return (cols <= rows) & ((mask[None, :] == 1) | (cols == rows))

def round_trip(value):
    return lax.optimization_barrier(value.astype(jnp.bfloat16)).astype(jnp.float32)

def attend(query, key_rows, value, allowed):
    scores = jnp.dot(query, key_rows.T, preferred_element_type=jnp.float32) * HD ** (-0.5)
    scores = jnp.where(allowed, scores, -1e+30)
    probs = jax.nn.softmax(scores, axis=-1)
    rounded = probs.astype(jnp.bfloat16)
    heads = jnp.dot(rounded, value, preferred_element_type=jnp.float32).astype(jnp.bfloat16)
    return (heads, probs, rounded)

def attend_back(grad_heads, query, key_rows, value, probs, rounded):
    grad_probs = jnp.dot(grad_heads, value.T, preferred_element_type=jnp.float32)
    grad_scores = probs * (grad_probs - lax.optimization_barrier(jnp.sum(probs * grad_probs, axis=-1, keepdims=True))) * HD ** (-0.5)
    grad_scores = grad_scores.astype(jnp.bfloat16)
    grad_value = jnp.dot(rounded.T, grad_heads, preferred_element_type=jnp.float32).astype(jnp.bfloat16)
    grad_query = jnp.dot(grad_scores, key_rows, preferred_element_type=jnp.float32).astype(jnp.bfloat16)
    grad_key = jnp.dot(grad_scores.T, query, preferred_element_type=jnp.float32).astype(jnp.bfloat16)
    return (grad_query, grad_key, grad_value)

def norm_back(proj, step_embed, depth_gain, cotangent):
    inner = proj[:, None, :] + step_embed.astype(jnp.float32)[None]
    inverse = lax.rsqrt(lax.optimization_barrier(jnp.mean(inner * inner, axis=-1, keepdims=True)) + 1e-06)
    arriving = cotangent.astype(jnp.float32)
    grad_gain = lax.optimization_barrier(jnp.sum(arriving * inner * inverse, axis=(0, 1)))
    scaled = arriving * depth_gain.astype(jnp.float32)
    grad_inner = inverse * scaled - inverse ** 3 * inner * lax.optimization_barrier(jnp.mean(inner * scaled, axis=-1, keepdims=True))
    return (grad_inner, grad_gain)

def one_dialogue(inputs, mask, cotangent, w_qkv, w_out, w_in, step_embed, depth_gain):
    length = inputs.shape[0]
    allowed = permitted(mask)
    head_qkv = w_qkv.reshape(3, D, H, HD).transpose(2, 0, 1, 3)
    head_out = w_out.reshape(H, HD, D)

    def forward(total, weights):
        triple, outward = weights
        query = jnp.dot(inputs, triple[0], preferred_element_type=jnp.float32).astype(jnp.bfloat16)
        key_rows = jnp.dot(inputs, triple[1], preferred_element_type=jnp.float32).astype(jnp.bfloat16)
        value = jnp.dot(inputs, triple[2], preferred_element_type=jnp.float32).astype(jnp.bfloat16)
        heads, probs, rounded = attend(query, key_rows, value, allowed)
        total = total + round_trip(jnp.dot(heads, outward, preferred_element_type=jnp.float32))
        return (total, (query, key_rows, value))
    total, saved = lax.scan(forward, jnp.zeros((length, D), jnp.float32), (head_qkv, head_out))
    hidden = (inputs.astype(jnp.float32) + total).astype(jnp.bfloat16)
    blocks = hidden.reshape(length, N_TENSOR, D // N_TENSOR).astype(jnp.float32)
    weight_blocks = w_in.reshape(N_TENSOR, D // N_TENSOR, DD).astype(jnp.float32)
    terms = jnp.einsum('lbc,bcd->bld', blocks, weight_blocks)
    proj = lax.optimization_barrier(jnp.sum(round_trip(terms), axis=0))
    grad_inner, grad_gain = norm_back(proj, step_embed, depth_gain, cotangent)
    grad_step = lax.optimization_barrier(jnp.sum(grad_inner, axis=0))
    grad_proj = lax.optimization_barrier(jnp.sum(grad_inner, axis=1)).astype(jnp.bfloat16)
    grad_in = jnp.dot(hidden.T, grad_proj, preferred_element_type=jnp.float32)
    grad_hidden = jnp.dot(grad_proj, w_in.T, preferred_element_type=jnp.float32).astype(jnp.bfloat16)

    def backward(total, items):
        triple, outward, query, key_rows, value = items
        heads, probs, rounded = attend(query, key_rows, value, allowed)
        grad_heads = jnp.dot(grad_hidden, outward.T, preferred_element_type=jnp.float32).astype(jnp.bfloat16)
        grad_query, grad_key, grad_value = attend_back(grad_heads, query, key_rows, value, probs, rounded)
        term = jnp.dot(grad_query, triple[0].T, preferred_element_type=jnp.float32)
        term = term + jnp.dot(grad_key, triple[1].T, preferred_element_type=jnp.float32)
        term = term + jnp.dot(grad_value, triple[2].T, preferred_element_type=jnp.float32)
        return (total + round_trip(term), None)
    total_back, unused = lax.scan(backward, jnp.zeros((length, D), jnp.float32), (head_qkv, head_out) + saved)
    grad_x = (grad_hidden.astype(jnp.float32) + total_back).astype(jnp.bfloat16)
    return (grad_x, grad_in, grad_step, grad_gain)

def reference(layer_input, frame_mask, w_qkv, w_out, w_in, step_embed, depth_gain, cotangent):

    def dialogue_step(carry, items):
        input_rows, mask_rows, arriving = items
        grad_x, grad_in, grad_step, grad_gain = one_dialogue(input_rows, mask_rows, arriving, w_qkv, w_out, w_in, step_embed, depth_gain)
        return ((carry[0] + grad_in, carry[1] + grad_step, carry[2] + grad_gain), grad_x)
    start = (jnp.zeros((D, DD), jnp.float32), jnp.zeros((STEPS, DD), jnp.float32), jnp.zeros((DD,), jnp.float32))
    sums, grad_x = lax.scan(dialogue_step, start, (layer_input, frame_mask, cotangent))
    return (grad_x, sums[0].astype(jnp.bfloat16), sums[1], sums[2])
```

```python
import functools

import jax
import jax.numpy as jnp
from jax import lax
from jax.experimental import pallas as pl
from jax.experimental.pallas import tpu as pltpu
from jax.sharding import PartitionSpec as P

MESH = pl.DeviceIdType.MESH
F32 = jnp.float32
BF16 = jnp.bfloat16
L, HD, DD, STEPS, FR = 192, 128, 1024, 17, 6
HALF = L // 2
LO, HI = pl.ds(0, HALF), pl.ds(HALF, HALF)
ROWS = FR * (DD // HD)
PIECE = 64
N_SEM = 200


def nt(a, b):
    return lax.dot_general(a, b, (((1,), (1,)), ((), ())), preferred_element_type=F32)


def nn(a, b):
    return lax.dot_general(a, b, (((1,), (0,)), ((), ())), preferred_element_type=F32)


def tn(a, b):
    return lax.dot_general(a, b, (((0,), (0,)), ((), ())), preferred_element_type=F32)


def around(v):
    return (v + 1) % 4, (v + 3) % 4, (v + 2) % 4


class Net:
    def __init__(self, send_sems, recv_sems):
        self.send_sems, self.recv_sems = send_sems, recv_sems
        self.count = 0
        self.open = []
        dp, t = lax.axis_index("dp"), lax.axis_index("tensor")
        self.dp, self.t = dp, t
        self.x, self.zl = dp // 4, dp % 4
        self.z, self.y, self.c = t // 8, (t // 2) % 4, t % 2

    def go(self, z=0, y=0, c=0, x=0, zl=0):
        dp, t = self.dp, self.t
        if x or zl:
            dp = ((self.x + x) % 4) * 4 + (self.zl + zl) % 4
        if z or y or c:
            cc = (self.c + c) % 2
            t = ((self.z + z) % 4) * 8 + ((self.y + y) % 4) * 2 + cc
        return (dp, t)

    def peers(self):
        found = [self.go(c=1)]
        for d in (1, 2, 3):
            found += [self.go(y=d), self.go(z=d), self.go(x=d), self.go(zl=d)]
        return found

    def make(self, src, dst, peer):
        i = self.count
        self.count += 1
        return pltpu.make_async_remote_copy(
            src_ref=src,
            dst_ref=dst,
            send_sem=self.send_sems.at[i],
            recv_sem=self.recv_sems.at[i],
            device_id=peer,
            device_id_type=MESH,
        )

    def send(self, src, dst, peer):
        copy = self.make(src, dst, peer)
        copy.start()
        self.open.append(copy)
        return copy

    def drain(self):
        for copy in self.open:
            copy.wait_send()
        self.open = []


class Gather:
    def __init__(self, net, g):
        self.net, self.g = net, g
        self.planes = (net.z, around(net.z)[1], around(net.z)[0], around(net.z)[2])
        self.along, self.forward, self.across = {}, {}, {}
        self.to_yp, self.to_ym, self.to_c = net.go(y=1), net.go(y=3), net.go(c=1)

    def whole(self, zz, yy, peer):
        at = self.g.at[zz, yy, self.net.c]
        return self.net.send(at, at, peer)

    def part(self, zz, yy, rows, peer):
        at = self.g.at[zz, yy, self.net.c, rows]
        return self.net.send(at, at, peer)

    def begin(self):
        z, y = self.net.z, self.net.y
        to_zp, to_zm = self.net.go(z=1), self.net.go(z=3)
        self.up_lo = self.part(z, y, LO, to_zp)
        self.dn_hi = self.part(z, y, HI, to_zm)
        self.up_hi = self.part(z, y, HI, to_zp)
        self.dn_lo = self.part(z, y, LO, to_zm)
        self.spread(0)

    def along_z(self):
        y = self.net.y
        to_zp, to_zm = self.net.go(z=1), self.net.go(z=3)
        self.up_lo.wait_recv()
        self.on = self.part(self.planes[1], y, LO, to_zp)
        self.dn_hi.wait_recv()
        self.back = self.part(self.planes[2], y, HI, to_zm)
        self.up_hi.wait_recv()
        self.spread(1)
        self.dn_lo.wait_recv()
        self.spread(2)

    def far_z(self):
        self.on.wait_recv()
        self.back.wait_recv()
        self.spread(3)

    def spread(self, i):
        zz, y = self.planes[i], self.net.y
        self.along[i] = (self.whole(zz, y, self.to_yp), self.whole(zz, y, self.to_ym))
        self.across[i] = []
        self.over(i, zz, y)

    def over(self, i, zz, yy):
        if i == 3:
            self.across[i].append(self.whole(zz, yy, self.to_c))

    def turn(self, i):
        zz = self.planes[i]
        yp, ym, _ = around(self.net.y)
        self.along[i][0].wait_recv()
        first = self.part(zz, ym, LO, self.to_yp)
        self.over(i, zz, ym)
        self.along[i][1].wait_recv()
        second = self.part(zz, yp, HI, self.to_ym)
        self.over(i, zz, yp)
        self.forward[i] = (first, second)

    def land(self, i):
        for copy in self.forward[i]:
            copy.wait_recv()
        self.over(i, self.planes[i], around(self.net.y)[2])
        if i < 3:
            at = self.g.at[self.planes[i], pl.ds(0, 4), self.net.c]
            self.across[i].append(self.net.send(at, at, self.to_c))

    def here(self, i):
        for copy in self.across[i]:
            copy.wait_recv()


def scatter_ring(net, p, fill, bufs, done, early=False):
    ya, yb, yup, ydn, q, za, zb, zup, zdn = bufs
    z, y = net.z, net.y
    zp, zm, z2 = around(z)
    yp, ym, y2 = around(y)
    to_zp, to_zm, to_yp, to_ym = net.go(z=1), net.go(z=3), net.go(y=1), net.go(y=3)
    order = (z2, zp, zm, z)

    pairs = (order[:2], order[2:])
    if early:
        for yy in (y2, yp, ym, y):
            for pair in pairs:
                fill(yy, pair)
        yield
    far = []
    for pair in pairs:
        if not early:
            fill(y2, pair)
        for zz in pair:
            far.append(
                (
                    net.send(p.at[zz, y2, LO], ya.at[zz], to_yp),
                    net.send(p.at[zz, y2, HI], yb.at[zz], to_ym),
                )
            )
    yield
    if not early:
        for pair in pairs:
            fill(yp, pair)
            fill(ym, pair)
        yield
    near = []
    for i, zz in enumerate(order):
        far[i][0].wait_recv()
        p[zz, yp, LO] = (p[zz, yp, LO].astype(F32) + ya[zz].astype(F32)).astype(BF16)
        up = net.send(p.at[zz, yp], yup.at[zz], to_yp)
        far[i][1].wait_recv()
        p[zz, ym, HI] = (p[zz, ym, HI].astype(F32) + yb[zz].astype(F32)).astype(BF16)
        near.append((up, net.send(p.at[zz, ym], ydn.at[zz], to_ym)))
    if not early:
        for pair in pairs:
            fill(y, pair)
    yield

    def mine(i):
        near[i][0].wait_recv()
        near[i][1].wait_recv()
        zz = order[i]
        return p[zz, y].astype(F32) + yup[zz].astype(F32) + ydn[zz].astype(F32)

    q[0] = mine(0).astype(BF16)
    a = net.send(q.at[0, LO], za, to_zp)
    b = net.send(q.at[0, HI], zb, to_zm)
    yield
    q[1] = mine(1).astype(BF16)
    q[2] = mine(2).astype(BF16)
    yield
    a.wait_recv()
    q[1, LO] = (q[1, LO].astype(F32) + za[...].astype(F32)).astype(BF16)
    up = net.send(q.at[1], zup, to_zp)
    b.wait_recv()
    q[2, HI] = (q[2, HI].astype(F32) + zb[...].astype(F32)).astype(BF16)
    down = net.send(q.at[2], zdn, to_zm)
    yield
    total = mine(3)
    yield
    up.wait_recv()
    down.wait_recv()
    done(total + zup[...].astype(F32) + zdn[...].astype(F32))


def kernel(
    x_hbm, mask_hbm, step_hbm, gain_hbm, wqkv_hbm, wout_hbm, win_hbm, cot_hbm,
    gx_ref, gw_ref, gs_ref, gg_ref,
    xg, maskv, stepv, gainv, wq, wqp, wo, wop, wi, wit, witp, cot,
    gm, mt, mtp,
    acc, qs, ks, vs, probs_s, hp, p1, hid, pf, p2, pyb, pq, pzb, pr, gpf,
    gpg, gpr, gpn, ghs, p3, gr, rows_s,
    wst, wxb, wsm, wzb, wfin,
    sst, syb, sm1, sxb, szb, slb, scb, sfin,
    *rest,
):
    bufs1, bufs2 = rest[:9], rest[9:18]
    send_sems, recv_sems, local_sems = rest[18:]
    net = Net(send_sems, recv_sems)
    x, zl, z, y, c = net.x, net.zl, net.z, net.y, net.c
    to_c = net.go(c=1)
    scale = HD ** (-0.5)

    barrier = pltpu.get_barrier_semaphore()
    peers = net.peers()
    for peer in peers:
        pl.semaphore_signal(barrier, inc=1, device_id=peer, device_id_type=MESH)
    loads = {}
    for i, (name, src, dst) in enumerate(
        (
            ("w_in", win_hbm, wi),
            ("x", x_hbm, xg.at[z, y, c]),
            ("w_out", wout_hbm, wo),
            ("w_qkv", wqkv_hbm, wq),
            ("mask", mask_hbm, maskv),
            ("step", step_hbm, stepv),
            ("gain", gain_hbm, gainv),
            ("cot", cot_hbm, cot),
        )
    ):
        loads[name] = pltpu.make_async_copy(src, dst, local_sems.at[i])
        loads[name].start()
    loads["w_in"].wait()
    for k in range(8):
        wit[k * HD : (k + 1) * HD, :] = wi[:, k * HD : (k + 1) * HD].T
    gm[z, y, c] = wit[pl.ds(pl.multiple_of(PIECE * net.dp, PIECE), PIECE), :]
    loads["x"].wait()
    pl.semaphore_wait(barrier, len(peers))

    every = pl.ds(0, 4)

    def weight_product():
        sent = [net.send(gm.at[z, y, c], gm.at[z, y, c], net.go(z=d)) for d in (1, 2, 3)]
        yield
        for copy in sent:
            copy.wait_recv()
        sent = [net.send(gm.at[every, y, c], gm.at[every, y, c], net.go(y=d)) for d in (1, 2, 3)]
        yield
        for copy in sent:
            copy.wait_recv()
        other = net.send(gm.at[every, every, c], gm.at[every, every, c], to_c)
        yield
        other.wait_recv()
        loads["w_out"].wait()
        left = jnp.concatenate(
            [gm[i, j, k] for i in range(4) for j in range(4) for k in range(2)], axis=1
        )
        mt[x, zl] = nt(left, wo[...]).astype(BF16)
        sent = [net.send(mt.at[x, zl], mt.at[x, zl], net.go(zl=d)) for d in (1, 2, 3)]
        yield
        for copy in sent:
            copy.wait_recv()
        sent = [net.send(mt.at[x], mt.at[x], net.go(x=d)) for d in (1, 2, 3)]
        last = [net.send(mt.at[x], mtp.at[x], to_c)]
        yield
        for d in (1, 2, 3):
            sent[d - 1].wait_recv()
            spot = (x + 4 - d) % 4
            last.append(net.send(mt.at[spot], mtp.at[spot], to_c))
        yield
        for copy in last:
            copy.wait_recv()

    def plane(i):
        zz = gather.planes[i]
        gather.here(i)
        left = jnp.concatenate([xg[zz, j, k] for j in range(4) for k in range(2)], axis=1)
        right = jnp.concatenate([wq[j, zz].reshape(DD, HD) for j in range(3)], axis=1)
        term = nn(left, right)
        acc[...] = term if i == 0 else acc[...] + term

    product = weight_product()
    next(product)
    gather = Gather(net, xg)
    gather.begin()
    next(product)
    gather.along_z()
    next(product)
    gather.turn(0)
    gather.far_z()
    gather.turn(1)
    gather.turn(2)
    gather.land(0)
    next(product)
    gather.turn(3)
    gather.land(1)
    gather.land(2)
    loads["w_qkv"].wait()
    plane(0)
    next(product)
    plane(1)
    gather.land(3)
    partner_in = net.send(wit, witp, to_c)
    plane(2)
    plane(3)

    spot = net.count
    partner_out = net.make(wop, wop, to_c)
    for i in range(16):
        cols = pl.ds(pl.multiple_of((2 * i + 1 - c) * HD, HD), HD)
        pltpu.make_async_remote_copy(
            src_ref=wout_hbm.at[:, cols],
            dst_ref=wop.at[i],
            send_sem=send_sems.at[spot],
            recv_sem=recv_sems.at[spot],
            device_id=to_c,
            device_id_type=MESH,
        ).start()
    net.open.append(partner_out)
    partner_qkv = []

    def swap_qkv(j):
        partner_qkv.append(net.send(wqkv_hbm.at[j, every, every, 1 - c], wqp.at[j], to_c))

    swap_qkv(0)

    query = acc[:, :HD].astype(BF16)
    key_rows = acc[:, HD : 2 * HD].astype(BF16)
    value = acc[:, 2 * HD :].astype(BF16)
    qs[...] = query
    ks[...] = key_rows
    vs[...] = value
    loads["mask"].wait()
    row = lax.broadcasted_iota(jnp.int32, (L, L), 0)
    col = lax.broadcasted_iota(jnp.int32, (L, L), 1)
    allowed = (col <= row) & ((maskv[...] == 1) | (col == row))
    scores = jnp.where(allowed, nt(query, key_rows) * scale, -1e30)
    next(product)
    raised = jnp.exp(scores - jnp.max(scores, axis=-1, keepdims=True))
    probs = raised / jnp.sum(raised, axis=-1, keepdims=True)
    probs_s[...] = probs
    hp[0] = nn(probs.astype(BF16), value).astype(BF16)
    heads_copy = net.send(hp.at[0], hp.at[1], to_c)
    partner_in.wait_recv()
    next(product, None)
    heads_copy.wait_recv()

    left = jnp.concatenate([hp[0], hp[1], xg[z, y, c], xg[z, y, 1 - c]], axis=1)
    right = jnp.concatenate(
        [mt[...].reshape(DD, HD), mtp[...].reshape(DD, HD), wit[...], witp[...]], axis=1
    )
    term = nt(left, right)
    for k in range(8):
        pf[pl.ds(k, L, stride=8), :] = term[:, k * HD : (k + 1) * HD]
    for i in range(4):
        for j in range(4):
            rows = pl.ds(pl.multiple_of((8 * i + 2 * j + c) * ROWS, 8), ROWS)
            p2[j, i] = pf[rows, :].astype(BF16)
    sent = [net.send(p2.at[(y + d) % 4], pyb.at[d - 1], net.go(y=d)) for d in (1, 2, 3)]
    def fill_out(yy, pair):
        left = jnp.concatenate([hp[0], hp[1]], axis=1)
        right = []
        for zz in pair:
            col0 = pl.multiple_of((zz * 8 + yy * 2 + c) * HD, HD)
            right.append(jnp.concatenate([wo[:, pl.ds(col0, HD)], wop[zz * 4 + yy]], axis=0))
        term = nn(left, jnp.concatenate(right, axis=1)).astype(BF16)
        p1[pair[0], yy] = term[:, :HD]
        p1[pair[1], yy] = term[:, HD:]

    def keep_hidden(summed):
        hid[...] = (xg[z, y, c].astype(F32) + summed).astype(BF16)

    outward = scatter_ring(net, p1, fill_out, bufs1, keep_hidden, early=True)
    partner_out.wait_recv()
    next(outward)
    total = p2[y].astype(F32)
    for d in range(3):
        sent[d].wait_recv()
        total += pyb[d].astype(F32)
    pq[...] = total.astype(BF16)
    sent = [net.send(pq.at[(z + d) % 4], pzb.at[d - 1], net.go(z=d)) for d in (1, 2, 3)]

    next(outward)
    total = pq[z].astype(F32)
    for d in range(3):
        sent[d].wait_recv()
        total += pzb[d].astype(F32)
    pr[...] = total
    swap_qkv(1)

    for name in ("step", "gain", "cot"):
        loads[name].wait()
    gains = gainv[...].astype(F32)[None]
    proj = jnp.concatenate([pr[pl.ds(k, FR, stride=8), :] for k in range(8)], axis=1)
    grad_rows = jnp.zeros((FR, DD), F32)
    gain_rows = jnp.zeros((FR, DD), F32)
    for s in range(STEPS):
        inner = proj + stepv[s : s + 1, :].astype(F32)
        inverse = lax.rsqrt(jnp.mean(inner * inner, axis=-1, keepdims=True) + 1e-06)
        arriving = cot[s].astype(F32)
        gain_rows += arriving * inner * inverse
        scaled = arriving * gains
        mixed = jnp.mean(inner * scaled, axis=-1, keepdims=True)
        grad_inner = inverse * scaled - inverse * inverse * inverse * inner * mixed
        grad_rows += grad_inner
        rows_s[s : s + 1, :] = jnp.sum(grad_inner, axis=0, keepdims=True)
    for k in range(8):
        gpf[pl.ds(k, FR, stride=8), :] = grad_rows[:, k * HD : (k + 1) * HD]
    gpg[z, y, c] = gpf[...].astype(BF16)

    sent = [net.send(gpg.at[z, y, c], gpg.at[z, y, c], net.go(z=d)) for d in (1, 2, 3)]
    rows_s[STEPS : STEPS + 1, :] = jnp.sum(gain_rows, axis=0, keepdims=True)
    for k in range(8):
        cols = slice(k * HD, (k + 1) * HD)
        j, i = k // 2, 2 * (k % 2)
        sst[j, i] = rows_s[:16, cols]
        sst[j, i + 1] = jnp.zeros((16, HD), F32)
        sst[j, i + 1, 0:2] = rows_s[16:18, cols]

    def small_sums():
        sent = [net.send(sst.at[(y + d) % 4], syb.at[d - 1], net.go(y=d)) for d in (1, 2, 3)]
        yield
        total = sst[y]
        for d in range(3):
            sent[d].wait_recv()
            total += syb[d]
        sm1[...] = total
        sent = [net.send(sm1.at[(x + d) % 4], sxb.at[d - 1], net.go(x=d)) for d in (1, 2, 3)]
        yield
        total = sm1[x]
        for d in range(3):
            sent[d].wait_recv()
            total += sxb[d]
        szb[z] = total
        sent = [net.send(szb.at[z], szb.at[z], net.go(z=d)) for d in (1, 2, 3)]
        yield
        for copy in sent:
            copy.wait_recv()
        slb[zl] = szb[0] + szb[1] + szb[2] + szb[3]
        sent = [net.send(slb.at[zl], slb.at[zl], net.go(zl=d)) for d in (1, 2, 3)]
        yield
        for copy in sent:
            copy.wait_recv()
        scb[c] = slb[0] + slb[1] + slb[2] + slb[3]
        other = net.send(scb.at[c], scb.at[c], to_c)
        yield
        other.wait_recv()
        sfin[y, x] = scb[0] + scb[1]
        sent = [net.send(sfin.at[y, x], sfin.at[y, x], net.go(x=d)) for d in (1, 2, 3)]
        yield
        for copy in sent:
            copy.wait_recv()
        sent = [net.send(sfin.at[y], sfin.at[y], net.go(y=d)) for d in (1, 2, 3)]
        yield
        for copy in sent:
            copy.wait_recv()
        for k in range(8):
            cols = slice(k * HD, (k + 1) * HD)
            j, i = k // 2, 2 * (k % 2)
            gs_ref[0:16, cols] = sfin[j, i]
            gs_ref[16:17, cols] = sfin[j, i + 1, 0:1]
            gg_ref[0:1, cols] = sfin[j, i + 1, 1:2]

    def weight_sums():
        grads = tn(hid[...], gpn[...]).astype(BF16)
        for k in range(8):
            cols = slice(k * HD, (k + 1) * HD)
            wst[2 * k] = grads[:64, cols]
            wst[2 * k + 1] = grads[64:, cols]
        sent = []
        for d in (1, 2, 3):
            rows = pl.ds(4 * ((x + d) % 4), 4)
            sent.append(net.send(wst.at[rows], wxb.at[d - 1], net.go(x=d)))
        yield
        total = wst[pl.ds(4 * x, 4)].astype(F32)
        for d in range(3):
            sent[d].wait_recv()
            total += wxb[d].astype(F32)
        wsm[...] = total.astype(BF16)
        sent = [net.send(wsm.at[(zl + d) % 4], wzb.at[d - 1], net.go(zl=d)) for d in (1, 2, 3)]
        yield
        total = wsm[zl].astype(F32)
        for d in range(3):
            sent[d].wait_recv()
            total += wzb[d].astype(F32)
        spot = 4 * x + zl
        wfin[spot] = total.astype(BF16)
        sent = [net.send(wfin.at[spot], wfin.at[spot], net.go(zl=d)) for d in (1, 2, 3)]
        yield
        for copy in sent:
            copy.wait_recv()
        rows = pl.ds(4 * x, 4)
        sent = [net.send(wfin.at[rows], wfin.at[rows], net.go(x=d)) for d in (1, 2, 3)]
        yield
        for copy in sent:
            copy.wait_recv()
        for k in range(8):
            cols = slice(k * HD, (k + 1) * HD)
            gw_ref[0:64, cols] = wfin[2 * k]
            gw_ref[64:128, cols] = wfin[2 * k + 1]

    small = small_sums()
    next(small)
    next(outward)
    for copy in sent:
        copy.wait_recv()
    sent = [net.send(gpg.at[every, y, c], gpg.at[every, y, c], net.go(y=d)) for d in (1, 2, 3)]
    next(outward)
    next(small)
    for copy in sent:
        copy.wait_recv()
    other = net.send(gpg.at[every, every, c], gpg.at[every, every, c], to_c)
    swap_qkv(2)
    next(outward)
    next(small)
    other.wait_recv()
    gpr[...] = gpg[...].reshape(32 * ROWS, HD).astype(F32)
    for k in range(8):
        gpn[:, k * HD : (k + 1) * HD] = gpr[pl.ds(k, L, stride=8), :].astype(BF16)
    back = nn(gpn[...], jnp.concatenate([mt[...].reshape(DD, HD), wit[...]], axis=1))
    ghs[...] = back[:, HD:].astype(BF16)

    grad_heads = back[:, :HD].astype(BF16)
    next(outward)
    probs = probs_s[...]
    grad_probs = nt(grad_heads, vs[...])
    inside = jnp.sum(probs * grad_probs, axis=-1, keepdims=True)
    grad_scores = (probs * (grad_probs - inside) * scale).astype(BF16)
    gr[0, 0] = nn(grad_scores, ks[...]).astype(BF16)
    gr[0, 1] = tn(grad_scores, qs[...]).astype(BF16)
    gr[0, 2] = tn(probs.astype(BF16), grad_heads).astype(BF16)
    grads_copy = net.send(gr.at[0], gr.at[1], to_c)
    next(outward)
    next(small)
    for copy in partner_qkv:
        copy.wait_recv()
    sums = weight_sums()
    grads_copy.wait_recv()

    def fill_in(yy, pair):
        left = jnp.concatenate([gr[i, j] for i in range(2) for j in range(3)], axis=1)
        right = []
        for zz in pair:
            right.append(
                jnp.concatenate(
                    [wq[j, zz, yy, c] for j in range(3)] + [wqp[j, zz, yy] for j in range(3)],
                    axis=1,
                )
            )
        term = nt(left, jnp.concatenate(right, axis=0)).astype(BF16)
        p3[pair[0], yy] = term[:, :HD]
        p3[pair[1], yy] = term[:, HD:]

    def keep_grad(summed):
        gx_ref[...] = (ghs[...].astype(F32) + summed).astype(BF16)

    for i, _ in enumerate(scatter_ring(net, p3, fill_in, bufs2, keep_grad)):
        if i == 1:
            next(outward, None)
        if i >= 1:
            next(sums, None)
        if i >= 2:
            next(small, None)
    for _ in small:
        pass
    for _ in sums:
        pass
    net.drain()


def ring_buffers():
    return [
        pltpu.VMEM((4, HALF, HD), BF16),
        pltpu.VMEM((4, HALF, HD), BF16),
        pltpu.VMEM((4, L, HD), BF16),
        pltpu.VMEM((4, L, HD), BF16),
        pltpu.VMEM((3, L, HD), BF16),
        pltpu.VMEM((HALF, HD), BF16),
        pltpu.VMEM((HALF, HD), BF16),
        pltpu.VMEM((L, HD), BF16),
        pltpu.VMEM((L, HD), BF16),
    ]


def shards(layer_input, frame_mask, w_qkv, w_out, w_in, step_embed, depth_gain, cotangent):
    def v(*shape, kind=BF16):
        return pltpu.VMEM(shape, kind)

    vmem = pl.BlockSpec(memory_space=pltpu.VMEM)
    hbm = pl.BlockSpec(memory_space=pltpu.HBM)
    scratch = [
        v(4, 4, 2, L, HD),
        v(1, L, kind=jnp.int32),
        v(STEPS, DD),
        v(DD),
        v(3, 4, 4, 2, HD, HD),
        v(3, 4, 4, HD, HD),
        v(HD, 32 * HD),
        v(16, HD, HD),
        v(HD, DD),
        v(DD, HD),
        v(DD, HD),
        v(STEPS, FR, DD),
        v(4, 4, 2, PIECE, HD),
        v(4, 4, PIECE, HD),
        v(4, 4, PIECE, HD),
        v(L, 3 * HD, kind=F32),
        v(L, HD),
        v(L, HD),
        v(L, HD),
        v(L, L, kind=F32),
        v(2, L, HD),
        v(4, 4, L, HD),
        v(L, HD),
        v(32 * ROWS, HD, kind=F32),
        v(4, 4, ROWS, HD),
        v(3, 4, ROWS, HD),
        v(4, ROWS, HD),
        v(3, ROWS, HD),
        v(ROWS, HD, kind=F32),
        v(ROWS, HD, kind=F32),
        v(4, 4, 2, ROWS, HD),
        v(32 * ROWS, HD, kind=F32),
        v(L, DD),
        v(L, HD),
        v(4, 4, L, HD),
        v(2, 3, L, HD),
        v(24, DD, kind=F32),
        v(16, 64, HD),
        v(3, 4, 64, HD),
        v(4, 64, HD),
        v(3, 64, HD),
        v(16, 64, HD),
        v(4, 4, 16, HD, kind=F32),
        v(3, 4, 16, HD, kind=F32),
        v(4, 16, HD, kind=F32),
        v(3, 16, HD, kind=F32),
        v(4, 16, HD, kind=F32),
        v(4, 16, HD, kind=F32),
        v(2, 16, HD, kind=F32),
        v(4, 4, 16, HD, kind=F32),
        *ring_buffers(),
        *ring_buffers(),
        pltpu.SemaphoreType.DMA((N_SEM,)),
        pltpu.SemaphoreType.DMA((N_SEM,)),
        pltpu.SemaphoreType.DMA((8,)),
    ]
    grad_x, grad_in, grad_step, grad_gain = pl.pallas_call(
        kernel,
        out_shape=(
            jax.ShapeDtypeStruct((L, HD), BF16),
            jax.ShapeDtypeStruct((HD, DD), BF16),
            jax.ShapeDtypeStruct((STEPS, DD), F32),
            jax.ShapeDtypeStruct((1, DD), F32),
        ),
        in_specs=[hbm] * 8,
        out_specs=(vmem,) * 4,
        scratch_shapes=scratch,
        compiler_params=pltpu.CompilerParams(
            collective_id=0, has_side_effects=True, vmem_limit_bytes=60 * 1024 * 1024
        ),
    )(
        layer_input[0],
        frame_mask,
        step_embed,
        depth_gain,
        w_qkv.reshape(3, 4, 4, 2, HD, HD),
        w_out,
        w_in,
        jnp.transpose(cotangent[0], (1, 0, 2)),
    )
    return (grad_x[None], grad_in, grad_step, grad_gain[0])


def solution(mesh):
    return jax.shard_map(
        shards,
        mesh=mesh,
        in_specs=(
            P("dp", None, "tensor"),
            P("dp", None),
            P(None, None, "tensor"),
            P("tensor", None),
            P("tensor", None),
            P(),
            P(),
            P("dp", "tensor", None, None),
        ),
        out_specs=(P("dp", None, "tensor"), P("tensor", None), P(), P()),
        check_vma=False,
    )
```

```python
import functools

import jax
import jax.numpy as jnp
from jax import lax
from jax.experimental import pallas as pl
from jax.experimental.pallas import tpu as pltpu
from jax.sharding import PartitionSpec as P

MESH = pl.DeviceIdType.MESH
F32 = jnp.float32
BF16 = jnp.bfloat16
L, HD, DD, STEPS, FR = 192, 128, 1024, 17, 6
HALF = L // 2
LO, HI = pl.ds(0, HALF), pl.ds(HALF, HALF)
ROWS = FR * (DD // HD)
PIECE = 64
N_SEM = 200


def nt(a, b):
    return lax.dot_general(a, b, (((1,), (1,)), ((), ())), preferred_element_type=F32)


def nn(a, b):
    return lax.dot_general(a, b, (((1,), (0,)), ((), ())), preferred_element_type=F32)


def tn(a, b):
    return lax.dot_general(a, b, (((0,), (0,)), ((), ())), preferred_element_type=F32)


def around(v):
    return (v + 1) % 4, (v + 3) % 4, (v + 2) % 4


class Net:
    def __init__(self, send_sems, recv_sems):
        self.send_sems, self.recv_sems = send_sems, recv_sems
        self.count = 0
        self.open = []
        dp, t = lax.axis_index("dp"), lax.axis_index("tensor")
        self.dp, self.t = dp, t
        self.x, self.zl = dp // 4, dp % 4
        self.z, self.y, self.c = t // 8, (t // 2) % 4, t % 2

    def go(self, z=0, y=0, c=0, x=0, zl=0):
        dp, t = self.dp, self.t
        if x or zl:
            dp = ((self.x + x) % 4) * 4 + (self.zl + zl) % 4
        if z or y or c:
            cc = (self.c + c) % 2
            t = ((self.z + z) % 4) * 8 + ((self.y + y) % 4) * 2 + cc
        return (dp, t)

    def peers(self):
        found = [self.go(c=1)]
        for d in (1, 2, 3):
            found += [self.go(y=d), self.go(z=d), self.go(x=d), self.go(zl=d)]
        return found

    def make(self, src, dst, peer):
        i = self.count
        self.count += 1
        return pltpu.make_async_remote_copy(
            src_ref=src,
            dst_ref=dst,
            send_sem=self.send_sems.at[i],
            recv_sem=self.recv_sems.at[i],
            device_id=peer,
            device_id_type=MESH,
        )

    def send(self, src, dst, peer):
        copy = self.make(src, dst, peer)
        copy.start()
        self.open.append(copy)
        return copy

    def drain(self):
        for copy in self.open:
            copy.wait_send()
        self.open = []


class Gather:
    def __init__(self, net, g):
        self.net, self.g = net, g
        self.planes = (net.z, around(net.z)[1], around(net.z)[0], around(net.z)[2])
        self.along, self.forward, self.across = {}, {}, {}
        self.to_yp, self.to_ym, self.to_c = net.go(y=1), net.go(y=3), net.go(c=1)

    def whole(self, zz, yy, peer):
        at = self.g.at[zz, yy, self.net.c]
        return self.net.send(at, at, peer)

    def part(self, zz, yy, rows, peer):
        at = self.g.at[zz, yy, self.net.c, rows]
        return self.net.send(at, at, peer)

    def begin(self):
        z, y = self.net.z, self.net.y
        to_zp, to_zm = self.net.go(z=1), self.net.go(z=3)
        self.up_lo = self.part(z, y, LO, to_zp)
        self.dn_hi = self.part(z, y, HI, to_zm)
        self.up_hi = self.part(z, y, HI, to_zp)
        self.dn_lo = self.part(z, y, LO, to_zm)
        self.spread(0)

    def along_z(self):
        y = self.net.y
        to_zp, to_zm = self.net.go(z=1), self.net.go(z=3)
        self.up_lo.wait_recv()
        self.on = self.part(self.planes[1], y, LO, to_zp)
        self.dn_hi.wait_recv()
        self.back = self.part(self.planes[2], y, HI, to_zm)
        self.up_hi.wait_recv()
        self.spread(1)
        self.dn_lo.wait_recv()
        self.spread(2)

    def far_z(self):
        self.on.wait_recv()
        self.back.wait_recv()
        self.spread(3)

    def spread(self, i):
        zz, y = self.planes[i], self.net.y
        if i == 3:
            self.along[i] = (
                self.part(zz, y, LO, self.to_yp),
                self.part(zz, y, HI, self.to_ym),
                self.part(zz, y, HI, self.to_yp),
                self.part(zz, y, LO, self.to_ym),
            )
        else:
            self.along[i] = (self.whole(zz, y, self.to_yp), self.whole(zz, y, self.to_ym))
        self.across[i] = []
        self.over(i, zz, y)

    def over(self, i, zz, yy):
        if i == 3:
            self.across[i].append(self.whole(zz, yy, self.to_c))

    def turn(self, i):
        zz = self.planes[i]
        yp, ym, _ = around(self.net.y)
        self.along[i][0].wait_recv()
        first = self.part(zz, ym, LO, self.to_yp)
        self.along[i][1].wait_recv()
        second = self.part(zz, yp, HI, self.to_ym)
        self.forward[i] = (first, second)
        for copy in self.along[i][2:]:
            copy.wait_recv()
        self.over(i, zz, ym)
        self.over(i, zz, yp)

    def land(self, i):
        for copy in self.forward[i]:
            copy.wait_recv()
        self.over(i, self.planes[i], around(self.net.y)[2])
        if i < 3:
            at = self.g.at[self.planes[i], pl.ds(0, 4), self.net.c]
            self.across[i].append(self.net.send(at, at, self.to_c))

    def here(self, i):
        for copy in self.across[i]:
            copy.wait_recv()


def scatter_ring(net, p, fill, bufs, done, ahead=False):
    ya, yb, yup, ydn, q, za, zb, zup, zdn = bufs
    z, y = net.z, net.y
    zp, zm, z2 = around(z)
    yp, ym, y2 = around(y)
    to_zp, to_zm, to_yp, to_ym = net.go(z=1), net.go(z=3), net.go(y=1), net.go(y=3)
    order = (z2, zp, zm, z)
    pairs = (order[:2], order[2:])

    far, near = [], [[], [], [], []]
    if ahead:
        for yy in (y2, yp, ym, y):
            for pair in pairs:
                fill(yy, pair)
        yield
    for pair in pairs:
        if not ahead:
            fill(y2, pair)
        for zz in pair:
            a = net.send(p.at[zz, y2, LO], ya.at[zz], to_yp)
            far.append((a, net.send(p.at[zz, y2, HI], yb.at[zz], to_ym)))

    def at_once(i):
        zz = order[i]
        near[i].append(net.send(p.at[zz, yp, HI], yup.at[zz, HI], to_yp))
        near[i].append(net.send(p.at[zz, ym, LO], ydn.at[zz, LO], to_ym))

    for j, pair in enumerate(pairs):
        if not ahead:
            fill(yp, pair)
            fill(ym, pair)
        at_once(2 * j)
        at_once(2 * j + 1)
    yield
    for i, zz in enumerate(order):
        far[i][0].wait_recv()
        p[zz, yp, LO] = (p[zz, yp, LO].astype(F32) + ya[zz].astype(F32)).astype(BF16)
        near[i].append(net.send(p.at[zz, yp, LO], yup.at[zz, LO], to_yp))
        far[i][1].wait_recv()
        p[zz, ym, HI] = (p[zz, ym, HI].astype(F32) + yb[zz].astype(F32)).astype(BF16)
        near[i].append(net.send(p.at[zz, ym, HI], ydn.at[zz, HI], to_ym))
    if not ahead:
        for pair in pairs:
            fill(y, pair)
    yield

    def mine(i):
        for copy in near[i]:
            copy.wait_recv()
        zz = order[i]
        return p[zz, y].astype(F32) + yup[zz].astype(F32) + ydn[zz].astype(F32)

    q[0] = mine(0).astype(BF16)
    a = net.send(q.at[0, LO], za, to_zp)
    b = net.send(q.at[0, HI], zb, to_zm)
    yield
    q[1] = mine(1).astype(BF16)
    last = [net.send(q.at[1, HI], zup.at[HI], to_zp)]
    q[2] = mine(2).astype(BF16)
    last.append(net.send(q.at[2, LO], zdn.at[LO], to_zm))
    yield
    a.wait_recv()
    q[1, LO] = (q[1, LO].astype(F32) + za[...].astype(F32)).astype(BF16)
    last.append(net.send(q.at[1, LO], zup.at[LO], to_zp))
    b.wait_recv()
    q[2, HI] = (q[2, HI].astype(F32) + zb[...].astype(F32)).astype(BF16)
    last.append(net.send(q.at[2, HI], zdn.at[HI], to_zm))
    yield
    total = mine(3)
    yield
    for copy in last:
        copy.wait_recv()
    done(total + zup[...].astype(F32) + zdn[...].astype(F32))


def kernel(
    x_hbm, mask_hbm, step_hbm, gain_hbm, wqkv_hbm, wout_hbm, win_hbm, cot_hbm,
    gx_ref, gw_ref, gs_ref, gg_ref,
    xg, maskv, stepv, gainv, wq, wqp, wo, wop, wi, wit, witp, cot,
    gm, mt, mtp,
    acc, qs, ks, vs, probs_s, hp, p1, hid, pf, p2, pyb, pq, pzb, pr, gpf,
    gpg, gpr, gpn, ghs, p3, gr, rows_s,
    wst, wxb, wsm, wzb, wfin,
    sst, syb, sm1, sxb, szb, slb, scb, sfin,
    *rest,
):
    bufs1, bufs2 = rest[:9], rest[9:18]
    send_sems, recv_sems, local_sems = rest[18:]
    net = Net(send_sems, recv_sems)
    x, zl, z, y, c = net.x, net.zl, net.z, net.y, net.c
    to_c = net.go(c=1)
    scale = HD ** (-0.5)

    barrier = pltpu.get_barrier_semaphore()
    peers = net.peers()
    for peer in peers:
        pl.semaphore_signal(barrier, inc=1, device_id=peer, device_id_type=MESH)
    loads = {}
    for i, (name, src, dst) in enumerate(
        (
            ("w_in", win_hbm, wi),
            ("x", x_hbm, xg.at[z, y, c]),
            ("w_out", wout_hbm, wo),
            ("w_qkv", wqkv_hbm, wq),
            ("mask", mask_hbm, maskv),
            ("step", step_hbm, stepv),
            ("gain", gain_hbm, gainv),
            ("cot", cot_hbm, cot),
        )
    ):
        loads[name] = pltpu.make_async_copy(src, dst, local_sems.at[i])
        loads[name].start()
    loads["w_in"].wait()
    for k in range(8):
        wit[k * HD : (k + 1) * HD, :] = wi[:, k * HD : (k + 1) * HD].T
    gm[z, y, c] = wit[pl.ds(pl.multiple_of(PIECE * net.dp, PIECE), PIECE), :]
    loads["x"].wait()
    pl.semaphore_wait(barrier, len(peers))

    every = pl.ds(0, 4)

    def weight_product():
        sent = [net.send(gm.at[z, y, c], gm.at[z, y, c], net.go(z=d)) for d in (1, 2, 3)]
        yield
        for copy in sent:
            copy.wait_recv()
        sent = [net.send(gm.at[every, y, c], gm.at[every, y, c], net.go(y=d)) for d in (1, 2, 3)]
        yield
        for copy in sent:
            copy.wait_recv()
        other = net.send(gm.at[every, every, c], gm.at[every, every, c], to_c)
        yield
        other.wait_recv()
        loads["w_out"].wait()
        left = jnp.concatenate(
            [gm[i, j, k] for i in range(4) for j in range(4) for k in range(2)], axis=1
        )
        mt[x, zl] = nt(left, wo[...]).astype(BF16)
        sent = [net.send(mt.at[x, zl], mt.at[x, zl], net.go(zl=d)) for d in (1, 2, 3)]
        yield
        for copy in sent:
            copy.wait_recv()
        sent = [net.send(mt.at[x], mt.at[x], net.go(x=d)) for d in (1, 2, 3)]
        last = [net.send(mt.at[x], mtp.at[x], to_c)]
        yield
        for d in (1, 2, 3):
            sent[d - 1].wait_recv()
            spot = (x + 4 - d) % 4
            last.append(net.send(mt.at[spot], mtp.at[spot], to_c))
        yield
        for copy in last:
            copy.wait_recv()

    def plane(i):
        zz = gather.planes[i]
        gather.here(i)
        left = jnp.concatenate([xg[zz, j, k] for j in range(4) for k in range(2)], axis=1)
        right = jnp.concatenate([wq[j, zz].reshape(DD, HD) for j in range(3)], axis=1)
        term = nn(left, right)
        acc[...] = term if i == 0 else acc[...] + term

    product = weight_product()
    gather = Gather(net, xg)
    gather.begin()
    next(product)
    next(product)
    gather.along_z()
    next(product)
    gather.turn(0)
    gather.far_z()
    gather.turn(1)
    gather.turn(2)
    gather.land(0)
    next(product)
    gather.turn(3)
    gather.land(1)
    gather.land(2)
    loads["w_qkv"].wait()
    plane(0)
    next(product)
    plane(1)
    gather.land(3)
    partner_in = net.send(wit, witp, to_c)
    plane(2)
    plane(3)

    spot = net.count
    partner_out = net.make(wop, wop, to_c)
    for i in range(16):
        cols = pl.ds(pl.multiple_of((2 * i + 1 - c) * HD, HD), HD)
        pltpu.make_async_remote_copy(
            src_ref=wout_hbm.at[:, cols],
            dst_ref=wop.at[i],
            send_sem=send_sems.at[spot],
            recv_sem=recv_sems.at[spot],
            device_id=to_c,
            device_id_type=MESH,
        ).start()
    net.open.append(partner_out)
    partner_qkv = []

    def swap_qkv(j):
        partner_qkv.append(net.send(wqkv_hbm.at[j, every, every, 1 - c], wqp.at[j], to_c))

    swap_qkv(0)

    query = acc[:, :HD].astype(BF16)
    key_rows = acc[:, HD : 2 * HD].astype(BF16)
    value = acc[:, 2 * HD :].astype(BF16)
    qs[...] = query
    ks[...] = key_rows
    vs[...] = value
    loads["mask"].wait()
    row = lax.broadcasted_iota(jnp.int32, (L, L), 0)
    col = lax.broadcasted_iota(jnp.int32, (L, L), 1)
    allowed = (col <= row) & ((maskv[...] == 1) | (col == row))
    scores = jnp.where(allowed, nt(query, key_rows) * scale, -1e30)
    next(product)
    raised = jnp.exp(scores - jnp.max(scores, axis=-1, keepdims=True))
    probs = raised / jnp.sum(raised, axis=-1, keepdims=True)
    probs_s[...] = probs
    hp[0] = nn(probs.astype(BF16), value).astype(BF16)
    heads_copy = net.send(hp.at[0], hp.at[1], to_c)
    partner_in.wait_recv()
    heads_copy.wait_recv()

    next(product, None)

    left = jnp.concatenate([hp[0], hp[1], xg[z, y, c], xg[z, y, 1 - c]], axis=1)
    right = jnp.concatenate(
        [mt[...].reshape(DD, HD), mtp[...].reshape(DD, HD), wit[...], witp[...]], axis=1
    )
    term = nt(left, right)
    for k in range(8):
        pf[pl.ds(k, L, stride=8), :] = term[:, k * HD : (k + 1) * HD]
    for i in range(4):
        for j in range(4):
            rows = pl.ds(pl.multiple_of((8 * i + 2 * j + c) * ROWS, 8), ROWS)
            p2[j, i] = pf[rows, :].astype(BF16)
    sent = [net.send(p2.at[(y + d) % 4], pyb.at[d - 1], net.go(y=d)) for d in (1, 2, 3)]

    def fill_out(yy, pair):
        left = jnp.concatenate([hp[0], hp[1]], axis=1)
        right = []
        for zz in pair:
            col0 = pl.multiple_of((zz * 8 + yy * 2 + c) * HD, HD)
            right.append(jnp.concatenate([wo[:, pl.ds(col0, HD)], wop[zz * 4 + yy]], axis=0))
        term = nn(left, jnp.concatenate(right, axis=1)).astype(BF16)
        p1[pair[0], yy] = term[:, :HD]
        p1[pair[1], yy] = term[:, HD:]

    def keep_hidden(summed):
        hid[...] = (xg[z, y, c].astype(F32) + summed).astype(BF16)

    outward = scatter_ring(net, p1, fill_out, bufs1, keep_hidden, ahead=True)
    partner_out.wait_recv()
    next(outward)
    total = p2[y].astype(F32)
    for d in range(3):
        sent[d].wait_recv()
        total += pyb[d].astype(F32)
    pq[...] = total.astype(BF16)
    sent = [net.send(pq.at[(z + d) % 4], pzb.at[d - 1], net.go(z=d)) for d in (1, 2, 3)]

    next(outward)
    total = pq[z].astype(F32)
    for d in range(3):
        sent[d].wait_recv()
        total += pzb[d].astype(F32)
    pr[...] = total
    swap_qkv(1)

    for name in ("step", "gain", "cot"):
        loads[name].wait()
    gains = gainv[...].astype(F32)[None]
    proj = jnp.concatenate([pr[pl.ds(k, FR, stride=8), :] for k in range(8)], axis=1)
    grad_rows = jnp.zeros((FR, DD), F32)
    gain_rows = jnp.zeros((FR, DD), F32)
    for s in range(STEPS):
        inner = proj + stepv[s : s + 1, :].astype(F32)
        inverse = lax.rsqrt(jnp.mean(inner * inner, axis=-1, keepdims=True) + 1e-06)
        arriving = cot[s].astype(F32)
        gain_rows += arriving * inner * inverse
        scaled = arriving * gains
        mixed = jnp.mean(inner * scaled, axis=-1, keepdims=True)
        grad_inner = inverse * scaled - inverse * inverse * inverse * inner * mixed
        grad_rows += grad_inner
        rows_s[s : s + 1, :] = jnp.sum(grad_inner, axis=0, keepdims=True)
    for k in range(8):
        gpf[pl.ds(k, FR, stride=8), :] = grad_rows[:, k * HD : (k + 1) * HD]
    gpg[z, y, c] = gpf[...].astype(BF16)

    sent = [net.send(gpg.at[z, y, c], gpg.at[z, y, c], net.go(z=d)) for d in (1, 2, 3)]
    next(outward)
    rows_s[STEPS : STEPS + 1, :] = jnp.sum(gain_rows, axis=0, keepdims=True)
    for k in range(8):
        cols = slice(k * HD, (k + 1) * HD)
        j, i = k // 2, 2 * (k % 2)
        sst[j, i] = rows_s[:16, cols]
        sst[j, i + 1] = jnp.zeros((16, HD), F32)
        sst[j, i + 1, 0:2] = rows_s[16:18, cols]

    def small_sums():
        sent = [net.send(sst.at[(y + d) % 4], syb.at[d - 1], net.go(y=d)) for d in (1, 2, 3)]
        yield
        total = sst[y]
        for d in range(3):
            sent[d].wait_recv()
            total += syb[d]
        sm1[...] = total
        sent = [net.send(sm1.at[(x + d) % 4], sxb.at[d - 1], net.go(x=d)) for d in (1, 2, 3)]
        yield
        total = sm1[x]
        for d in range(3):
            sent[d].wait_recv()
            total += sxb[d]
        szb[z] = total
        sent = [net.send(szb.at[z], szb.at[z], net.go(z=d)) for d in (1, 2, 3)]
        yield
        for copy in sent:
            copy.wait_recv()
        slb[zl] = szb[0] + szb[1] + szb[2] + szb[3]
        sent = [net.send(slb.at[zl], slb.at[zl], net.go(zl=d)) for d in (1, 2, 3)]
        yield
        for copy in sent:
            copy.wait_recv()
        scb[c] = slb[0] + slb[1] + slb[2] + slb[3]
        other = net.send(scb.at[c], scb.at[c], to_c)
        yield
        other.wait_recv()
        sfin[y, x] = scb[0] + scb[1]
        sent = [net.send(sfin.at[y, x], sfin.at[y, x], net.go(x=d)) for d in (1, 2, 3)]
        yield
        for copy in sent:
            copy.wait_recv()
        sent = [net.send(sfin.at[y], sfin.at[y], net.go(y=d)) for d in (1, 2, 3)]
        yield
        for copy in sent:
            copy.wait_recv()
        for k in range(8):
            cols = slice(k * HD, (k + 1) * HD)
            j, i = k // 2, 2 * (k % 2)
            gs_ref[0:16, cols] = sfin[j, i]
            gs_ref[16:17, cols] = sfin[j, i + 1, 0:1]
            gg_ref[0:1, cols] = sfin[j, i + 1, 1:2]

    def weight_sums():
        grads = tn(hid[...], gpn[...]).astype(BF16)
        for k in range(8):
            cols = slice(k * HD, (k + 1) * HD)
            wst[2 * k] = grads[:64, cols]
            wst[2 * k + 1] = grads[64:, cols]
        sent = []
        for d in (1, 2, 3):
            rows = pl.ds(4 * ((x + d) % 4), 4)
            sent.append(net.send(wst.at[rows], wxb.at[d - 1], net.go(x=d)))
        yield
        total = wst[pl.ds(4 * x, 4)].astype(F32)
        for d in range(3):
            sent[d].wait_recv()
            total += wxb[d].astype(F32)
        wsm[...] = total.astype(BF16)
        sent = [net.send(wsm.at[(zl + d) % 4], wzb.at[d - 1], net.go(zl=d)) for d in (1, 2, 3)]
        yield
        total = wsm[zl].astype(F32)
        for d in range(3):
            sent[d].wait_recv()
            total += wzb[d].astype(F32)
        spot = 4 * x + zl
        wfin[spot] = total.astype(BF16)
        sent = [net.send(wfin.at[spot], wfin.at[spot], net.go(zl=d)) for d in (1, 2, 3)]
        yield
        for copy in sent:
            copy.wait_recv()
        rows = pl.ds(4 * x, 4)
        sent = [net.send(wfin.at[rows], wfin.at[rows], net.go(x=d)) for d in (1, 2, 3)]
        yield
        for copy in sent:
            copy.wait_recv()
        for k in range(8):
            cols = slice(k * HD, (k + 1) * HD)
            gw_ref[0:64, cols] = wfin[2 * k]
            gw_ref[64:128, cols] = wfin[2 * k + 1]

    for copy in sent:
        copy.wait_recv()
    sent = [net.send(gpg.at[every, y, c], gpg.at[every, y, c], net.go(y=d)) for d in (1, 2, 3)]
    next(outward)
    for copy in sent:
        copy.wait_recv()
    other = net.send(gpg.at[every, every, c], gpg.at[every, every, c], to_c)
    swap_qkv(2)
    small = small_sums()
    next(small)
    next(outward)
    other.wait_recv()
    gpr[...] = gpg[...].reshape(32 * ROWS, HD).astype(F32)
    for k in range(8):
        gpn[:, k * HD : (k + 1) * HD] = gpr[pl.ds(k, L, stride=8), :].astype(BF16)
    back = nn(gpn[...], jnp.concatenate([mt[...].reshape(DD, HD), wit[...]], axis=1))
    ghs[...] = back[:, HD:].astype(BF16)
    next(outward)
    next(small)

    grad_heads = back[:, :HD].astype(BF16)
    probs = probs_s[...]
    grad_probs = nt(grad_heads, vs[...])
    inside = jnp.sum(probs * grad_probs, axis=-1, keepdims=True)
    grad_scores = (probs * (grad_probs - inside) * scale).astype(BF16)
    gr[0, 0] = nn(grad_scores, ks[...]).astype(BF16)
    gr[0, 1] = tn(grad_scores, qs[...]).astype(BF16)
    gr[0, 2] = tn(probs.astype(BF16), grad_heads).astype(BF16)
    grads_copy = net.send(gr.at[0], gr.at[1], to_c)
    next(outward)
    next(small)
    sums = weight_sums()
    for copy in partner_qkv:
        copy.wait_recv()
    grads_copy.wait_recv()

    def fill_in(yy, pair):
        left = jnp.concatenate([gr[i, j] for i in range(2) for j in range(3)], axis=1)
        right = []
        for zz in pair:
            right.append(
                jnp.concatenate(
                    [wq[j, zz, yy, c] for j in range(3)] + [wqp[j, zz, yy] for j in range(3)],
                    axis=1,
                )
            )
        term = nt(left, jnp.concatenate(right, axis=0)).astype(BF16)
        p3[pair[0], yy] = term[:, :HD]
        p3[pair[1], yy] = term[:, HD:]

    def keep_grad(summed):
        gx_ref[...] = (ghs[...].astype(F32) + summed).astype(BF16)

    for i, _ in enumerate(scatter_ring(net, p3, fill_in, bufs2, keep_grad)):
        if i == 0:
            next(outward, None)
        if i < 4:
            next(sums)
        next(small, None)
    for _ in small:
        pass
    for _ in sums:
        pass
    net.drain()


def hand_out(*refs):
    sems = refs[8]
    copies = [pltpu.make_async_copy(refs[i], refs[4 + i], sems.at[i]) for i in range(4)]
    for copy in copies:
        copy.start()
    for copy in copies:
        copy.wait()


def ring_buffers():
    return [
        pltpu.VMEM((4, HALF, HD), BF16),
        pltpu.VMEM((4, HALF, HD), BF16),
        pltpu.VMEM((4, L, HD), BF16),
        pltpu.VMEM((4, L, HD), BF16),
        pltpu.VMEM((3, L, HD), BF16),
        pltpu.VMEM((HALF, HD), BF16),
        pltpu.VMEM((HALF, HD), BF16),
        pltpu.VMEM((L, HD), BF16),
        pltpu.VMEM((L, HD), BF16),
    ]


def shards(layer_input, frame_mask, w_qkv, w_out, w_in, step_embed, depth_gain, cotangent):
    def v(*shape, kind=BF16):
        return pltpu.VMEM(shape, kind)

    vmem = pl.BlockSpec(memory_space=pltpu.VMEM)
    hbm = pl.BlockSpec(memory_space=pltpu.HBM)
    scratch = [
        v(4, 4, 2, L, HD),
        v(1, L, kind=jnp.int32),
        v(STEPS, DD),
        v(DD),
        v(3, 4, 4, 2, HD, HD),
        v(3, 4, 4, HD, HD),
        v(HD, 32 * HD),
        v(16, HD, HD),
        v(HD, DD),
        v(DD, HD),
        v(DD, HD),
        v(STEPS, FR, DD),
        v(4, 4, 2, PIECE, HD),
        v(4, 4, PIECE, HD),
        v(4, 4, PIECE, HD),
        v(L, 3 * HD, kind=F32),
        v(L, HD),
        v(L, HD),
        v(L, HD),
        v(L, L, kind=F32),
        v(2, L, HD),
        v(4, 4, L, HD),
        v(L, HD),
        v(32 * ROWS, HD, kind=F32),
        v(4, 4, ROWS, HD),
        v(3, 4, ROWS, HD),
        v(4, ROWS, HD),
        v(3, ROWS, HD),
        v(ROWS, HD, kind=F32),
        v(ROWS, HD, kind=F32),
        v(4, 4, 2, ROWS, HD),
        v(32 * ROWS, HD, kind=F32),
        v(L, DD),
        v(L, HD),
        v(4, 4, L, HD),
        v(2, 3, L, HD),
        v(24, DD, kind=F32),
        v(16, 64, HD),
        v(3, 4, 64, HD),
        v(4, 64, HD),
        v(3, 64, HD),
        v(16, 64, HD),
        v(4, 4, 16, HD, kind=F32),
        v(3, 4, 16, HD, kind=F32),
        v(4, 16, HD, kind=F32),
        v(3, 16, HD, kind=F32),
        v(4, 16, HD, kind=F32),
        v(4, 16, HD, kind=F32),
        v(2, 16, HD, kind=F32),
        v(4, 4, 16, HD, kind=F32),
        *ring_buffers(),
        *ring_buffers(),
        pltpu.SemaphoreType.DMA((N_SEM,)),
        pltpu.SemaphoreType.DMA((N_SEM,)),
        pltpu.SemaphoreType.DMA((8,)),
    ]
    grad_x, grad_in, grad_step, grad_gain = pl.pallas_call(
        kernel,
        out_shape=(
            pltpu.VMEM((L, HD), BF16),
            pltpu.VMEM((HD, DD), BF16),
            pltpu.VMEM((STEPS, DD), F32),
            pltpu.VMEM((1, DD), F32),
        ),
        in_specs=[hbm] * 8,
        out_specs=(vmem,) * 4,
        scratch_shapes=scratch,
        compiler_params=pltpu.CompilerParams(
            collective_id=0, has_side_effects=True, vmem_limit_bytes=60 * 1024 * 1024
        ),
    )(
        layer_input[0],
        frame_mask,
        step_embed,
        depth_gain,
        w_qkv.reshape(3, 4, 4, 2, HD, HD),
        w_out,
        w_in,
        jnp.transpose(cotangent[0], (1, 0, 2)),
    )
    grad_x, grad_in, grad_step, grad_gain = pl.pallas_call(
        hand_out,
        out_shape=(
            jax.ShapeDtypeStruct((L, HD), BF16),
            jax.ShapeDtypeStruct((HD, DD), BF16),
            jax.ShapeDtypeStruct((STEPS, DD), F32),
            jax.ShapeDtypeStruct((1, DD), F32),
        ),
        in_specs=[vmem] * 4,
        out_specs=(hbm,) * 4,
        scratch_shapes=[pltpu.SemaphoreType.DMA((4,))],
        compiler_params=pltpu.CompilerParams(vmem_limit_bytes=2 * 1024 * 1024),
    )(grad_x, grad_in, grad_step, grad_gain)
    return (grad_x[None], grad_in, grad_step, grad_gain[0])


def solution(mesh):
    return jax.shard_map(
        shards,
        mesh=mesh,
        in_specs=(
            P("dp", None, "tensor"),
            P("dp", None),
            P(None, None, "tensor"),
            P("tensor", None),
            P("tensor", None),
            P(),
            P(),
            P("dp", "tensor", None, None),
        ),
        out_specs=(P("dp", None, "tensor"), P("tensor", None), P(), P()),
        check_vma=False,
    )
```

```python
import functools

import jax
import jax.numpy as jnp
from jax import lax
from jax.experimental import pallas as pl
from jax.experimental.pallas import tpu as pltpu
from jax.sharding import PartitionSpec as P

MESH = pl.DeviceIdType.MESH
F32 = jnp.float32
BF16 = jnp.bfloat16
L, HD, DD, STEPS, FR = 192, 128, 1024, 17, 6
HALF = L // 2
LO, HI = pl.ds(0, HALF), pl.ds(HALF, HALF)
ROWS = FR * (DD // HD)
PIECE = 64
N_SEM = 200


def nt(a, b):
    return lax.dot_general(a, b, (((1,), (1,)), ((), ())), preferred_element_type=F32)


def nn(a, b):
    return lax.dot_general(a, b, (((1,), (0,)), ((), ())), preferred_element_type=F32)


def tn(a, b):
    return lax.dot_general(a, b, (((0,), (0,)), ((), ())), preferred_element_type=F32)


def around(v):
    return (v + 1) % 4, (v + 3) % 4, (v + 2) % 4


class Net:
    def __init__(self, send_sems, recv_sems):
        self.send_sems, self.recv_sems = send_sems, recv_sems
        self.count = 0
        self.open = []
        dp, t = lax.axis_index("dp"), lax.axis_index("tensor")
        self.dp, self.t = dp, t
        self.x, self.zl = dp // 4, dp % 4
        self.z, self.y, self.c = t // 8, (t // 2) % 4, t % 2

    def go(self, z=0, y=0, c=0, x=0, zl=0):
        dp, t = self.dp, self.t
        if x or zl:
            dp = ((self.x + x) % 4) * 4 + (self.zl + zl) % 4
        if z or y or c:
            cc = (self.c + c) % 2
            t = ((self.z + z) % 4) * 8 + ((self.y + y) % 4) * 2 + cc
        return (dp, t)

    def peers(self):
        found = [self.go(c=1)]
        for d in (1, 2, 3):
            found += [self.go(y=d), self.go(z=d), self.go(x=d), self.go(zl=d)]
        return found

    def make(self, src, dst, peer):
        i = self.count
        self.count += 1
        return pltpu.make_async_remote_copy(
            src_ref=src,
            dst_ref=dst,
            send_sem=self.send_sems.at[i],
            recv_sem=self.recv_sems.at[i],
            device_id=peer,
            device_id_type=MESH,
        )

    def send(self, src, dst, peer):
        copy = self.make(src, dst, peer)
        copy.start()
        self.open.append(copy)
        return copy

    def drain(self):
        for copy in self.open:
            copy.wait_send()
        self.open = []


class Gather:
    def __init__(self, net, g):
        self.net, self.g = net, g
        self.planes = (net.z, around(net.z)[1], around(net.z)[0], around(net.z)[2])
        self.along, self.forward, self.across = {}, {}, {}
        self.to_yp, self.to_ym, self.to_c = net.go(y=1), net.go(y=3), net.go(c=1)

    def whole(self, zz, yy, peer):
        at = self.g.at[zz, yy, self.net.c]
        return self.net.send(at, at, peer)

    def part(self, zz, yy, rows, peer):
        at = self.g.at[zz, yy, self.net.c, rows]
        return self.net.send(at, at, peer)

    def begin(self):
        z, y = self.net.z, self.net.y
        to_zp, to_zm = self.net.go(z=1), self.net.go(z=3)
        self.up_lo = self.part(z, y, LO, to_zp)
        self.dn_hi = self.part(z, y, HI, to_zm)
        self.up_hi = self.part(z, y, HI, to_zp)
        self.dn_lo = self.part(z, y, LO, to_zm)
        self.spread(0)

    def along_z(self):
        y = self.net.y
        to_zp, to_zm = self.net.go(z=1), self.net.go(z=3)
        self.up_lo.wait_recv()
        self.on = self.part(self.planes[1], y, LO, to_zp)
        self.dn_hi.wait_recv()
        self.back = self.part(self.planes[2], y, HI, to_zm)
        self.up_hi.wait_recv()
        self.spread(1)
        self.dn_lo.wait_recv()
        self.spread(2)

    def far_z(self):
        self.on.wait_recv()
        self.back.wait_recv()
        self.spread(3)

    def spread(self, i):
        zz, y = self.planes[i], self.net.y
        if i == 3:
            self.along[i] = (
                self.part(zz, y, LO, self.to_yp),
                self.part(zz, y, HI, self.to_ym),
                self.part(zz, y, HI, self.to_yp),
                self.part(zz, y, LO, self.to_ym),
            )
        else:
            self.along[i] = (self.whole(zz, y, self.to_yp), self.whole(zz, y, self.to_ym))
        self.across[i] = []
        self.over(i, zz, y)

    def over(self, i, zz, yy):
        if i == 3:
            self.across[i].append(self.whole(zz, yy, self.to_c))

    def turn(self, i):
        zz = self.planes[i]
        yp, ym, _ = around(self.net.y)
        self.along[i][0].wait_recv()
        first = self.part(zz, ym, LO, self.to_yp)
        self.along[i][1].wait_recv()
        second = self.part(zz, yp, HI, self.to_ym)
        self.forward[i] = (first, second)
        for copy in self.along[i][2:]:
            copy.wait_recv()
        self.over(i, zz, ym)
        self.over(i, zz, yp)

    def land(self, i):
        for copy in self.forward[i]:
            copy.wait_recv()
        self.over(i, self.planes[i], around(self.net.y)[2])
        if i < 3:
            at = self.g.at[self.planes[i], pl.ds(0, 4), self.net.c]
            self.across[i].append(self.net.send(at, at, self.to_c))

    def here(self, i):
        for copy in self.across[i]:
            copy.wait_recv()


def scatter_ring(net, p, fill, bufs, done, ahead=False):
    ya, yb, yup, ydn, q, za, zb, zup, zdn = bufs
    z, y = net.z, net.y
    zp, zm, z2 = around(z)
    yp, ym, y2 = around(y)
    to_zp, to_zm, to_yp, to_ym = net.go(z=1), net.go(z=3), net.go(y=1), net.go(y=3)
    order = (z2, zp, zm, z)
    pairs = (order[:2], order[2:])

    far, near = [], [[], [], [], []]
    if ahead:
        for yy in (y2, yp, ym, y):
            for pair in pairs:
                fill(yy, pair)
        yield
    for pair in pairs:
        if not ahead:
            fill(y2, pair)
        for zz in pair:
            a = net.send(p.at[zz, y2, LO], ya.at[zz], to_yp)
            far.append((a, net.send(p.at[zz, y2, HI], yb.at[zz], to_ym)))

    def at_once(i):
        zz = order[i]
        near[i].append(net.send(p.at[zz, yp, HI], yup.at[zz, HI], to_yp))
        near[i].append(net.send(p.at[zz, ym, LO], ydn.at[zz, LO], to_ym))

    for j, pair in enumerate(pairs):
        if not ahead:
            fill(yp, pair)
            fill(ym, pair)
        at_once(2 * j)
        at_once(2 * j + 1)
    yield
    for i, zz in enumerate(order):
        far[i][0].wait_recv()
        p[zz, yp, LO] = (p[zz, yp, LO].astype(F32) + ya[zz].astype(F32)).astype(BF16)
        near[i].append(net.send(p.at[zz, yp, LO], yup.at[zz, LO], to_yp))
        far[i][1].wait_recv()
        p[zz, ym, HI] = (p[zz, ym, HI].astype(F32) + yb[zz].astype(F32)).astype(BF16)
        near[i].append(net.send(p.at[zz, ym, HI], ydn.at[zz, HI], to_ym))
    if not ahead:
        for pair in pairs:
            fill(y, pair)
    yield

    def mine(i):
        for copy in near[i]:
            copy.wait_recv()
        zz = order[i]
        return p[zz, y].astype(F32) + yup[zz].astype(F32) + ydn[zz].astype(F32)

    q[0] = mine(0).astype(BF16)
    a = net.send(q.at[0, LO], za, to_zp)
    b = net.send(q.at[0, HI], zb, to_zm)
    yield
    q[1] = mine(1).astype(BF16)
    last = [net.send(q.at[1, HI], zup.at[HI], to_zp)]
    q[2] = mine(2).astype(BF16)
    last.append(net.send(q.at[2, LO], zdn.at[LO], to_zm))
    yield
    a.wait_recv()
    q[1, LO] = (q[1, LO].astype(F32) + za[...].astype(F32)).astype(BF16)
    last.append(net.send(q.at[1, LO], zup.at[LO], to_zp))
    b.wait_recv()
    q[2, HI] = (q[2, HI].astype(F32) + zb[...].astype(F32)).astype(BF16)
    last.append(net.send(q.at[2, HI], zdn.at[HI], to_zm))
    yield
    total = mine(3)
    yield
    for copy in last:
        copy.wait_recv()
    done(total + zup[...].astype(F32) + zdn[...].astype(F32))


def kernel(
    x_hbm, mask_hbm, step_hbm, gain_hbm, wqkv_hbm, wout_hbm, win_hbm, cot_hbm,
    gx_ref, gw_ref, gs_ref, gg_ref,
    xg, maskv, stepv, gainv, wq, wqp, wo, wop, wi, wit, witp, cot,
    gm, mt, mtp,
    acc, qs, ks, vs, probs_s, hp, p1, hid, pf, p2, pyb, pq, pzb, pr, gpf,
    gpg, gpr, gpn, ghs, p3, gr, rows_s,
    wst, wxb, wsm, wzb, wfin,
    sst, syb, sm1, sxb, szb, slb, scb, sfin,
    *rest,
):
    bufs1, bufs2 = rest[:9], rest[9:18]
    send_sems, recv_sems, local_sems = rest[18:]
    net = Net(send_sems, recv_sems)
    x, zl, z, y, c = net.x, net.zl, net.z, net.y, net.c
    to_c = net.go(c=1)
    scale = HD ** (-0.5)

    barrier = pltpu.get_barrier_semaphore()
    peers = net.peers()
    for peer in peers:
        pl.semaphore_signal(barrier, inc=1, device_id=peer, device_id_type=MESH)
    loads = {}
    for i, (name, src, dst) in enumerate(
        (
            ("w_in", win_hbm, wi),
            ("x", x_hbm, xg.at[z, y, c]),
            ("w_out", wout_hbm, wo),
            ("w_qkv", wqkv_hbm, wq),
            ("mask", mask_hbm, maskv),
            ("step", step_hbm, stepv),
            ("gain", gain_hbm, gainv),
            ("cot", cot_hbm, cot),
        )
    ):
        loads[name] = pltpu.make_async_copy(src, dst, local_sems.at[i])
        loads[name].start()
    loads["w_in"].wait()
    for k in range(8):
        wit[k * HD : (k + 1) * HD, :] = wi[:, k * HD : (k + 1) * HD].T
    gm[z, y, c] = wit[pl.ds(pl.multiple_of(PIECE * net.dp, PIECE), PIECE), :]
    loads["x"].wait()
    pl.semaphore_wait(barrier, len(peers))

    every = pl.ds(0, 4)

    def weight_product():
        sent = [net.send(gm.at[z, y, c], gm.at[z, y, c], net.go(z=d)) for d in (1, 2, 3)]
        yield
        for copy in sent:
            copy.wait_recv()
        sent = [net.send(gm.at[every, y, c], gm.at[every, y, c], net.go(y=d)) for d in (1, 2, 3)]
        yield
        for copy in sent:
            copy.wait_recv()
        other = net.send(gm.at[every, every, c], gm.at[every, every, c], to_c)
        yield
        other.wait_recv()
        loads["w_out"].wait()
        left = jnp.concatenate(
            [gm[i, j, k] for i in range(4) for j in range(4) for k in range(2)], axis=1
        )
        mt[x, zl] = nt(left, wo[...]).astype(BF16)
        sent = [net.send(mt.at[x, zl], mt.at[x, zl], net.go(zl=d)) for d in (1, 2, 3)]
        yield
        for copy in sent:
            copy.wait_recv()
        sent = [net.send(mt.at[x], mt.at[x], net.go(x=d)) for d in (1, 2, 3)]
        last = [net.send(mt.at[x], mtp.at[x], to_c)]
        yield
        for d in (1, 2, 3):
            sent[d - 1].wait_recv()
            spot = (x + 4 - d) % 4
            last.append(net.send(mt.at[spot], mtp.at[spot], to_c))
        yield
        for copy in last:
            copy.wait_recv()

    def plane(i):
        zz = gather.planes[i]
        gather.here(i)
        left = jnp.concatenate([xg[zz, j, k] for j in range(4) for k in range(2)], axis=1)
        right = jnp.concatenate([wq[j, zz].reshape(DD, HD) for j in range(3)], axis=1)
        term = nn(left, right)
        acc[...] = term if i == 0 else acc[...] + term

    product = weight_product()
    gather = Gather(net, xg)
    gather.begin()
    next(product)
    next(product)
    gather.along_z()
    next(product)
    gather.turn(0)
    gather.far_z()
    gather.turn(1)
    gather.turn(2)
    gather.land(0)
    next(product)
    gather.turn(3)
    gather.land(1)
    gather.land(2)
    loads["w_qkv"].wait()
    plane(0)
    next(product)
    plane(1)
    gather.land(3)
    partner_in = net.send(wit, witp, to_c)
    plane(2)
    plane(3)

    spot = net.count
    partner_out = net.make(wop, wop, to_c)
    for i in range(16):
        cols = pl.ds(pl.multiple_of((2 * i + 1 - c) * HD, HD), HD)
        pltpu.make_async_remote_copy(
            src_ref=wout_hbm.at[:, cols],
            dst_ref=wop.at[i],
            send_sem=send_sems.at[spot],
            recv_sem=recv_sems.at[spot],
            device_id=to_c,
            device_id_type=MESH,
        ).start()
    net.open.append(partner_out)
    partner_qkv = []

    def swap_qkv(j):
        partner_qkv.append(net.send(wqkv_hbm.at[j, every, every, 1 - c], wqp.at[j], to_c))

    swap_qkv(0)

    query = acc[:, :HD].astype(BF16)
    key_rows = acc[:, HD : 2 * HD].astype(BF16)
    value = acc[:, 2 * HD :].astype(BF16)
    qs[...] = query
    ks[...] = key_rows
    vs[...] = value
    loads["mask"].wait()
    row = lax.broadcasted_iota(jnp.int32, (L, L), 0)
    col = lax.broadcasted_iota(jnp.int32, (L, L), 1)
    allowed = (col <= row) & ((maskv[...] == 1) | (col == row))
    scores = jnp.where(allowed, nt(query, key_rows) * scale, -1e30)
    next(product)
    raised = jnp.exp(scores - jnp.max(scores, axis=-1, keepdims=True))
    probs = raised / jnp.sum(raised, axis=-1, keepdims=True)
    probs_s[...] = probs
    hp[0] = nn(probs.astype(BF16), value).astype(BF16)
    heads_copy = net.send(hp.at[0], hp.at[1], to_c)
    partner_in.wait_recv()
    heads_copy.wait_recv()

    next(product, None)

    left = jnp.concatenate([hp[0], hp[1], xg[z, y, c], xg[z, y, 1 - c]], axis=1)
    right = jnp.concatenate(
        [mt[...].reshape(DD, HD), mtp[...].reshape(DD, HD), wit[...], witp[...]], axis=1
    )
    term = nt(left, right)
    for k in range(8):
        pf[pl.ds(k, L, stride=8), :] = term[:, k * HD : (k + 1) * HD]
    for i in range(4):
        for j in range(4):
            rows = pl.ds(pl.multiple_of((8 * i + 2 * j + c) * ROWS, 8), ROWS)
            p2[j, i] = pf[rows, :].astype(BF16)
    sent = [net.send(p2.at[(y + d) % 4], pyb.at[d - 1], net.go(y=d)) for d in (1, 2, 3)]

    def fill_out(yy, pair):
        left = jnp.concatenate([hp[0], hp[1]], axis=1)
        right = []
        for zz in pair:
            col0 = pl.multiple_of((zz * 8 + yy * 2 + c) * HD, HD)
            right.append(jnp.concatenate([wo[:, pl.ds(col0, HD)], wop[zz * 4 + yy]], axis=0))
        term = nn(left, jnp.concatenate(right, axis=1)).astype(BF16)
        p1[pair[0], yy] = term[:, :HD]
        p1[pair[1], yy] = term[:, HD:]

    def keep_hidden(summed):
        hid[...] = (xg[z, y, c].astype(F32) + summed).astype(BF16)

    outward = scatter_ring(net, p1, fill_out, bufs1, keep_hidden, ahead=True)
    partner_out.wait_recv()
    next(outward)
    total = p2[y].astype(F32)
    for d in range(3):
        sent[d].wait_recv()
        total += pyb[d].astype(F32)
    pq[...] = total.astype(BF16)
    sent = [net.send(pq.at[(z + d) % 4], pzb.at[d - 1], net.go(z=d)) for d in (1, 2, 3)]

    next(outward)
    total = pq[z].astype(F32)
    for d in range(3):
        sent[d].wait_recv()
        total += pzb[d].astype(F32)
    pr[...] = total
    swap_qkv(1)

    for name in ("step", "gain", "cot"):
        loads[name].wait()
    gains = gainv[...].astype(F32)[None]
    proj = jnp.concatenate([pr[pl.ds(k, FR, stride=8), :] for k in range(8)], axis=1)
    grad_rows = jnp.zeros((FR, DD), F32)
    gain_rows = jnp.zeros((FR, DD), F32)
    for s in range(STEPS):
        if s == 8:
            next(outward)
        inner = proj + stepv[s : s + 1, :].astype(F32)
        inverse = lax.rsqrt(jnp.mean(inner * inner, axis=-1, keepdims=True) + 1e-06)
        arriving = cot[s].astype(F32)
        gain_rows += arriving * inner * inverse
        scaled = arriving * gains
        mixed = jnp.mean(inner * scaled, axis=-1, keepdims=True)
        grad_inner = inverse * scaled - inverse * inverse * inverse * inner * mixed
        grad_rows += grad_inner
        rows_s[s : s + 1, :] = jnp.sum(grad_inner, axis=0, keepdims=True)
    for k in range(8):
        gpf[pl.ds(k, FR, stride=8), :] = grad_rows[:, k * HD : (k + 1) * HD]
    gpg[z, y, c] = gpf[...].astype(BF16)

    sent = [net.send(gpg.at[z, y, c], gpg.at[z, y, c], net.go(z=d)) for d in (1, 2, 3)]
    next(outward)
    rows_s[STEPS : STEPS + 1, :] = jnp.sum(gain_rows, axis=0, keepdims=True)
    for k in range(8):
        cols = slice(k * HD, (k + 1) * HD)
        j, i = k // 2, 2 * (k % 2)
        sst[j, i] = rows_s[:16, cols]
        sst[j, i + 1] = jnp.zeros((16, HD), F32)
        sst[j, i + 1, 0:2] = rows_s[16:18, cols]

    def small_sums():
        sent = [net.send(sst.at[(y + d) % 4], syb.at[d - 1], net.go(y=d)) for d in (1, 2, 3)]
        yield
        total = sst[y]
        for d in range(3):
            sent[d].wait_recv()
            total += syb[d]
        sm1[...] = total
        sent = [net.send(sm1.at[(x + d) % 4], sxb.at[d - 1], net.go(x=d)) for d in (1, 2, 3)]
        yield
        total = sm1[x]
        for d in range(3):
            sent[d].wait_recv()
            total += sxb[d]
        szb[z] = total
        sent = [net.send(szb.at[z], szb.at[z], net.go(z=d)) for d in (1, 2, 3)]
        yield
        for copy in sent:
            copy.wait_recv()
        slb[zl] = szb[0] + szb[1] + szb[2] + szb[3]
        sent = [net.send(slb.at[zl], slb.at[zl], net.go(zl=d)) for d in (1, 2, 3)]
        yield
        for copy in sent:
            copy.wait_recv()
        scb[c] = slb[0] + slb[1] + slb[2] + slb[3]
        other = net.send(scb.at[c], scb.at[c], to_c)
        yield
        other.wait_recv()
        sfin[y, x] = scb[0] + scb[1]
        sent = [net.send(sfin.at[y, x], sfin.at[y, x], net.go(x=d)) for d in (1, 2, 3)]
        yield
        for copy in sent:
            copy.wait_recv()
        sent = [net.send(sfin.at[y], sfin.at[y], net.go(y=d)) for d in (1, 2, 3)]
        yield
        for copy in sent:
            copy.wait_recv()
        for k in range(8):
            cols = slice(k * HD, (k + 1) * HD)
            j, i = k // 2, 2 * (k % 2)
            gs_ref[0:16, cols] = sfin[j, i]
            gs_ref[16:17, cols] = sfin[j, i + 1, 0:1]
            gg_ref[0:1, cols] = sfin[j, i + 1, 1:2]

    def weight_sums():
        grads = tn(hid[...], gpn[...]).astype(BF16)
        for k in range(8):
            cols = slice(k * HD, (k + 1) * HD)
            wst[2 * k] = grads[:64, cols]
            wst[2 * k + 1] = grads[64:, cols]
        sent = []
        for d in (1, 2, 3):
            rows = pl.ds(4 * ((x + d) % 4), 4)
            sent.append(net.send(wst.at[rows], wxb.at[d - 1], net.go(x=d)))
        yield
        total = wst[pl.ds(4 * x, 4)].astype(F32)
        for d in range(3):
            sent[d].wait_recv()
            total += wxb[d].astype(F32)
        wsm[...] = total.astype(BF16)
        sent = [net.send(wsm.at[(zl + d) % 4], wzb.at[d - 1], net.go(zl=d)) for d in (1, 2, 3)]
        yield
        total = wsm[zl].astype(F32)
        for d in range(3):
            sent[d].wait_recv()
            total += wzb[d].astype(F32)
        spot = 4 * x + zl
        wfin[spot] = total.astype(BF16)
        sent = [net.send(wfin.at[spot], wfin.at[spot], net.go(zl=d)) for d in (1, 2, 3)]
        yield
        for copy in sent:
            copy.wait_recv()
        rows = pl.ds(4 * x, 4)
        sent = [net.send(wfin.at[rows], wfin.at[rows], net.go(x=d)) for d in (1, 2, 3)]
        yield
        for copy in sent:
            copy.wait_recv()
        for k in range(8):
            cols = slice(k * HD, (k + 1) * HD)
            gw_ref[0:64, cols] = wfin[2 * k]
            gw_ref[64:128, cols] = wfin[2 * k + 1]

    for copy in sent:
        copy.wait_recv()
    sent = [net.send(gpg.at[every, y, c], gpg.at[every, y, c], net.go(y=d)) for d in (1, 2, 3)]
    next(outward)
    next(outward)
    for copy in sent:
        copy.wait_recv()
    other = net.send(gpg.at[every, every, c], gpg.at[every, every, c], to_c)
    swap_qkv(2)
    small = small_sums()
    next(small)
    next(outward)
    next(outward, None)
    other.wait_recv()
    gpr[...] = gpg[...].reshape(32 * ROWS, HD).astype(F32)
    for k in range(8):
        gpn[:, k * HD : (k + 1) * HD] = gpr[pl.ds(k, L, stride=8), :].astype(BF16)
    back = nn(gpn[...], jnp.concatenate([mt[...].reshape(DD, HD), wit[...]], axis=1))
    ghs[...] = back[:, HD:].astype(BF16)
    sums = weight_sums()
    next(sums)
    next(small)

    grad_heads = back[:, :HD].astype(BF16)
    probs = probs_s[...]
    grad_probs = nt(grad_heads, vs[...])
    inside = jnp.sum(probs * grad_probs, axis=-1, keepdims=True)
    grad_scores = (probs * (grad_probs - inside) * scale).astype(BF16)
    gr[0, 0] = nn(grad_scores, ks[...]).astype(BF16)
    gr[0, 1] = tn(grad_scores, qs[...]).astype(BF16)
    gr[0, 2] = tn(probs.astype(BF16), grad_heads).astype(BF16)
    grads_copy = net.send(gr.at[0], gr.at[1], to_c)
    next(sums)
    next(small)
    for copy in partner_qkv:
        copy.wait_recv()
    grads_copy.wait_recv()

    def fill_in(yy, pair):
        left = jnp.concatenate([gr[i, j] for i in range(2) for j in range(3)], axis=1)
        right = []
        for zz in pair:
            right.append(
                jnp.concatenate(
                    [wq[j, zz, yy, c] for j in range(3)] + [wqp[j, zz, yy] for j in range(3)],
                    axis=1,
                )
            )
        term = nt(left, jnp.concatenate(right, axis=0)).astype(BF16)
        p3[pair[0], yy] = term[:, :HD]
        p3[pair[1], yy] = term[:, HD:]

    def keep_grad(summed):
        gx_ref[...] = (ghs[...].astype(F32) + summed).astype(BF16)

    for i, _ in enumerate(scatter_ring(net, p3, fill_in, bufs2, keep_grad)):
        if i < 2:
            next(sums)
        next(small, None)
    for _ in small:
        pass
    for _ in sums:
        pass
    net.drain()


def hand_out(*refs):
    sems = refs[8]
    copies = [pltpu.make_async_copy(refs[i], refs[4 + i], sems.at[i]) for i in range(4)]
    for copy in copies:
        copy.start()
    for copy in copies:
        copy.wait()


def ring_buffers():
    return [
        pltpu.VMEM((4, HALF, HD), BF16),
        pltpu.VMEM((4, HALF, HD), BF16),
        pltpu.VMEM((4, L, HD), BF16),
        pltpu.VMEM((4, L, HD), BF16),
        pltpu.VMEM((3, L, HD), BF16),
        pltpu.VMEM((HALF, HD), BF16),
        pltpu.VMEM((HALF, HD), BF16),
        pltpu.VMEM((L, HD), BF16),
        pltpu.VMEM((L, HD), BF16),
    ]


def shards(layer_input, frame_mask, w_qkv, w_out, w_in, step_embed, depth_gain, cotangent):
    def v(*shape, kind=BF16):
        return pltpu.VMEM(shape, kind)

    vmem = pl.BlockSpec(memory_space=pltpu.VMEM)
    hbm = pl.BlockSpec(memory_space=pltpu.HBM)
    scratch = [
        v(4, 4, 2, L, HD),
        v(1, L, kind=jnp.int32),
        v(STEPS, DD),
        v(DD),
        v(3, 4, 4, 2, HD, HD),
        v(3, 4, 4, HD, HD),
        v(HD, 32 * HD),
        v(16, HD, HD),
        v(HD, DD),
        v(DD, HD),
        v(DD, HD),
        v(STEPS, FR, DD),
        v(4, 4, 2, PIECE, HD),
        v(4, 4, PIECE, HD),
        v(4, 4, PIECE, HD),
        v(L, 3 * HD, kind=F32),
        v(L, HD),
        v(L, HD),
        v(L, HD),
        v(L, L, kind=F32),
        v(2, L, HD),
        v(4, 4, L, HD),
        v(L, HD),
        v(32 * ROWS, HD, kind=F32),
        v(4, 4, ROWS, HD),
        v(3, 4, ROWS, HD),
        v(4, ROWS, HD),
        v(3, ROWS, HD),
        v(ROWS, HD, kind=F32),
        v(ROWS, HD, kind=F32),
        v(4, 4, 2, ROWS, HD),
        v(32 * ROWS, HD, kind=F32),
        v(L, DD),
        v(L, HD),
        v(4, 4, L, HD),
        v(2, 3, L, HD),
        v(24, DD, kind=F32),
        v(16, 64, HD),
        v(3, 4, 64, HD),
        v(4, 64, HD),
        v(3, 64, HD),
        v(16, 64, HD),
        v(4, 4, 16, HD, kind=F32),
        v(3, 4, 16, HD, kind=F32),
        v(4, 16, HD, kind=F32),
        v(3, 16, HD, kind=F32),
        v(4, 16, HD, kind=F32),
        v(4, 16, HD, kind=F32),
        v(2, 16, HD, kind=F32),
        v(4, 4, 16, HD, kind=F32),
        *ring_buffers(),
        *ring_buffers(),
        pltpu.SemaphoreType.DMA((N_SEM,)),
        pltpu.SemaphoreType.DMA((N_SEM,)),
        pltpu.SemaphoreType.DMA((8,)),
    ]
    grad_x, grad_in, grad_step, grad_gain = pl.pallas_call(
        kernel,
        out_shape=(
            pltpu.VMEM((L, HD), BF16),
            pltpu.VMEM((HD, DD), BF16),
            pltpu.VMEM((STEPS, DD), F32),
            pltpu.VMEM((1, DD), F32),
        ),
        in_specs=[hbm] * 8,
        out_specs=(vmem,) * 4,
        scratch_shapes=scratch,
        compiler_params=pltpu.CompilerParams(
            collective_id=0, has_side_effects=True, vmem_limit_bytes=60 * 1024 * 1024
        ),
    )(
        layer_input[0],
        frame_mask,
        step_embed,
        depth_gain,
        w_qkv.reshape(3, 4, 4, 2, HD, HD),
        w_out,
        w_in,
        jnp.transpose(cotangent[0], (1, 0, 2)),
    )
    grad_x, grad_in, grad_step, grad_gain = pl.pallas_call(
        hand_out,
        out_shape=(
            jax.ShapeDtypeStruct((L, HD), BF16),
            jax.ShapeDtypeStruct((HD, DD), BF16),
            jax.ShapeDtypeStruct((STEPS, DD), F32),
            jax.ShapeDtypeStruct((1, DD), F32),
        ),
        in_specs=[vmem] * 4,
        out_specs=(hbm,) * 4,
        scratch_shapes=[pltpu.SemaphoreType.DMA((4,))],
        compiler_params=pltpu.CompilerParams(vmem_limit_bytes=2 * 1024 * 1024),
    )(grad_x, grad_in, grad_step, grad_gain)
    return (grad_x[None], grad_in, grad_step, grad_gain[0])


def solution(mesh):
    return jax.shard_map(
        shards,
        mesh=mesh,
        in_specs=(
            P("dp", None, "tensor"),
            P("dp", None),
            P(None, None, "tensor"),
            P("tensor", None),
            P("tensor", None),
            P(),
            P(),
            P("dp", "tensor", None, None),
        ),
        out_specs=(P("dp", None, "tensor"), P("tensor", None), P(), P()),
        check_vma=False,
    )
```

```python
import functools

import jax
import jax.numpy as jnp
from jax import lax
from jax.experimental import pallas as pl
from jax.experimental.pallas import tpu as pltpu
from jax.sharding import PartitionSpec as P

MESH = pl.DeviceIdType.MESH
F32 = jnp.float32
BF16 = jnp.bfloat16
L, HD, DD, STEPS, FR = 192, 128, 1024, 17, 6
HALF = L // 2
LO, HI = pl.ds(0, HALF), pl.ds(HALF, HALF)
ROWS = FR * (DD // HD)
PIECE = 64
N_SEM = 200


def nt(a, b):
    return lax.dot_general(a, b, (((1,), (1,)), ((), ())), preferred_element_type=F32)


def nn(a, b):
    return lax.dot_general(a, b, (((1,), (0,)), ((), ())), preferred_element_type=F32)


def tn(a, b):
    return lax.dot_general(a, b, (((0,), (0,)), ((), ())), preferred_element_type=F32)


def around(v):
    return (v + 1) % 4, (v + 3) % 4, (v + 2) % 4


class Net:
    def __init__(self, send_sems, recv_sems):
        self.send_sems, self.recv_sems = send_sems, recv_sems
        self.count = 0
        self.open = []
        dp, t = lax.axis_index("dp"), lax.axis_index("tensor")
        self.dp, self.t = dp, t
        self.x, self.zl = dp // 4, dp % 4
        self.z, self.y, self.c = t // 8, (t // 2) % 4, t % 2

    def go(self, z=0, y=0, c=0, x=0, zl=0):
        dp, t = self.dp, self.t
        if x or zl:
            dp = ((self.x + x) % 4) * 4 + (self.zl + zl) % 4
        if z or y or c:
            cc = (self.c + c) % 2
            t = ((self.z + z) % 4) * 8 + ((self.y + y) % 4) * 2 + cc
        return (dp, t)

    def peers(self):
        found = [self.go(c=1)]
        for d in (1, 2, 3):
            found += [self.go(y=d), self.go(z=d), self.go(x=d), self.go(zl=d)]
        return found

    def make(self, src, dst, peer):
        i = self.count
        self.count += 1
        return pltpu.make_async_remote_copy(
            src_ref=src,
            dst_ref=dst,
            send_sem=self.send_sems.at[i],
            recv_sem=self.recv_sems.at[i],
            device_id=peer,
            device_id_type=MESH,
        )

    def send(self, src, dst, peer):
        copy = self.make(src, dst, peer)
        copy.start()
        self.open.append(copy)
        return copy

    def drain(self):
        for copy in self.open:
            copy.wait_send()
        self.open = []


class Gather:
    def __init__(self, net, g):
        self.net, self.g = net, g
        self.planes = (net.z, around(net.z)[1], around(net.z)[0], around(net.z)[2])
        self.along, self.forward, self.across = {}, {}, {}
        self.to_yp, self.to_ym, self.to_c = net.go(y=1), net.go(y=3), net.go(c=1)

    def whole(self, zz, yy, peer):
        at = self.g.at[zz, yy, self.net.c]
        return self.net.send(at, at, peer)

    def part(self, zz, yy, rows, peer):
        at = self.g.at[zz, yy, self.net.c, rows]
        return self.net.send(at, at, peer)

    def begin(self):
        z, y = self.net.z, self.net.y
        to_zp, to_zm = self.net.go(z=1), self.net.go(z=3)
        self.up_lo = self.part(z, y, LO, to_zp)
        self.dn_hi = self.part(z, y, HI, to_zm)
        self.up_hi = self.part(z, y, HI, to_zp)
        self.dn_lo = self.part(z, y, LO, to_zm)
        self.spread(0, LO)
        self.spread(0, HI)

    def along_z(self):
        y = self.net.y
        to_zp, to_zm = self.net.go(z=1), self.net.go(z=3)
        self.up_lo.wait_recv()
        self.on = self.part(self.planes[1], y, LO, to_zp)
        self.dn_hi.wait_recv()
        self.back = self.part(self.planes[2], y, HI, to_zm)
        self.spread(1, LO)
        self.spread(2, HI)
        self.up_hi.wait_recv()
        self.spread(1, HI)
        self.dn_lo.wait_recv()
        self.spread(2, LO)

    def far_z(self):
        self.on.wait_recv()
        self.spread(3, LO)
        self.back.wait_recv()
        self.spread(3, HI)

    def spread(self, i, rows):
        zz, y = self.planes[i], self.net.y
        up = self.part(zz, y, rows, self.to_yp)
        self.along[i, rows.start] = (up, self.part(zz, y, rows, self.to_ym))
        self.across.setdefault(i, [])
        if rows.start == (HI if i == 3 else LO).start:
            self.over(i, zz, y)

    def over(self, i, zz, yy):
        if i == 3:
            self.across[i].append(self.whole(zz, yy, self.to_c))

    def turn(self, i):
        zz = self.planes[i]
        yp, ym, _ = around(self.net.y)
        lo, hi = self.along[i, LO.start], self.along[i, HI.start]
        lo[0].wait_recv()
        first = self.part(zz, ym, LO, self.to_yp)
        hi[1].wait_recv()
        second = self.part(zz, yp, HI, self.to_ym)
        self.forward[i] = (first, second)
        hi[0].wait_recv()
        self.over(i, zz, ym)
        lo[1].wait_recv()
        self.over(i, zz, yp)

    def land(self, i):
        for copy in self.forward[i]:
            copy.wait_recv()
        self.over(i, self.planes[i], around(self.net.y)[2])
        if i < 3:
            at = self.g.at[self.planes[i], pl.ds(0, 4), self.net.c]
            self.across[i].append(self.net.send(at, at, self.to_c))

    def here(self, i):
        for copy in self.across[i]:
            copy.wait_recv()


def scatter_ring(net, p, fill, bufs, done, ahead=False):
    ya, yb, yup, ydn, q, za, zb, zup, zdn = bufs
    z, y = net.z, net.y
    zp, zm, z2 = around(z)
    yp, ym, y2 = around(y)
    to_zp, to_zm, to_yp, to_ym = net.go(z=1), net.go(z=3), net.go(y=1), net.go(y=3)
    order = (z2, zp, zm, z)
    pairs = (order[:2], order[2:])

    far, near = [], [[], [], [], []]
    if ahead:
        for yy in (y2, yp, ym, y):
            for pair in pairs:
                fill(yy, pair)
        yield
    for pair in pairs:
        if not ahead:
            fill(y2, pair)
        for zz in pair:
            a = net.send(p.at[zz, y2, LO], ya.at[zz], to_yp)
            far.append((a, net.send(p.at[zz, y2, HI], yb.at[zz], to_ym)))

    def at_once(i):
        zz = order[i]
        near[i].append(net.send(p.at[zz, yp, HI], yup.at[zz, HI], to_yp))
        near[i].append(net.send(p.at[zz, ym, LO], ydn.at[zz, LO], to_ym))

    for j, pair in enumerate(pairs):
        if not ahead:
            fill(yp, pair)
            fill(ym, pair)
        at_once(2 * j)
        at_once(2 * j + 1)
    yield
    for i, zz in enumerate(order):
        far[i][0].wait_recv()
        p[zz, yp, LO] = (p[zz, yp, LO].astype(F32) + ya[zz].astype(F32)).astype(BF16)
        near[i].append(net.send(p.at[zz, yp, LO], yup.at[zz, LO], to_yp))
        far[i][1].wait_recv()
        p[zz, ym, HI] = (p[zz, ym, HI].astype(F32) + yb[zz].astype(F32)).astype(BF16)
        near[i].append(net.send(p.at[zz, ym, HI], ydn.at[zz, HI], to_ym))
    if not ahead:
        for pair in pairs:
            fill(y, pair)
    yield

    def mine(i):
        for copy in near[i]:
            copy.wait_recv()
        zz = order[i]
        return p[zz, y].astype(F32) + yup[zz].astype(F32) + ydn[zz].astype(F32)

    q[0] = mine(0).astype(BF16)
    a = net.send(q.at[0, LO], za, to_zp)
    b = net.send(q.at[0, HI], zb, to_zm)
    yield
    q[1] = mine(1).astype(BF16)
    last = [net.send(q.at[1, HI], zup.at[HI], to_zp)]
    q[2] = mine(2).astype(BF16)
    last.append(net.send(q.at[2, LO], zdn.at[LO], to_zm))
    yield
    a.wait_recv()
    q[1, LO] = (q[1, LO].astype(F32) + za[...].astype(F32)).astype(BF16)
    last.append(net.send(q.at[1, LO], zup.at[LO], to_zp))
    b.wait_recv()
    q[2, HI] = (q[2, HI].astype(F32) + zb[...].astype(F32)).astype(BF16)
    last.append(net.send(q.at[2, HI], zdn.at[HI], to_zm))
    yield
    total = mine(3)
    yield
    for copy in last:
        copy.wait_recv()
    done(total + zup[...].astype(F32) + zdn[...].astype(F32))


def kernel(
    x_hbm, mask_hbm, step_hbm, gain_hbm, wqkv_hbm, wout_hbm, win_hbm, cot_hbm,
    gx_ref, gw_ref, gs_ref, gg_ref,
    xg, maskv, stepv, gainv, wq, wqp, wo, wop, wi, wit, witp, cot,
    gm, mt, mtp,
    acc, qs, ks, vs, probs_s, hp, p1, hid, pf, p2, pyb, pq, pzb, pr, gpf,
    gpg, gpr, gpn, ghs, p3, gr, rows_s,
    wst, wxb, wsm, wzb, wfin,
    sst, syb, sm1, sxb, szb, slb, scb, sfin,
    *rest,
):
    bufs1, bufs2 = rest[:9], rest[9:18]
    send_sems, recv_sems, local_sems = rest[18:]
    net = Net(send_sems, recv_sems)
    x, zl, z, y, c = net.x, net.zl, net.z, net.y, net.c
    to_c = net.go(c=1)
    scale = HD ** (-0.5)

    barrier = pltpu.get_barrier_semaphore()
    peers = net.peers()
    for peer in peers:
        pl.semaphore_signal(barrier, inc=1, device_id=peer, device_id_type=MESH)
    loads = {}
    for i, (name, src, dst) in enumerate(
        (
            ("w_in", win_hbm, wi),
            ("x", x_hbm, xg.at[z, y, c]),
            ("w_out", wout_hbm, wo),
            ("w_qkv", wqkv_hbm, wq),
            ("mask", mask_hbm, maskv),
            ("step", step_hbm, stepv),
            ("gain", gain_hbm, gainv),
            ("cot", cot_hbm, cot),
        )
    ):
        loads[name] = pltpu.make_async_copy(src, dst, local_sems.at[i])
        loads[name].start()
    loads["w_in"].wait()
    for k in range(8):
        wit[k * HD : (k + 1) * HD, :] = wi[:, k * HD : (k + 1) * HD].T
    gm[z, y, c] = wit[pl.ds(pl.multiple_of(PIECE * net.dp, PIECE), PIECE), :]
    loads["x"].wait()
    pl.semaphore_wait(barrier, len(peers))

    every = pl.ds(0, 4)

    def weight_product():
        sent = [net.send(gm.at[z, y, c], gm.at[z, y, c], net.go(z=d)) for d in (1, 2, 3)]
        yield
        for copy in sent:
            copy.wait_recv()
        sent = [net.send(gm.at[every, y, c], gm.at[every, y, c], net.go(y=d)) for d in (1, 2, 3)]
        yield
        for copy in sent:
            copy.wait_recv()
        other = net.send(gm.at[every, every, c], gm.at[every, every, c], to_c)
        yield
        other.wait_recv()
        loads["w_out"].wait()
        left = jnp.concatenate(
            [gm[i, j, k] for i in range(4) for j in range(4) for k in range(2)], axis=1
        )
        mt[x, zl] = nt(left, wo[...]).astype(BF16)
        sent = [net.send(mt.at[x, zl], mt.at[x, zl], net.go(zl=d)) for d in (1, 2, 3)]
        yield
        for copy in sent:
            copy.wait_recv()
        sent = [net.send(mt.at[x], mt.at[x], net.go(x=d)) for d in (1, 2, 3)]
        last = [net.send(mt.at[x], mtp.at[x], to_c)]
        yield
        for d in (1, 2, 3):
            sent[d - 1].wait_recv()
            spot = (x + 4 - d) % 4
            last.append(net.send(mt.at[spot], mtp.at[spot], to_c))
        yield
        for copy in last:
            copy.wait_recv()

    def plane(i):
        zz = gather.planes[i]
        gather.here(i)
        left = jnp.concatenate([xg[zz, j, k] for j in range(4) for k in range(2)], axis=1)
        right = jnp.concatenate([wq[j, zz].reshape(DD, HD) for j in range(3)], axis=1)
        term = nn(left, right)
        acc[...] = term if i == 0 else acc[...] + term

    product = weight_product()
    gather = Gather(net, xg)
    gather.begin()
    next(product)
    gather.along_z()
    next(product)
    gather.turn(0)
    gather.far_z()
    gather.turn(1)
    gather.turn(2)
    gather.land(0)
    next(product)
    gather.turn(3)
    gather.land(1)
    gather.land(2)
    next(product)
    loads["w_qkv"].wait()
    plane(0)
    next(product)
    plane(1)
    gather.land(3)
    partner_in = net.send(wit, witp, to_c)
    plane(2)
    plane(3)

    spot = net.count
    partner_out = net.make(wop, wop, to_c)
    for i in range(16):
        cols = pl.ds(pl.multiple_of((2 * i + 1 - c) * HD, HD), HD)
        pltpu.make_async_remote_copy(
            src_ref=wout_hbm.at[:, cols],
            dst_ref=wop.at[i],
            send_sem=send_sems.at[spot],
            recv_sem=recv_sems.at[spot],
            device_id=to_c,
            device_id_type=MESH,
        ).start()
    net.open.append(partner_out)
    partner_qkv = []

    def swap_qkv(j):
        partner_qkv.append(net.send(wqkv_hbm.at[j, every, every, 1 - c], wqp.at[j], to_c))

    swap_qkv(0)

    query = acc[:, :HD].astype(BF16)
    key_rows = acc[:, HD : 2 * HD].astype(BF16)
    value = acc[:, 2 * HD :].astype(BF16)
    qs[...] = query
    ks[...] = key_rows
    vs[...] = value
    loads["mask"].wait()
    row = lax.broadcasted_iota(jnp.int32, (L, L), 0)
    col = lax.broadcasted_iota(jnp.int32, (L, L), 1)
    allowed = (col <= row) & ((maskv[...] == 1) | (col == row))
    scores = jnp.where(allowed, nt(query, key_rows) * scale, -1e30)
    raised = jnp.exp(scores - jnp.max(scores, axis=-1, keepdims=True))
    probs = raised / jnp.sum(raised, axis=-1, keepdims=True)
    probs_s[...] = probs
    hp[0] = nn(probs.astype(BF16), value).astype(BF16)
    heads_copy = net.send(hp.at[0], hp.at[1], to_c)
    next(product)
    partner_in.wait_recv()
    heads_copy.wait_recv()

    next(product, None)

    left = jnp.concatenate([hp[0], hp[1], xg[z, y, c], xg[z, y, 1 - c]], axis=1)
    right = jnp.concatenate(
        [mt[...].reshape(DD, HD), mtp[...].reshape(DD, HD), wit[...], witp[...]], axis=1
    )
    term = nt(left, right)
    for k in range(8):
        pf[pl.ds(k, L, stride=8), :] = term[:, k * HD : (k + 1) * HD]
    for i in range(4):
        for j in range(4):
            rows = pl.ds(pl.multiple_of((8 * i + 2 * j + c) * ROWS, 8), ROWS)
            p2[j, i] = pf[rows, :].astype(BF16)
    sent = [net.send(p2.at[(y + d) % 4], pyb.at[d - 1], net.go(y=d)) for d in (1, 2, 3)]

    def fill_out(yy, pair):
        left = jnp.concatenate([hp[0], hp[1]], axis=1)
        right = []
        for zz in pair:
            col0 = pl.multiple_of((zz * 8 + yy * 2 + c) * HD, HD)
            right.append(jnp.concatenate([wo[:, pl.ds(col0, HD)], wop[zz * 4 + yy]], axis=0))
        term = nn(left, jnp.concatenate(right, axis=1)).astype(BF16)
        p1[pair[0], yy] = term[:, :HD]
        p1[pair[1], yy] = term[:, HD:]

    def keep_hidden(summed):
        hid[...] = (xg[z, y, c].astype(F32) + summed).astype(BF16)

    outward = scatter_ring(net, p1, fill_out, bufs1, keep_hidden, ahead=True)
    partner_out.wait_recv()
    next(outward)
    total = p2[y].astype(F32)
    for d in range(3):
        sent[d].wait_recv()
        total += pyb[d].astype(F32)
    pq[...] = total.astype(BF16)
    sent = [net.send(pq.at[(z + d) % 4], pzb.at[d - 1], net.go(z=d)) for d in (1, 2, 3)]

    next(outward)
    total = pq[z].astype(F32)
    for d in range(3):
        sent[d].wait_recv()
        total += pzb[d].astype(F32)
    pr[...] = total
    swap_qkv(1)

    for name in ("step", "gain", "cot"):
        loads[name].wait()
    gains = gainv[...].astype(F32)[None]
    proj = jnp.concatenate([pr[pl.ds(k, FR, stride=8), :] for k in range(8)], axis=1)
    grad_rows = jnp.zeros((FR, DD), F32)
    gain_rows = jnp.zeros((FR, DD), F32)
    for s in range(STEPS):
        inner = proj + stepv[s : s + 1, :].astype(F32)
        inverse = lax.rsqrt(jnp.mean(inner * inner, axis=-1, keepdims=True) + 1e-06)
        arriving = cot[s].astype(F32)
        gain_rows += arriving * inner * inverse
        scaled = arriving * gains
        mixed = jnp.mean(inner * scaled, axis=-1, keepdims=True)
        grad_inner = inverse * scaled - inverse * inverse * inverse * inner * mixed
        grad_rows += grad_inner
        rows_s[s : s + 1, :] = jnp.sum(grad_inner, axis=0, keepdims=True)
    for k in range(8):
        gpf[pl.ds(k, FR, stride=8), :] = grad_rows[:, k * HD : (k + 1) * HD]
    gpg[z, y, c] = gpf[...].astype(BF16)

    sent = [net.send(gpg.at[z, y, c], gpg.at[z, y, c], net.go(z=d)) for d in (1, 2, 3)]
    next(outward)
    rows_s[STEPS : STEPS + 1, :] = jnp.sum(gain_rows, axis=0, keepdims=True)
    for k in range(8):
        cols = slice(k * HD, (k + 1) * HD)
        j, i = k // 2, 2 * (k % 2)
        sst[j, i] = rows_s[:16, cols]
        sst[j, i + 1] = jnp.zeros((16, HD), F32)
        sst[j, i + 1, 0:2] = rows_s[16:18, cols]

    def small_sums():
        sent = [net.send(sst.at[(y + d) % 4], syb.at[d - 1], net.go(y=d)) for d in (1, 2, 3)]
        yield
        total = sst[y]
        for d in range(3):
            sent[d].wait_recv()
            total += syb[d]
        sm1[...] = total
        sent = [net.send(sm1.at[(x + d) % 4], sxb.at[d - 1], net.go(x=d)) for d in (1, 2, 3)]
        yield
        total = sm1[x]
        for d in range(3):
            sent[d].wait_recv()
            total += sxb[d]
        szb[z] = total
        sent = [net.send(szb.at[z], szb.at[z], net.go(z=d)) for d in (1, 2, 3)]
        yield
        for copy in sent:
            copy.wait_recv()
        slb[zl] = szb[0] + szb[1] + szb[2] + szb[3]
        sent = [net.send(slb.at[zl], slb.at[zl], net.go(zl=d)) for d in (1, 2, 3)]
        yield
        for copy in sent:
            copy.wait_recv()
        scb[c] = slb[0] + slb[1] + slb[2] + slb[3]
        other = net.send(scb.at[c], scb.at[c], to_c)
        yield
        other.wait_recv()
        sfin[y, x] = scb[0] + scb[1]
        sent = [net.send(sfin.at[y, x], sfin.at[y, x], net.go(x=d)) for d in (1, 2, 3)]
        yield
        for copy in sent:
            copy.wait_recv()
        sent = [net.send(sfin.at[y], sfin.at[y], net.go(y=d)) for d in (1, 2, 3)]
        yield
        for copy in sent:
            copy.wait_recv()
        for k in range(8):
            cols = slice(k * HD, (k + 1) * HD)
            j, i = k // 2, 2 * (k % 2)
            gs_ref[0:16, cols] = sfin[j, i]
            gs_ref[16:17, cols] = sfin[j, i + 1, 0:1]
            gg_ref[0:1, cols] = sfin[j, i + 1, 1:2]

    def weight_sums():
        grads = tn(hid[...], gpn[...]).astype(BF16)
        for k in range(8):
            cols = slice(k * HD, (k + 1) * HD)
            wst[2 * k] = grads[:64, cols]
            wst[2 * k + 1] = grads[64:, cols]
        sent = []
        for d in (1, 2, 3):
            rows = pl.ds(4 * ((x + d) % 4), 4)
            sent.append(net.send(wst.at[rows], wxb.at[d - 1], net.go(x=d)))
        yield
        total = wst[pl.ds(4 * x, 4)].astype(F32)
        for d in range(3):
            sent[d].wait_recv()
            total += wxb[d].astype(F32)
        wsm[...] = total.astype(BF16)
        sent = [net.send(wsm.at[(zl + d) % 4], wzb.at[d - 1], net.go(zl=d)) for d in (1, 2, 3)]
        yield
        total = wsm[zl].astype(F32)
        for d in range(3):
            sent[d].wait_recv()
            total += wzb[d].astype(F32)
        spot = 4 * x + zl
        wfin[spot] = total.astype(BF16)
        sent = [net.send(wfin.at[spot], wfin.at[spot], net.go(zl=d)) for d in (1, 2, 3)]
        yield
        for copy in sent:
            copy.wait_recv()
        rows = pl.ds(4 * x, 4)
        sent = [net.send(wfin.at[rows], wfin.at[rows], net.go(x=d)) for d in (1, 2, 3)]
        yield
        for copy in sent:
            copy.wait_recv()
        for k in range(8):
            cols = slice(k * HD, (k + 1) * HD)
            gw_ref[0:64, cols] = wfin[2 * k]
            gw_ref[64:128, cols] = wfin[2 * k + 1]

    for copy in sent:
        copy.wait_recv()
    sent = [net.send(gpg.at[every, y, c], gpg.at[every, y, c], net.go(y=d)) for d in (1, 2, 3)]
    next(outward)
    for copy in sent:
        copy.wait_recv()
    other = net.send(gpg.at[every, every, c], gpg.at[every, every, c], to_c)
    swap_qkv(2)
    small = small_sums()
    next(small)
    next(outward)
    other.wait_recv()
    gpr[...] = gpg[...].reshape(32 * ROWS, HD).astype(F32)
    for k in range(8):
        gpn[:, k * HD : (k + 1) * HD] = gpr[pl.ds(k, L, stride=8), :].astype(BF16)
    back = nn(gpn[...], jnp.concatenate([mt[...].reshape(DD, HD), wit[...]], axis=1))
    ghs[...] = back[:, HD:].astype(BF16)
    next(outward)

    grad_heads = back[:, :HD].astype(BF16)
    probs = probs_s[...]
    grad_probs = nt(grad_heads, vs[...])
    inside = jnp.sum(probs * grad_probs, axis=-1, keepdims=True)
    grad_scores = (probs * (grad_probs - inside) * scale).astype(BF16)
    gr[0, 0] = nn(grad_scores, ks[...]).astype(BF16)
    gr[0, 1] = tn(grad_scores, qs[...]).astype(BF16)
    gr[0, 2] = tn(probs.astype(BF16), grad_heads).astype(BF16)
    grads_copy = net.send(gr.at[0], gr.at[1], to_c)
    next(outward)
    next(small)
    sums = weight_sums()
    for copy in partner_qkv:
        copy.wait_recv()
    grads_copy.wait_recv()

    def fill_in(yy, pair):
        left = jnp.concatenate([gr[i, j] for i in range(2) for j in range(3)], axis=1)
        right = []
        for zz in pair:
            right.append(
                jnp.concatenate(
                    [wq[j, zz, yy, c] for j in range(3)] + [wqp[j, zz, yy] for j in range(3)],
                    axis=1,
                )
            )
        term = nt(left, jnp.concatenate(right, axis=0)).astype(BF16)
        p3[pair[0], yy] = term[:, :HD]
        p3[pair[1], yy] = term[:, HD:]

    def keep_grad(summed):
        gx_ref[...] = (ghs[...].astype(F32) + summed).astype(BF16)

    for i, _ in enumerate(scatter_ring(net, p3, fill_in, bufs2, keep_grad)):
        if i == 0:
            next(outward, None)
        if i < 4:
            next(sums)
        next(small, None)
    for _ in small:
        pass
    for _ in sums:
        pass
    net.drain()


def hand_out(*refs):
    sems = refs[8]
    copies = [pltpu.make_async_copy(refs[i], refs[4 + i], sems.at[i]) for i in range(4)]
    for copy in copies:
        copy.start()
    for copy in copies:
        copy.wait()


def ring_buffers():
    return [
        pltpu.VMEM((4, HALF, HD), BF16),
        pltpu.VMEM((4, HALF, HD), BF16),
        pltpu.VMEM((4, L, HD), BF16),
        pltpu.VMEM((4, L, HD), BF16),
        pltpu.VMEM((3, L, HD), BF16),
        pltpu.VMEM((HALF, HD), BF16),
        pltpu.VMEM((HALF, HD), BF16),
        pltpu.VMEM((L, HD), BF16),
        pltpu.VMEM((L, HD), BF16),
    ]


def shards(layer_input, frame_mask, w_qkv, w_out, w_in, step_embed, depth_gain, cotangent):
    def v(*shape, kind=BF16):
        return pltpu.VMEM(shape, kind)

    vmem = pl.BlockSpec(memory_space=pltpu.VMEM)
    hbm = pl.BlockSpec(memory_space=pltpu.HBM)
    scratch = [
        v(4, 4, 2, L, HD),
        v(1, L, kind=jnp.int32),
        v(STEPS, DD),
        v(DD),
        v(3, 4, 4, 2, HD, HD),
        v(3, 4, 4, HD, HD),
        v(HD, 32 * HD),
        v(16, HD, HD),
        v(HD, DD),
        v(DD, HD),
        v(DD, HD),
        v(STEPS, FR, DD),
        v(4, 4, 2, PIECE, HD),
        v(4, 4, PIECE, HD),
        v(4, 4, PIECE, HD),
        v(L, 3 * HD, kind=F32),
        v(L, HD),
        v(L, HD),
        v(L, HD),
        v(L, L, kind=F32),
        v(2, L, HD),
        v(4, 4, L, HD),
        v(L, HD),
        v(32 * ROWS, HD, kind=F32),
        v(4, 4, ROWS, HD),
        v(3, 4, ROWS, HD),
        v(4, ROWS, HD),
        v(3, ROWS, HD),
        v(ROWS, HD, kind=F32),
        v(ROWS, HD, kind=F32),
        v(4, 4, 2, ROWS, HD),
        v(32 * ROWS, HD, kind=F32),
        v(L, DD),
        v(L, HD),
        v(4, 4, L, HD),
        v(2, 3, L, HD),
        v(24, DD, kind=F32),
        v(16, 64, HD),
        v(3, 4, 64, HD),
        v(4, 64, HD),
        v(3, 64, HD),
        v(16, 64, HD),
        v(4, 4, 16, HD, kind=F32),
        v(3, 4, 16, HD, kind=F32),
        v(4, 16, HD, kind=F32),
        v(3, 16, HD, kind=F32),
        v(4, 16, HD, kind=F32),
        v(4, 16, HD, kind=F32),
        v(2, 16, HD, kind=F32),
        v(4, 4, 16, HD, kind=F32),
        *ring_buffers(),
        *ring_buffers(),
        pltpu.SemaphoreType.DMA((N_SEM,)),
        pltpu.SemaphoreType.DMA((N_SEM,)),
        pltpu.SemaphoreType.DMA((8,)),
    ]
    grad_x, grad_in, grad_step, grad_gain = pl.pallas_call(
        kernel,
        out_shape=(
            pltpu.VMEM((L, HD), BF16),
            pltpu.VMEM((HD, DD), BF16),
            pltpu.VMEM((STEPS, DD), F32),
            pltpu.VMEM((1, DD), F32),
        ),
        in_specs=[hbm] * 8,
        out_specs=(vmem,) * 4,
        scratch_shapes=scratch,
        compiler_params=pltpu.CompilerParams(
            collective_id=0, has_side_effects=True, vmem_limit_bytes=60 * 1024 * 1024
        ),
    )(
        layer_input[0],
        frame_mask,
        step_embed,
        depth_gain,
        w_qkv.reshape(3, 4, 4, 2, HD, HD),
        w_out,
        w_in,
        jnp.transpose(cotangent[0], (1, 0, 2)),
    )
    grad_x, grad_in, grad_step, grad_gain = pl.pallas_call(
        hand_out,
        out_shape=(
            jax.ShapeDtypeStruct((L, HD), BF16),
            jax.ShapeDtypeStruct((HD, DD), BF16),
            jax.ShapeDtypeStruct((STEPS, DD), F32),
            jax.ShapeDtypeStruct((1, DD), F32),
        ),
        in_specs=[vmem] * 4,
        out_specs=(hbm,) * 4,
        scratch_shapes=[pltpu.SemaphoreType.DMA((4,))],
        compiler_params=pltpu.CompilerParams(vmem_limit_bytes=2 * 1024 * 1024),
    )(grad_x, grad_in, grad_step, grad_gain)
    return (grad_x[None], grad_in, grad_step, grad_gain[0])


def solution(mesh):
    return jax.shard_map(
        shards,
        mesh=mesh,
        in_specs=(
            P("dp", None, "tensor"),
            P("dp", None),
            P(None, None, "tensor"),
            P("tensor", None),
            P("tensor", None),
            P(),
            P(),
            P("dp", "tensor", None, None),
        ),
        out_specs=(P("dp", None, "tensor"), P("tensor", None), P(), P()),
        check_vma=False,
    )
```

```python
import functools

import jax
import jax.numpy as jnp
from jax import lax
from jax.experimental import pallas as pl
from jax.experimental.pallas import tpu as pltpu
from jax.sharding import PartitionSpec as P

MESH = pl.DeviceIdType.MESH
F32 = jnp.float32
BF16 = jnp.bfloat16
L, HD, DD, STEPS, FR = 192, 128, 1024, 17, 6
HALF = L // 2
LO, HI = pl.ds(0, HALF), pl.ds(HALF, HALF)
ROWS = FR * (DD // HD)
PIECE = 64
N_SEM = 200


def nt(a, b):
    return lax.dot_general(a, b, (((1,), (1,)), ((), ())), preferred_element_type=F32)


def nn(a, b):
    return lax.dot_general(a, b, (((1,), (0,)), ((), ())), preferred_element_type=F32)


def tn(a, b):
    return lax.dot_general(a, b, (((0,), (0,)), ((), ())), preferred_element_type=F32)


def around(v):
    return (v + 1) % 4, (v + 3) % 4, (v + 2) % 4


class Net:
    def __init__(self, send_sems, recv_sems):
        self.send_sems, self.recv_sems = send_sems, recv_sems
        self.count = 0
        self.open = []
        dp, t = lax.axis_index("dp"), lax.axis_index("tensor")
        self.dp, self.t = dp, t
        self.x, self.zl = dp // 4, dp % 4
        self.z, self.y, self.c = t // 8, (t // 2) % 4, t % 2

    def go(self, z=0, y=0, c=0, x=0, zl=0):
        dp, t = self.dp, self.t
        if x or zl:
            dp = ((self.x + x) % 4) * 4 + (self.zl + zl) % 4
        if z or y or c:
            cc = (self.c + c) % 2
            t = ((self.z + z) % 4) * 8 + ((self.y + y) % 4) * 2 + cc
        return (dp, t)

    def peers(self):
        found = [self.go(c=1)]
        for d in (1, 2, 3):
            found += [self.go(y=d), self.go(z=d), self.go(x=d), self.go(zl=d)]
        return found

    def make(self, src, dst, peer):
        i = self.count
        self.count += 1
        return pltpu.make_async_remote_copy(
            src_ref=src,
            dst_ref=dst,
            send_sem=self.send_sems.at[i],
            recv_sem=self.recv_sems.at[i],
            device_id=peer,
            device_id_type=MESH,
        )

    def send(self, src, dst, peer):
        copy = self.make(src, dst, peer)
        copy.start()
        self.open.append(copy)
        return copy

    def drain(self):
        for copy in self.open:
            copy.wait_send()
        self.open = []


class Gather:
    def __init__(self, net, g):
        self.net, self.g = net, g
        self.planes = (net.z, around(net.z)[1], around(net.z)[0], around(net.z)[2])
        self.along, self.forward, self.across = {}, {}, {}
        self.to_yp, self.to_ym, self.to_c = net.go(y=1), net.go(y=3), net.go(c=1)

    def whole(self, zz, yy, peer):
        at = self.g.at[zz, yy, self.net.c]
        return self.net.send(at, at, peer)

    def part(self, zz, yy, rows, peer):
        at = self.g.at[zz, yy, self.net.c, rows]
        return self.net.send(at, at, peer)

    def begin(self):
        z, y = self.net.z, self.net.y
        to_zp, to_zm = self.net.go(z=1), self.net.go(z=3)
        self.up_lo = self.part(z, y, LO, to_zp)
        self.dn_hi = self.part(z, y, HI, to_zm)
        self.up_hi = self.part(z, y, HI, to_zp)
        self.dn_lo = self.part(z, y, LO, to_zm)
        self.spread(0)

    def along_z(self):
        y = self.net.y
        to_zp, to_zm = self.net.go(z=1), self.net.go(z=3)
        self.up_lo.wait_recv()
        self.on = self.part(self.planes[1], y, LO, to_zp)
        self.dn_hi.wait_recv()
        self.back = self.part(self.planes[2], y, HI, to_zm)
        self.up_hi.wait_recv()
        self.spread(1)
        self.dn_lo.wait_recv()
        self.spread(2)

    def far_z(self):
        self.on.wait_recv()
        self.back.wait_recv()
        self.spread(3)

    def spread(self, i):
        zz, y = self.planes[i], self.net.y
        if i == 3:
            self.along[i] = (
                self.part(zz, y, LO, self.to_yp),
                self.part(zz, y, HI, self.to_ym),
                self.part(zz, y, HI, self.to_yp),
                self.part(zz, y, LO, self.to_ym),
            )
        else:
            self.along[i] = (self.whole(zz, y, self.to_yp), self.whole(zz, y, self.to_ym))
        self.across[i] = []
        self.over(i, zz, y)

    def over(self, i, zz, yy):
        if i == 3:
            self.across[i].append(self.whole(zz, yy, self.to_c))

    def turn(self, i):
        zz = self.planes[i]
        yp, ym, _ = around(self.net.y)
        self.along[i][0].wait_recv()
        first = self.part(zz, ym, LO, self.to_yp)
        self.along[i][1].wait_recv()
        second = self.part(zz, yp, HI, self.to_ym)
        self.forward[i] = (first, second)
        for copy in self.along[i][2:]:
            copy.wait_recv()
        self.over(i, zz, ym)
        self.over(i, zz, yp)

    def land(self, i):
        for copy in self.forward[i]:
            copy.wait_recv()
        self.over(i, self.planes[i], around(self.net.y)[2])
        if i < 3:
            at = self.g.at[self.planes[i], pl.ds(0, 4), self.net.c]
            self.across[i].append(self.net.send(at, at, self.to_c))

    def here(self, i):
        for copy in self.across[i]:
            copy.wait_recv()


def scatter_ring(net, p, fill, bufs, done, ahead=False):
    ya, yb, yup, ydn, q, za, zb, zup, zdn = bufs
    z, y = net.z, net.y
    zp, zm, z2 = around(z)
    yp, ym, y2 = around(y)
    to_zp, to_zm, to_yp, to_ym = net.go(z=1), net.go(z=3), net.go(y=1), net.go(y=3)
    order = (z2, zp, zm, z)
    pairs = (order[:2], order[2:])

    far, near = [], [[], [], [], []]
    if ahead:
        for yy in (y2, yp, ym, y):
            for pair in pairs:
                fill(yy, pair)
        yield
    for pair in pairs:
        if not ahead:
            fill(y2, pair)
        for zz in pair:
            a = net.send(p.at[zz, y2, LO], ya.at[zz], to_yp)
            far.append((a, net.send(p.at[zz, y2, HI], yb.at[zz], to_ym)))

    def at_once(i):
        zz = order[i]
        near[i].append(net.send(p.at[zz, yp, HI], yup.at[zz, HI], to_yp))
        near[i].append(net.send(p.at[zz, ym, LO], ydn.at[zz, LO], to_ym))

    for j, pair in enumerate(pairs):
        if not ahead:
            fill(yp, pair)
            fill(ym, pair)
        at_once(2 * j)
        at_once(2 * j + 1)
    yield
    for i, zz in enumerate(order):
        far[i][0].wait_recv()
        p[zz, yp, LO] = (p[zz, yp, LO].astype(F32) + ya[zz].astype(F32)).astype(BF16)
        near[i].append(net.send(p.at[zz, yp, LO], yup.at[zz, LO], to_yp))
        far[i][1].wait_recv()
        p[zz, ym, HI] = (p[zz, ym, HI].astype(F32) + yb[zz].astype(F32)).astype(BF16)
        near[i].append(net.send(p.at[zz, ym, HI], ydn.at[zz, HI], to_ym))
    if not ahead:
        for pair in pairs:
            fill(y, pair)
    yield

    def mine(i):
        for copy in near[i]:
            copy.wait_recv()
        zz = order[i]
        return p[zz, y].astype(F32) + yup[zz].astype(F32) + ydn[zz].astype(F32)

    q[0] = mine(0).astype(BF16)
    a = net.send(q.at[0, LO], za, to_zp)
    b = net.send(q.at[0, HI], zb, to_zm)
    yield
    q[1] = mine(1).astype(BF16)
    last = [net.send(q.at[1, HI], zup.at[HI], to_zp)]
    q[2] = mine(2).astype(BF16)
    last.append(net.send(q.at[2, LO], zdn.at[LO], to_zm))
    yield
    a.wait_recv()
    q[1, LO] = (q[1, LO].astype(F32) + za[...].astype(F32)).astype(BF16)
    last.append(net.send(q.at[1, LO], zup.at[LO], to_zp))
    b.wait_recv()
    q[2, HI] = (q[2, HI].astype(F32) + zb[...].astype(F32)).astype(BF16)
    last.append(net.send(q.at[2, HI], zdn.at[HI], to_zm))
    yield
    total = mine(3)
    yield
    for copy in last:
        copy.wait_recv()
    done(total + zup[...].astype(F32) + zdn[...].astype(F32))


def kernel(
    x_hbm, mask_hbm, step_hbm, gain_hbm, wqkv_hbm, wout_hbm, win_hbm, cot_hbm,
    gx_ref, gw_ref, gs_ref, gg_ref,
    xg, maskv, stepv, gainv, wq, wqp, wo, wop, wi, wit, witp, cot,
    gm, mt, mtp,
    acc, qs, ks, vs, probs_s, hp, p1, hid, pf, p2, pyb, pq, pzb, pr, gpf,
    gpg, gpr, gpn, ghs, p3, gr, rows_s,
    wst, wxb, wsm, wzb, wfin,
    sst, syb, sm1, sxb, szb, slb, scb, sfin,
    *rest,
):
    bufs1, bufs2 = rest[:9], rest[9:18]
    send_sems, recv_sems, local_sems = rest[18:]
    net = Net(send_sems, recv_sems)
    x, zl, z, y, c = net.x, net.zl, net.z, net.y, net.c
    to_c = net.go(c=1)
    scale = HD ** (-0.5)

    barrier = pltpu.get_barrier_semaphore()
    peers = net.peers()
    for peer in peers:
        pl.semaphore_signal(barrier, inc=1, device_id=peer, device_id_type=MESH)
    loads = {}
    for i, (name, src, dst) in enumerate(
        (
            ("w_in", win_hbm, wi),
            ("x", x_hbm, xg.at[z, y, c]),
            ("w_out", wout_hbm, wo),
            ("w_qkv", wqkv_hbm, wq),
            ("mask", mask_hbm, maskv),
            ("step", step_hbm, stepv),
            ("gain", gain_hbm, gainv),
            ("cot", cot_hbm, cot),
        )
    ):
        loads[name] = pltpu.make_async_copy(src, dst, local_sems.at[i])
        loads[name].start()
    loads["w_in"].wait()
    for k in range(8):
        wit[k * HD : (k + 1) * HD, :] = wi[:, k * HD : (k + 1) * HD].T
    gm[z, y, c] = wit[pl.ds(pl.multiple_of(PIECE * net.dp, PIECE), PIECE), :]
    loads["x"].wait()
    pl.semaphore_wait(barrier, len(peers))

    every = pl.ds(0, 4)

    def weight_product():
        sent = [net.send(gm.at[z, y, c], gm.at[z, y, c], net.go(z=d)) for d in (1, 2, 3)]
        yield
        for copy in sent:
            copy.wait_recv()
        sent = [net.send(gm.at[every, y, c], gm.at[every, y, c], net.go(y=d)) for d in (1, 2, 3)]
        yield
        for copy in sent:
            copy.wait_recv()
        other = net.send(gm.at[every, every, c], gm.at[every, every, c], to_c)
        yield
        other.wait_recv()
        loads["w_out"].wait()
        left = jnp.concatenate(
            [gm[i, j, k] for i in range(4) for j in range(4) for k in range(2)], axis=1
        )
        mt[x, zl] = nt(left, wo[...]).astype(BF16)
        sent = [net.send(mt.at[x, zl], mt.at[x, zl], net.go(zl=d)) for d in (1, 2, 3)]
        yield
        for copy in sent:
            copy.wait_recv()
        sent = [net.send(mt.at[x], mt.at[x], net.go(x=d)) for d in (1, 2, 3)]
        last = [net.send(mt.at[x], mtp.at[x], to_c)]
        yield
        for d in (1, 2, 3):
            sent[d - 1].wait_recv()
            spot = (x + 4 - d) % 4
            last.append(net.send(mt.at[spot], mtp.at[spot], to_c))
        yield
        for copy in last:
            copy.wait_recv()

    def plane(i):
        zz = gather.planes[i]
        gather.here(i)
        left = jnp.concatenate([xg[zz, j, k] for j in range(4) for k in range(2)], axis=1)
        right = jnp.concatenate([wq[j, zz].reshape(DD, HD) for j in range(3)], axis=1)
        term = nn(left, right)
        acc[...] = term if i == 0 else acc[...] + term

    product = weight_product()
    gather = Gather(net, xg)
    next(product)
    gather.begin()
    partner_in = net.send(wit, witp, to_c)
    spot = net.count
    partner_out = net.make(wop, wop, to_c)
    for i in range(16):
        cols = pl.ds(pl.multiple_of((2 * i + 1 - c) * HD, HD), HD)
        pltpu.make_async_remote_copy(
            src_ref=wout_hbm.at[:, cols],
            dst_ref=wop.at[i],
            send_sem=send_sems.at[spot],
            recv_sem=recv_sems.at[spot],
            device_id=to_c,
            device_id_type=MESH,
        ).start()
    net.open.append(partner_out)

    next(product)
    gather.along_z()
    next(product)
    gather.turn(0)
    gather.far_z()
    gather.turn(1)
    gather.turn(2)
    gather.land(0)
    next(product)
    gather.turn(3)
    gather.land(1)
    gather.land(2)
    loads["w_qkv"].wait()
    plane(0)
    next(product)
    plane(1)
    gather.land(3)
    plane(2)
    plane(3)

    partner_qkv = []

    def swap_qkv(j):
        partner_qkv.append(net.send(wqkv_hbm.at[j, every, every, 1 - c], wqp.at[j], to_c))

    query = acc[:, :HD].astype(BF16)
    key_rows = acc[:, HD : 2 * HD].astype(BF16)
    value = acc[:, 2 * HD :].astype(BF16)
    qs[...] = query
    ks[...] = key_rows
    vs[...] = value
    loads["mask"].wait()
    row = lax.broadcasted_iota(jnp.int32, (L, L), 0)
    col = lax.broadcasted_iota(jnp.int32, (L, L), 1)
    allowed = (col <= row) & ((maskv[...] == 1) | (col == row))
    scores = jnp.where(allowed, nt(query, key_rows) * scale, -1e30)
    next(product)
    raised = jnp.exp(scores - jnp.max(scores, axis=-1, keepdims=True))
    probs = raised / jnp.sum(raised, axis=-1, keepdims=True)
    probs_s[...] = probs
    hp[0] = nn(probs.astype(BF16), value).astype(BF16)
    heads_copy = net.send(hp.at[0], hp.at[1], to_c)
    partner_in.wait_recv()
    heads_copy.wait_recv()

    next(product, None)

    left = jnp.concatenate([hp[0], hp[1], xg[z, y, c], xg[z, y, 1 - c]], axis=1)
    right = jnp.concatenate(
        [mt[...].reshape(DD, HD), mtp[...].reshape(DD, HD), wit[...], witp[...]], axis=1
    )
    term = nt(left, right)
    for k in range(8):
        pf[pl.ds(k, L, stride=8), :] = term[:, k * HD : (k + 1) * HD]
    for i in range(4):
        for j in range(4):
            rows = pl.ds(pl.multiple_of((8 * i + 2 * j + c) * ROWS, 8), ROWS)
            p2[j, i] = pf[rows, :].astype(BF16)
    sent = [net.send(p2.at[(y + d) % 4], pyb.at[d - 1], net.go(y=d)) for d in (1, 2, 3)]
    swap_qkv(0)

    def fill_out(yy, pair):
        left = jnp.concatenate([hp[0], hp[1]], axis=1)
        right = []
        for zz in pair:
            col0 = pl.multiple_of((zz * 8 + yy * 2 + c) * HD, HD)
            right.append(jnp.concatenate([wo[:, pl.ds(col0, HD)], wop[zz * 4 + yy]], axis=0))
        term = nn(left, jnp.concatenate(right, axis=1)).astype(BF16)
        p1[pair[0], yy] = term[:, :HD]
        p1[pair[1], yy] = term[:, HD:]

    def keep_hidden(summed):
        hid[...] = (xg[z, y, c].astype(F32) + summed).astype(BF16)

    outward = scatter_ring(net, p1, fill_out, bufs1, keep_hidden, ahead=True)
    partner_out.wait_recv()
    next(outward)
    total = p2[y].astype(F32)
    for d in range(3):
        sent[d].wait_recv()
        total += pyb[d].astype(F32)
    pq[...] = total.astype(BF16)
    sent = [net.send(pq.at[(z + d) % 4], pzb.at[d - 1], net.go(z=d)) for d in (1, 2, 3)]
    swap_qkv(1)

    next(outward)
    total = pq[z].astype(F32)
    for d in range(3):
        sent[d].wait_recv()
        total += pzb[d].astype(F32)
    pr[...] = total
    swap_qkv(2)

    for name in ("step", "gain", "cot"):
        loads[name].wait()
    gains = gainv[...].astype(F32)[None]
    proj = jnp.concatenate([pr[pl.ds(k, FR, stride=8), :] for k in range(8)], axis=1)
    grad_rows = jnp.zeros((FR, DD), F32)
    gain_rows = jnp.zeros((FR, DD), F32)
    for s in range(STEPS):
        inner = proj + stepv[s : s + 1, :].astype(F32)
        inverse = lax.rsqrt(jnp.mean(inner * inner, axis=-1, keepdims=True) + 1e-06)
        arriving = cot[s].astype(F32)
        gain_rows += arriving * inner * inverse
        scaled = arriving * gains
        mixed = jnp.mean(inner * scaled, axis=-1, keepdims=True)
        grad_inner = inverse * scaled - inverse * inverse * inverse * inner * mixed
        grad_rows += grad_inner
        rows_s[s : s + 1, :] = jnp.sum(grad_inner, axis=0, keepdims=True)
    for k in range(8):
        gpf[pl.ds(k, FR, stride=8), :] = grad_rows[:, k * HD : (k + 1) * HD]
    gpg[z, y, c] = gpf[...].astype(BF16)

    sent = [net.send(gpg.at[z, y, c], gpg.at[z, y, c], net.go(z=d)) for d in (1, 2, 3)]
    next(outward)
    rows_s[STEPS : STEPS + 1, :] = jnp.sum(gain_rows, axis=0, keepdims=True)
    for k in range(8):
        cols = slice(k * HD, (k + 1) * HD)
        j, i = k // 2, 2 * (k % 2)
        sst[j, i] = rows_s[:16, cols]
        sst[j, i + 1] = jnp.zeros((16, HD), F32)
        sst[j, i + 1, 0:2] = rows_s[16:18, cols]

    def small_sums():
        sent = [net.send(sst.at[(y + d) % 4], syb.at[d - 1], net.go(y=d)) for d in (1, 2, 3)]
        yield
        total = sst[y]
        for d in range(3):
            sent[d].wait_recv()
            total += syb[d]
        sm1[...] = total
        sent = [net.send(sm1.at[(x + d) % 4], sxb.at[d - 1], net.go(x=d)) for d in (1, 2, 3)]
        yield
        total = sm1[x]
        for d in range(3):
            sent[d].wait_recv()
            total += sxb[d]
        szb[z] = total
        sent = [net.send(szb.at[z], szb.at[z], net.go(z=d)) for d in (1, 2, 3)]
        yield
        for copy in sent:
            copy.wait_recv()
        slb[zl] = szb[0] + szb[1] + szb[2] + szb[3]
        sent = [net.send(slb.at[zl], slb.at[zl], net.go(zl=d)) for d in (1, 2, 3)]
        yield
        for copy in sent:
            copy.wait_recv()
        scb[c] = slb[0] + slb[1] + slb[2] + slb[3]
        other = net.send(scb.at[c], scb.at[c], to_c)
        yield
        other.wait_recv()
        sfin[y, x] = scb[0] + scb[1]
        sent = [net.send(sfin.at[y, x], sfin.at[y, x], net.go(x=d)) for d in (1, 2, 3)]
        yield
        for copy in sent:
            copy.wait_recv()
        sent = [net.send(sfin.at[y], sfin.at[y], net.go(y=d)) for d in (1, 2, 3)]
        yield
        for copy in sent:
            copy.wait_recv()
        for k in range(8):
            cols = slice(k * HD, (k + 1) * HD)
            j, i = k // 2, 2 * (k % 2)
            gs_ref[0:16, cols] = sfin[j, i]
            gs_ref[16:17, cols] = sfin[j, i + 1, 0:1]
            gg_ref[0:1, cols] = sfin[j, i + 1, 1:2]

    def weight_sums():
        grads = tn(hid[...], gpn[...]).astype(BF16)
        for k in range(8):
            cols = slice(k * HD, (k + 1) * HD)
            wst[2 * k] = grads[:64, cols]
            wst[2 * k + 1] = grads[64:, cols]
        sent = []
        for d in (1, 2, 3):
            rows = pl.ds(4 * ((x + d) % 4), 4)
            sent.append(net.send(wst.at[rows], wxb.at[d - 1], net.go(x=d)))
        yield
        total = wst[pl.ds(4 * x, 4)].astype(F32)
        for d in range(3):
            sent[d].wait_recv()
            total += wxb[d].astype(F32)
        wsm[...] = total.astype(BF16)
        sent = [net.send(wsm.at[(zl + d) % 4], wzb.at[d - 1], net.go(zl=d)) for d in (1, 2, 3)]
        yield
        total = wsm[zl].astype(F32)
        for d in range(3):
            sent[d].wait_recv()
            total += wzb[d].astype(F32)
        spot = 4 * x + zl
        wfin[spot] = total.astype(BF16)
        sent = [net.send(wfin.at[spot], wfin.at[spot], net.go(zl=d)) for d in (1, 2, 3)]
        yield
        for copy in sent:
            copy.wait_recv()
        rows = pl.ds(4 * x, 4)
        sent = [net.send(wfin.at[rows], wfin.at[rows], net.go(x=d)) for d in (1, 2, 3)]
        yield
        for copy in sent:
            copy.wait_recv()
        for k in range(8):
            cols = slice(k * HD, (k + 1) * HD)
            gw_ref[0:64, cols] = wfin[2 * k]
            gw_ref[64:128, cols] = wfin[2 * k + 1]

    for copy in sent:
        copy.wait_recv()
    sent = [net.send(gpg.at[every, y, c], gpg.at[every, y, c], net.go(y=d)) for d in (1, 2, 3)]
    next(outward)
    for copy in sent:
        copy.wait_recv()
    other = net.send(gpg.at[every, every, c], gpg.at[every, every, c], to_c)
    small = small_sums()
    next(small)
    next(outward)
    other.wait_recv()
    gpr[...] = gpg[...].reshape(32 * ROWS, HD).astype(F32)
    for k in range(8):
        gpn[:, k * HD : (k + 1) * HD] = gpr[pl.ds(k, L, stride=8), :].astype(BF16)
    back = nn(gpn[...], jnp.concatenate([mt[...].reshape(DD, HD), wit[...]], axis=1))
    ghs[...] = back[:, HD:].astype(BF16)
    next(outward)

    grad_heads = back[:, :HD].astype(BF16)
    probs = probs_s[...]
    grad_probs = nt(grad_heads, vs[...])
    inside = jnp.sum(probs * grad_probs, axis=-1, keepdims=True)
    grad_scores = (probs * (grad_probs - inside) * scale).astype(BF16)
    gr[0, 0] = nn(grad_scores, ks[...]).astype(BF16)
    gr[0, 1] = tn(grad_scores, qs[...]).astype(BF16)
    gr[0, 2] = tn(probs.astype(BF16), grad_heads).astype(BF16)
    grads_copy = net.send(gr.at[0], gr.at[1], to_c)
    next(outward)
    next(small)
    sums = weight_sums()
    for copy in partner_qkv:
        copy.wait_recv()
    grads_copy.wait_recv()

    def fill_in(yy, pair):
        left = jnp.concatenate([gr[i, j] for i in range(2) for j in range(3)], axis=1)
        right = []
        for zz in pair:
            right.append(
                jnp.concatenate(
                    [wq[j, zz, yy, c] for j in range(3)] + [wqp[j, zz, yy] for j in range(3)],
                    axis=1,
                )
            )
        term = nt(left, jnp.concatenate(right, axis=0)).astype(BF16)
        p3[pair[0], yy] = term[:, :HD]
        p3[pair[1], yy] = term[:, HD:]

    def keep_grad(summed):
        gx_ref[...] = (ghs[...].astype(F32) + summed).astype(BF16)

    for i, _ in enumerate(scatter_ring(net, p3, fill_in, bufs2, keep_grad)):
        if i == 0:
            next(outward, None)
        if i < 4:
            next(sums)
        next(small, None)
    for _ in small:
        pass
    for _ in sums:
        pass
    net.drain()


def hand_out(*refs):
    sems = refs[8]
    copies = [pltpu.make_async_copy(refs[i], refs[4 + i], sems.at[i]) for i in range(4)]
    for copy in copies:
        copy.start()
    for copy in copies:
        copy.wait()


def ring_buffers():
    return [
        pltpu.VMEM((4, HALF, HD), BF16),
        pltpu.VMEM((4, HALF, HD), BF16),
        pltpu.VMEM((4, L, HD), BF16),
        pltpu.VMEM((4, L, HD), BF16),
        pltpu.VMEM((3, L, HD), BF16),
        pltpu.VMEM((HALF, HD), BF16),
        pltpu.VMEM((HALF, HD), BF16),
        pltpu.VMEM((L, HD), BF16),
        pltpu.VMEM((L, HD), BF16),
    ]


def shards(layer_input, frame_mask, w_qkv, w_out, w_in, step_embed, depth_gain, cotangent):
    def v(*shape, kind=BF16):
        return pltpu.VMEM(shape, kind)

    vmem = pl.BlockSpec(memory_space=pltpu.VMEM)
    hbm = pl.BlockSpec(memory_space=pltpu.HBM)
    scratch = [
        v(4, 4, 2, L, HD),
        v(1, L, kind=jnp.int32),
        v(STEPS, DD),
        v(DD),
        v(3, 4, 4, 2, HD, HD),
        v(3, 4, 4, HD, HD),
        v(HD, 32 * HD),
        v(16, HD, HD),
        v(HD, DD),
        v(DD, HD),
        v(DD, HD),
        v(STEPS, FR, DD),
        v(4, 4, 2, PIECE, HD),
        v(4, 4, PIECE, HD),
        v(4, 4, PIECE, HD),
        v(L, 3 * HD, kind=F32),
        v(L, HD),
        v(L, HD),
        v(L, HD),
        v(L, L, kind=F32),
        v(2, L, HD),
        v(4, 4, L, HD),
        v(L, HD),
        v(32 * ROWS, HD, kind=F32),
        v(4, 4, ROWS, HD),
        v(3, 4, ROWS, HD),
        v(4, ROWS, HD),
        v(3, ROWS, HD),
        v(ROWS, HD, kind=F32),
        v(ROWS, HD, kind=F32),
        v(4, 4, 2, ROWS, HD),
        v(32 * ROWS, HD, kind=F32),
        v(L, DD),
        v(L, HD),
        v(4, 4, L, HD),
        v(2, 3, L, HD),
        v(24, DD, kind=F32),
        v(16, 64, HD),
        v(3, 4, 64, HD),
        v(4, 64, HD),
        v(3, 64, HD),
        v(16, 64, HD),
        v(4, 4, 16, HD, kind=F32),
        v(3, 4, 16, HD, kind=F32),
        v(4, 16, HD, kind=F32),
        v(3, 16, HD, kind=F32),
        v(4, 16, HD, kind=F32),
        v(4, 16, HD, kind=F32),
        v(2, 16, HD, kind=F32),
        v(4, 4, 16, HD, kind=F32),
        *ring_buffers(),
        *ring_buffers(),
        pltpu.SemaphoreType.DMA((N_SEM,)),
        pltpu.SemaphoreType.DMA((N_SEM,)),
        pltpu.SemaphoreType.DMA((8,)),
    ]
    grad_x, grad_in, grad_step, grad_gain = pl.pallas_call(
        kernel,
        out_shape=(
            pltpu.VMEM((L, HD), BF16),
            pltpu.VMEM((HD, DD), BF16),
            pltpu.VMEM((STEPS, DD), F32),
            pltpu.VMEM((1, DD), F32),
        ),
        in_specs=[hbm] * 8,
        out_specs=(vmem,) * 4,
        scratch_shapes=scratch,
        compiler_params=pltpu.CompilerParams(
            collective_id=0, has_side_effects=True, vmem_limit_bytes=60 * 1024 * 1024
        ),
    )(
        layer_input[0],
        frame_mask,
        step_embed,
        depth_gain,
        w_qkv.reshape(3, 4, 4, 2, HD, HD),
        w_out,
        w_in,
        jnp.transpose(cotangent[0], (1, 0, 2)),
    )
    grad_x, grad_in, grad_step, grad_gain = pl.pallas_call(
        hand_out,
        out_shape=(
            jax.ShapeDtypeStruct((L, HD), BF16),
            jax.ShapeDtypeStruct((HD, DD), BF16),
            jax.ShapeDtypeStruct((STEPS, DD), F32),
            jax.ShapeDtypeStruct((1, DD), F32),
        ),
        in_specs=[vmem] * 4,
        out_specs=(hbm,) * 4,
        scratch_shapes=[pltpu.SemaphoreType.DMA((4,))],
        compiler_params=pltpu.CompilerParams(vmem_limit_bytes=2 * 1024 * 1024),
    )(grad_x, grad_in, grad_step, grad_gain)
    return (grad_x[None], grad_in, grad_step, grad_gain[0])


def solution(mesh):
    return jax.shard_map(
        shards,
        mesh=mesh,
        in_specs=(
            P("dp", None, "tensor"),
            P("dp", None),
            P(None, None, "tensor"),
            P("tensor", None),
            P("tensor", None),
            P(),
            P(),
            P("dp", "tensor", None, None),
        ),
        out_specs=(P("dp", None, "tensor"), P("tensor", None), P(), P()),
        check_vma=False,
    )
```

```python
import functools

import jax
import jax.numpy as jnp
from jax import lax
from jax.experimental import pallas as pl
from jax.experimental.pallas import tpu as pltpu
from jax.sharding import PartitionSpec as P

MESH = pl.DeviceIdType.MESH
F32 = jnp.float32
BF16 = jnp.bfloat16
L, HD, DD, STEPS, FR = 192, 128, 1024, 17, 6
HALF = L // 2
LO, HI = pl.ds(0, HALF), pl.ds(HALF, HALF)
ROWS = FR * (DD // HD)
PIECE = 64
N_SEM = 200


def nt(a, b):
    return lax.dot_general(a, b, (((1,), (1,)), ((), ())), preferred_element_type=F32)


def nn(a, b):
    return lax.dot_general(a, b, (((1,), (0,)), ((), ())), preferred_element_type=F32)


def tn(a, b):
    return lax.dot_general(a, b, (((0,), (0,)), ((), ())), preferred_element_type=F32)


def around(v):
    return (v + 1) % 4, (v + 3) % 4, (v + 2) % 4


class Net:
    def __init__(self, send_sems, recv_sems):
        self.send_sems, self.recv_sems = send_sems, recv_sems
        self.count = 0
        self.open = []
        dp, t = lax.axis_index("dp"), lax.axis_index("tensor")
        self.dp, self.t = dp, t
        self.x, self.zl = dp // 4, dp % 4
        self.z, self.y, self.c = t // 8, (t // 2) % 4, t % 2

    def go(self, z=0, y=0, c=0, x=0, zl=0):
        dp, t = self.dp, self.t
        if x or zl:
            dp = ((self.x + x) % 4) * 4 + (self.zl + zl) % 4
        if z or y or c:
            cc = (self.c + c) % 2
            t = ((self.z + z) % 4) * 8 + ((self.y + y) % 4) * 2 + cc
        return (dp, t)

    def peers(self):
        found = [self.go(c=1)]
        for d in (1, 2, 3):
            found += [self.go(y=d), self.go(z=d), self.go(x=d), self.go(zl=d)]
        return found

    def make(self, src, dst, peer):
        i = self.count
        self.count += 1
        return pltpu.make_async_remote_copy(
            src_ref=src,
            dst_ref=dst,
            send_sem=self.send_sems.at[i],
            recv_sem=self.recv_sems.at[i],
            device_id=peer,
            device_id_type=MESH,
        )

    def send(self, src, dst, peer):
        copy = self.make(src, dst, peer)
        copy.start()
        self.open.append(copy)
        return copy

    def drain(self, keep=0):
        done = self.open[: len(self.open) - keep]
        for copy in done:
            copy.wait_send()
        self.open = self.open[len(done) :]


class Gather:
    def __init__(self, net, g):
        self.net, self.g = net, g
        self.planes = (net.z, around(net.z)[1], around(net.z)[0], around(net.z)[2])
        self.along, self.forward, self.across = {}, {}, {}
        self.to_yp, self.to_ym, self.to_c = net.go(y=1), net.go(y=3), net.go(c=1)

    def whole(self, zz, yy, peer):
        at = self.g.at[zz, yy, self.net.c]
        return self.net.send(at, at, peer)

    def part(self, zz, yy, rows, peer):
        at = self.g.at[zz, yy, self.net.c, rows]
        return self.net.send(at, at, peer)

    def begin(self):
        z, y = self.net.z, self.net.y
        to_zp, to_zm = self.net.go(z=1), self.net.go(z=3)
        self.up_lo = self.part(z, y, LO, to_zp)
        self.dn_hi = self.part(z, y, HI, to_zm)
        self.up_hi = self.part(z, y, HI, to_zp)
        self.dn_lo = self.part(z, y, LO, to_zm)
        self.spread(0)

    def along_z(self):
        y = self.net.y
        to_zp, to_zm = self.net.go(z=1), self.net.go(z=3)
        self.up_lo.wait_recv()
        self.on = self.part(self.planes[1], y, LO, to_zp)
        self.dn_hi.wait_recv()
        self.back = self.part(self.planes[2], y, HI, to_zm)
        self.up_hi.wait_recv()
        self.spread(1)
        self.dn_lo.wait_recv()
        self.spread(2)

    def far_z(self):
        self.on.wait_recv()
        self.back.wait_recv()
        self.spread(3)

    def spread(self, i):
        zz, y = self.planes[i], self.net.y
        if i == 3:
            self.along[i] = (
                self.part(zz, y, LO, self.to_yp),
                self.part(zz, y, HI, self.to_ym),
                self.part(zz, y, HI, self.to_yp),
                self.part(zz, y, LO, self.to_ym),
            )
        else:
            self.along[i] = (self.whole(zz, y, self.to_yp), self.whole(zz, y, self.to_ym))
        self.across[i] = []
        self.over(i, zz, y)

    def over(self, i, zz, yy):
        if i == 3:
            self.across[i].append(self.whole(zz, yy, self.to_c))

    def turn(self, i):
        zz = self.planes[i]
        yp, ym, _ = around(self.net.y)
        self.along[i][0].wait_recv()
        first = self.part(zz, ym, LO, self.to_yp)
        self.along[i][1].wait_recv()
        second = self.part(zz, yp, HI, self.to_ym)
        self.forward[i] = (first, second)
        for copy in self.along[i][2:]:
            copy.wait_recv()
        self.over(i, zz, ym)
        self.over(i, zz, yp)

    def land(self, i):
        for copy in self.forward[i]:
            copy.wait_recv()
        self.over(i, self.planes[i], around(self.net.y)[2])
        if i < 3:
            at = self.g.at[self.planes[i], pl.ds(0, 4), self.net.c]
            self.across[i].append(self.net.send(at, at, self.to_c))

    def here(self, i):
        for copy in self.across[i]:
            copy.wait_recv()


def scatter_ring(net, p, fill, bufs, done, ahead=False):
    ya, yb, yup, ydn, q, za, zb, zup, zdn = bufs
    z, y = net.z, net.y
    zp, zm, z2 = around(z)
    yp, ym, y2 = around(y)
    to_zp, to_zm, to_yp, to_ym = net.go(z=1), net.go(z=3), net.go(y=1), net.go(y=3)
    order = (z2, zp, zm, z)

    def fill_rows(first, step, count):
        @pl.loop(0, 2 * count)
        def _(k):
            j = k % 2
            yy = (y + first + step * (k // 2)) % 4
            fill(yy, ((z + 2 + j) % 4, (z + 5 - j) % 4))

    far, near = [], [[], [], [], []]
    if ahead:
        fill_rows(0, 1, 4)
        yield
    else:
        fill_rows(2, 0, 1)
    for zz in order:
        a = net.send(p.at[zz, y2, LO], ya.at[zz], to_yp)
        far.append((a, net.send(p.at[zz, y2, HI], yb.at[zz], to_ym)))

    def at_once(i):
        zz = order[i]
        near[i].append(net.send(p.at[zz, yp, HI], yup.at[zz, HI], to_yp))
        near[i].append(net.send(p.at[zz, ym, LO], ydn.at[zz, LO], to_ym))

    if not ahead:
        fill_rows(1, 2, 2)
    for i in range(4):
        at_once(i)
    yield
    for i, zz in enumerate(order):
        far[i][0].wait_recv()
        p[zz, yp, LO] = (p[zz, yp, LO].astype(F32) + ya[zz].astype(F32)).astype(BF16)
        near[i].append(net.send(p.at[zz, yp, LO], yup.at[zz, LO], to_yp))
        far[i][1].wait_recv()
        p[zz, ym, HI] = (p[zz, ym, HI].astype(F32) + yb[zz].astype(F32)).astype(BF16)
        near[i].append(net.send(p.at[zz, ym, HI], ydn.at[zz, HI], to_ym))
    if not ahead:
        fill_rows(0, 0, 1)
    yield

    def mine(i):
        for copy in near[i]:
            copy.wait_recv()
        zz = order[i]
        return p[zz, y].astype(F32) + yup[zz].astype(F32) + ydn[zz].astype(F32)

    q[0] = mine(0).astype(BF16)
    a = net.send(q.at[0, LO], za, to_zp)
    b = net.send(q.at[0, HI], zb, to_zm)
    yield
    q[1] = mine(1).astype(BF16)
    last = [net.send(q.at[1, HI], zup.at[HI], to_zp)]
    q[2] = mine(2).astype(BF16)
    last.append(net.send(q.at[2, LO], zdn.at[LO], to_zm))
    yield
    a.wait_recv()
    q[1, LO] = (q[1, LO].astype(F32) + za[...].astype(F32)).astype(BF16)
    last.append(net.send(q.at[1, LO], zup.at[LO], to_zp))
    b.wait_recv()
    q[2, HI] = (q[2, HI].astype(F32) + zb[...].astype(F32)).astype(BF16)
    last.append(net.send(q.at[2, HI], zdn.at[HI], to_zm))
    yield
    total = mine(3)
    yield
    for copy in last:
        copy.wait_recv()
    done(total + zup[...].astype(F32) + zdn[...].astype(F32))


def kernel(
    x_hbm, mask_hbm, step_hbm, gain_hbm, wqkv_hbm, wout_hbm, win_hbm, cot_hbm,
    gx_ref, gw_ref, gs_ref, gg_ref,
    xg, maskv, stepv, gainv, wq, wqp, wo, wop, wi, wit, witp, cot,
    gm, mt, mtp,
    acc, qs, ks, vs, probs_s, hp, p1, hid, pf, p2, pyb, pq, pzb, pr, gpf,
    gpg, gpr, gpn, ghs, p3, gr, rows_s,
    wst, wxb, wsm, wzb, wfin,
    sst, syb, sm1, sxb, szb, slb, scb, sfin,
    *rest,
):
    bufs1, bufs2 = rest[:9], rest[9:18]
    send_sems, recv_sems, local_sems = rest[18:]
    net = Net(send_sems, recv_sems)
    x, zl, z, y, c = net.x, net.zl, net.z, net.y, net.c
    to_c = net.go(c=1)
    scale = HD ** (-0.5)

    barrier = pltpu.get_barrier_semaphore()
    peers = net.peers()
    for peer in peers:
        pl.semaphore_signal(barrier, inc=1, device_id=peer, device_id_type=MESH)
    loads = {}
    for i, (name, src, dst) in enumerate(
        (
            ("w_in", win_hbm, wi),
            ("x", x_hbm, xg.at[z, y, c]),
            ("w_out", wout_hbm, wo),
            ("w_qkv", wqkv_hbm, wq),
            ("mask", mask_hbm, maskv),
            ("step", step_hbm, stepv),
            ("gain", gain_hbm, gainv),
            ("cot", cot_hbm, cot),
        )
    ):
        loads[name] = pltpu.make_async_copy(src, dst, local_sems.at[i])
        loads[name].start()
    loads["w_in"].wait()
    for k in range(8):
        wit[k * HD : (k + 1) * HD, :] = wi[:, k * HD : (k + 1) * HD].T
    gm[z, y, c] = wit[pl.ds(pl.multiple_of(PIECE * net.dp, PIECE), PIECE), :]
    loads["x"].wait()
    pl.semaphore_wait(barrier, len(peers))

    every = pl.ds(0, 4)

    def weight_product():
        sent = [net.send(gm.at[z, y, c], gm.at[z, y, c], net.go(z=d)) for d in (1, 2, 3)]
        yield
        for copy in sent:
            copy.wait_recv()
        sent = [net.send(gm.at[every, y, c], gm.at[every, y, c], net.go(y=d)) for d in (1, 2, 3)]
        yield
        for copy in sent:
            copy.wait_recv()
        other = net.send(gm.at[every, every, c], gm.at[every, every, c], to_c)
        yield
        other.wait_recv()
        loads["w_out"].wait()
        left = jnp.concatenate(
            [gm[i, j, k] for i in range(4) for j in range(4) for k in range(2)], axis=1
        )
        mt[x, zl] = nt(left, wo[...]).astype(BF16)
        sent = [net.send(mt.at[x, zl], mt.at[x, zl], net.go(zl=d)) for d in (1, 2, 3)]
        yield
        for copy in sent:
            copy.wait_recv()
        sent = [net.send(mt.at[x], mt.at[x], net.go(x=d)) for d in (1, 2, 3)]
        last = [net.send(mt.at[x], mtp.at[x], to_c)]
        yield
        for d in (1, 2, 3):
            sent[d - 1].wait_recv()
            spot = (x + 4 - d) % 4
            last.append(net.send(mt.at[spot], mtp.at[spot], to_c))
        yield
        for copy in last:
            copy.wait_recv()

    def plane(i):
        zz = gather.planes[i]
        gather.here(i)
        left = jnp.concatenate([xg[zz, j, k] for j in range(4) for k in range(2)], axis=1)
        right = jnp.concatenate([wq[j, zz].reshape(DD, HD) for j in range(3)], axis=1)
        term = nn(left, right)
        acc[...] = term if i == 0 else acc[...] + term

    product = weight_product()
    gather = Gather(net, xg)
    next(product)
    gather.begin()
    partner_in = net.send(wit, witp, to_c)
    spot = net.count
    partner_out = net.make(wop, wop, to_c)
    for i in range(16):
        cols = pl.ds(pl.multiple_of((2 * i + 1 - c) * HD, HD), HD)
        pltpu.make_async_remote_copy(
            src_ref=wout_hbm.at[:, cols],
            dst_ref=wop.at[i],
            send_sem=send_sems.at[spot],
            recv_sem=recv_sems.at[spot],
            device_id=to_c,
            device_id_type=MESH,
        ).start()
    net.open.append(partner_out)

    next(product)
    gather.along_z()
    next(product)
    gather.turn(0)
    gather.far_z()
    gather.turn(1)
    gather.turn(2)
    gather.land(0)
    next(product)
    gather.turn(3)
    gather.land(1)
    gather.land(2)
    loads["w_qkv"].wait()
    plane(0)
    next(product)
    plane(1)
    gather.land(3)
    plane(2)
    plane(3)

    partner_qkv = []

    def swap_qkv(j):
        partner_qkv.append(net.send(wqkv_hbm.at[j, every, every, 1 - c], wqp.at[j], to_c))

    query = acc[:, :HD].astype(BF16)
    key_rows = acc[:, HD : 2 * HD].astype(BF16)
    value = acc[:, 2 * HD :].astype(BF16)
    qs[...] = query
    ks[...] = key_rows
    vs[...] = value
    loads["mask"].wait()
    row = lax.broadcasted_iota(jnp.int32, (L, L), 0)
    col = lax.broadcasted_iota(jnp.int32, (L, L), 1)
    allowed = (col <= row) & ((maskv[...] == 1) | (col == row))
    scores = jnp.where(allowed, nt(query, key_rows) * scale, -1e30)
    next(product)
    raised = jnp.exp(scores - jnp.max(scores, axis=-1, keepdims=True))
    probs = raised / jnp.sum(raised, axis=-1, keepdims=True)
    probs_s[...] = probs
    hp[0] = nn(probs.astype(BF16), value).astype(BF16)
    heads_copy = net.send(hp.at[0], hp.at[1], to_c)
    partner_in.wait_recv()
    heads_copy.wait_recv()

    next(product, None)

    left = jnp.concatenate([hp[0], hp[1], xg[z, y, c], xg[z, y, 1 - c]], axis=1)
    right = jnp.concatenate(
        [mt[...].reshape(DD, HD), mtp[...].reshape(DD, HD), wit[...], witp[...]], axis=1
    )
    term = nt(left, right)
    for k in range(8):
        pf[pl.ds(k, L, stride=8), :] = term[:, k * HD : (k + 1) * HD]
    for i in range(4):
        for j in range(4):
            rows = pl.ds(pl.multiple_of((8 * i + 2 * j + c) * ROWS, 8), ROWS)
            p2[j, i] = pf[rows, :].astype(BF16)
    sent = [net.send(p2.at[(y + d) % 4], pyb.at[d - 1], net.go(y=d)) for d in (1, 2, 3)]
    swap_qkv(0)

    def fill_out(yy, pair):
        left = jnp.concatenate([hp[0], hp[1]], axis=1)
        right = []
        for zz in pair:
            col0 = pl.multiple_of((zz * 8 + yy * 2 + c) * HD, HD)
            right.append(jnp.concatenate([wo[:, pl.ds(col0, HD)], wop[zz * 4 + yy]], axis=0))
        term = nn(left, jnp.concatenate(right, axis=1)).astype(BF16)
        p1[pair[0], yy] = term[:, :HD]
        p1[pair[1], yy] = term[:, HD:]

    def keep_hidden(summed):
        hid[...] = (xg[z, y, c].astype(F32) + summed).astype(BF16)

    outward = scatter_ring(net, p1, fill_out, bufs1, keep_hidden, ahead=True)
    partner_out.wait_recv()
    next(outward)
    total = p2[y].astype(F32)
    for d in range(3):
        sent[d].wait_recv()
        total += pyb[d].astype(F32)
    pq[...] = total.astype(BF16)
    sent = [net.send(pq.at[(z + d) % 4], pzb.at[d - 1], net.go(z=d)) for d in (1, 2, 3)]
    swap_qkv(1)
    net.drain(8)

    next(outward)
    total = pq[z].astype(F32)
    for d in range(3):
        sent[d].wait_recv()
        total += pzb[d].astype(F32)
    pr[...] = total
    swap_qkv(2)

    for name in ("step", "gain", "cot"):
        loads[name].wait()
    gains = gainv[...].astype(F32)[None]
    proj = jnp.concatenate([pr[pl.ds(k, FR, stride=8), :] for k in range(8)], axis=1)
    grad_rows = jnp.zeros((FR, DD), F32)
    gain_rows = jnp.zeros((FR, DD), F32)
    for s in range(STEPS):
        inner = proj + stepv[s : s + 1, :].astype(F32)
        inverse = lax.rsqrt(jnp.mean(inner * inner, axis=-1, keepdims=True) + 1e-06)
        arriving = cot[s].astype(F32)
        gain_rows += arriving * inner * inverse
        scaled = arriving * gains
        mixed = jnp.mean(inner * scaled, axis=-1, keepdims=True)
        grad_inner = inverse * scaled - inverse * inverse * inverse * inner * mixed
        grad_rows += grad_inner
        rows_s[s : s + 1, :] = jnp.sum(grad_inner, axis=0, keepdims=True)
    for k in range(8):
        gpf[pl.ds(k, FR, stride=8), :] = grad_rows[:, k * HD : (k + 1) * HD]
    gpg[z, y, c] = gpf[...].astype(BF16)

    sent = [net.send(gpg.at[z, y, c], gpg.at[z, y, c], net.go(z=d)) for d in (1, 2, 3)]
    next(outward)
    net.drain(20)
    rows_s[STEPS : STEPS + 1, :] = jnp.sum(gain_rows, axis=0, keepdims=True)
    for k in range(8):
        cols = slice(k * HD, (k + 1) * HD)
        j, i = k // 2, 2 * (k % 2)
        sst[j, i] = rows_s[:16, cols]
        sst[j, i + 1] = jnp.zeros((16, HD), F32)
        sst[j, i + 1, 0:2] = rows_s[16:18, cols]

    def small_sums():
        sent = [net.send(sst.at[(y + d) % 4], syb.at[d - 1], net.go(y=d)) for d in (1, 2, 3)]
        yield
        total = sst[y]
        for d in range(3):
            sent[d].wait_recv()
            total += syb[d]
        sm1[...] = total
        sent = [net.send(sm1.at[(x + d) % 4], sxb.at[d - 1], net.go(x=d)) for d in (1, 2, 3)]
        yield
        total = sm1[x]
        for d in range(3):
            sent[d].wait_recv()
            total += sxb[d]
        szb[z] = total
        sent = [net.send(szb.at[z], szb.at[z], net.go(z=d)) for d in (1, 2, 3)]
        yield
        for copy in sent:
            copy.wait_recv()
        slb[zl] = szb[0] + szb[1] + szb[2] + szb[3]
        sent = [net.send(slb.at[zl], slb.at[zl], net.go(zl=d)) for d in (1, 2, 3)]
        yield
        for copy in sent:
            copy.wait_recv()
        scb[c] = slb[0] + slb[1] + slb[2] + slb[3]
        other = net.send(scb.at[c], scb.at[c], to_c)
        yield
        other.wait_recv()
        sfin[y, x] = scb[0] + scb[1]
        sent = [net.send(sfin.at[y, x], sfin.at[y, x], net.go(x=d)) for d in (1, 2, 3)]
        yield
        for copy in sent:
            copy.wait_recv()
        sent = [net.send(sfin.at[y], sfin.at[y], net.go(y=d)) for d in (1, 2, 3)]
        yield
        for copy in sent:
            copy.wait_recv()
        for k in range(8):
            cols = slice(k * HD, (k + 1) * HD)
            j, i = k // 2, 2 * (k % 2)
            gs_ref[0:16, cols] = sfin[j, i]
            gs_ref[16:17, cols] = sfin[j, i + 1, 0:1]
            gg_ref[0:1, cols] = sfin[j, i + 1, 1:2]

    def weight_sums():
        grads = tn(hid[...], gpn[...]).astype(BF16)
        for k in range(8):
            cols = slice(k * HD, (k + 1) * HD)
            wst[2 * k] = grads[:64, cols]
            wst[2 * k + 1] = grads[64:, cols]
        sent = []
        for d in (1, 2, 3):
            rows = pl.ds(4 * ((x + d) % 4), 4)
            sent.append(net.send(wst.at[rows], wxb.at[d - 1], net.go(x=d)))
        yield
        total = wst[pl.ds(4 * x, 4)].astype(F32)
        for d in range(3):
            sent[d].wait_recv()
            total += wxb[d].astype(F32)
        wsm[...] = total.astype(BF16)
        sent = [net.send(wsm.at[(zl + d) % 4], wzb.at[d - 1], net.go(zl=d)) for d in (1, 2, 3)]
        yield
        total = wsm[zl].astype(F32)
        for d in range(3):
            sent[d].wait_recv()
            total += wzb[d].astype(F32)
        spot = 4 * x + zl
        wfin[spot] = total.astype(BF16)
        sent = [net.send(wfin.at[spot], wfin.at[spot], net.go(zl=d)) for d in (1, 2, 3)]
        yield
        for copy in sent:
            copy.wait_recv()
        rows = pl.ds(4 * x, 4)
        sent = [net.send(wfin.at[rows], wfin.at[rows], net.go(x=d)) for d in (1, 2, 3)]
        yield
        for copy in sent:
            copy.wait_recv()
        for k in range(8):
            cols = slice(k * HD, (k + 1) * HD)
            gw_ref[0:64, cols] = wfin[2 * k]
            gw_ref[64:128, cols] = wfin[2 * k + 1]

    for copy in sent:
        copy.wait_recv()
    sent = [net.send(gpg.at[every, y, c], gpg.at[every, y, c], net.go(y=d)) for d in (1, 2, 3)]
    next(outward)
    net.drain(16)
    for copy in sent:
        copy.wait_recv()
    other = net.send(gpg.at[every, every, c], gpg.at[every, every, c], to_c)
    small = small_sums()
    next(small)
    next(outward)
    net.drain(12)
    other.wait_recv()
    gpr[...] = gpg[...].reshape(32 * ROWS, HD).astype(F32)
    for k in range(8):
        gpn[:, k * HD : (k + 1) * HD] = gpr[pl.ds(k, L, stride=8), :].astype(BF16)
    back = nn(gpn[...], jnp.concatenate([mt[...].reshape(DD, HD), wit[...]], axis=1))
    ghs[...] = back[:, HD:].astype(BF16)
    next(outward)

    grad_heads = back[:, :HD].astype(BF16)
    probs = probs_s[...]
    grad_probs = nt(grad_heads, vs[...])
    inside = jnp.sum(probs * grad_probs, axis=-1, keepdims=True)
    grad_scores = (probs * (grad_probs - inside) * scale).astype(BF16)
    gr[0, 0] = nn(grad_scores, ks[...]).astype(BF16)
    gr[0, 1] = tn(grad_scores, qs[...]).astype(BF16)
    gr[0, 2] = tn(probs.astype(BF16), grad_heads).astype(BF16)
    grads_copy = net.send(gr.at[0], gr.at[1], to_c)
    next(outward)
    next(small)
    sums = weight_sums()
    for copy in partner_qkv:
        copy.wait_recv()
    grads_copy.wait_recv()

    def fill_in(yy, pair):
        left = jnp.concatenate([gr[i, j] for i in range(2) for j in range(3)], axis=1)
        right = []
        for zz in pair:
            right.append(
                jnp.concatenate(
                    [wq[j, zz, yy, c] for j in range(3)] + [wqp[j, zz, yy] for j in range(3)],
                    axis=1,
                )
            )
        term = nt(left, jnp.concatenate(right, axis=0)).astype(BF16)
        p3[pair[0], yy] = term[:, :HD]
        p3[pair[1], yy] = term[:, HD:]

    def keep_grad(summed):
        gx_ref[...] = (ghs[...].astype(F32) + summed).astype(BF16)

    for i, _ in enumerate(scatter_ring(net, p3, fill_in, bufs2, keep_grad)):
        if i == 0:
            next(outward, None)
        if i < 4:
            next(sums)
        next(small, None)
        net.drain(24)
    for _ in small:
        pass
    for _ in sums:
        pass
    net.drain()


def hand_out(*refs):
    sems = refs[8]
    copies = [pltpu.make_async_copy(refs[i], refs[4 + i], sems.at[i]) for i in range(4)]
    for copy in copies:
        copy.start()
    for copy in copies:
        copy.wait()


def ring_buffers():
    return [
        pltpu.VMEM((4, HALF, HD), BF16),
        pltpu.VMEM((4, HALF, HD), BF16),
        pltpu.VMEM((4, L, HD), BF16),
        pltpu.VMEM((4, L, HD), BF16),
        pltpu.VMEM((3, L, HD), BF16),
        pltpu.VMEM((HALF, HD), BF16),
        pltpu.VMEM((HALF, HD), BF16),
        pltpu.VMEM((L, HD), BF16),
        pltpu.VMEM((L, HD), BF16),
    ]


def shards(layer_input, frame_mask, w_qkv, w_out, w_in, step_embed, depth_gain, cotangent):
    def v(*shape, kind=BF16):
        return pltpu.VMEM(shape, kind)

    vmem = pl.BlockSpec(memory_space=pltpu.VMEM)
    hbm = pl.BlockSpec(memory_space=pltpu.HBM)
    scratch = [
        v(4, 4, 2, L, HD),
        v(1, L, kind=jnp.int32),
        v(STEPS, DD),
        v(DD),
        v(3, 4, 4, 2, HD, HD),
        v(3, 4, 4, HD, HD),
        v(HD, 32 * HD),
        v(16, HD, HD),
        v(HD, DD),
        v(DD, HD),
        v(DD, HD),
        v(STEPS, FR, DD),
        v(4, 4, 2, PIECE, HD),
        v(4, 4, PIECE, HD),
        v(4, 4, PIECE, HD),
        v(L, 3 * HD, kind=F32),
        v(L, HD),
        v(L, HD),
        v(L, HD),
        v(L, L, kind=F32),
        v(2, L, HD),
        v(4, 4, L, HD),
        v(L, HD),
        v(32 * ROWS, HD, kind=F32),
        v(4, 4, ROWS, HD),
        v(3, 4, ROWS, HD),
        v(4, ROWS, HD),
        v(3, ROWS, HD),
        v(ROWS, HD, kind=F32),
        v(ROWS, HD, kind=F32),
        v(4, 4, 2, ROWS, HD),
        v(32 * ROWS, HD, kind=F32),
        v(L, DD),
        v(L, HD),
        v(4, 4, L, HD),
        v(2, 3, L, HD),
        v(24, DD, kind=F32),
        v(16, 64, HD),
        v(3, 4, 64, HD),
        v(4, 64, HD),
        v(3, 64, HD),
        v(16, 64, HD),
        v(4, 4, 16, HD, kind=F32),
        v(3, 4, 16, HD, kind=F32),
        v(4, 16, HD, kind=F32),
        v(3, 16, HD, kind=F32),
        v(4, 16, HD, kind=F32),
        v(4, 16, HD, kind=F32),
        v(2, 16, HD, kind=F32),
        v(4, 4, 16, HD, kind=F32),
        *ring_buffers(),
        *ring_buffers(),
        pltpu.SemaphoreType.DMA((N_SEM,)),
        pltpu.SemaphoreType.DMA((N_SEM,)),
        pltpu.SemaphoreType.DMA((8,)),
    ]
    grad_x, grad_in, grad_step, grad_gain = pl.pallas_call(
        kernel,
        out_shape=(
            pltpu.VMEM((L, HD), BF16),
            pltpu.VMEM((HD, DD), BF16),
            pltpu.VMEM((STEPS, DD), F32),
            pltpu.VMEM((1, DD), F32),
        ),
        in_specs=[hbm] * 8,
        out_specs=(vmem,) * 4,
        scratch_shapes=scratch,
        compiler_params=pltpu.CompilerParams(
            collective_id=0, has_side_effects=True, vmem_limit_bytes=60 * 1024 * 1024
        ),
    )(
        layer_input[0],
        frame_mask,
        step_embed,
        depth_gain,
        w_qkv.reshape(3, 4, 4, 2, HD, HD),
        w_out,
        w_in,
        jnp.transpose(cotangent[0], (1, 0, 2)),
    )
    grad_x, grad_in, grad_step, grad_gain = pl.pallas_call(
        hand_out,
        out_shape=(
            jax.ShapeDtypeStruct((L, HD), BF16),
            jax.ShapeDtypeStruct((HD, DD), BF16),
            jax.ShapeDtypeStruct((STEPS, DD), F32),
            jax.ShapeDtypeStruct((1, DD), F32),
        ),
        in_specs=[vmem] * 4,
        out_specs=(hbm,) * 4,
        scratch_shapes=[pltpu.SemaphoreType.DMA((4,))],
        compiler_params=pltpu.CompilerParams(vmem_limit_bytes=2 * 1024 * 1024),
    )(grad_x, grad_in, grad_step, grad_gain)
    return (grad_x[None], grad_in, grad_step, grad_gain[0])


def solution(mesh):
    return jax.shard_map(
        shards,
        mesh=mesh,
        in_specs=(
            P("dp", None, "tensor"),
            P("dp", None),
            P(None, None, "tensor"),
            P("tensor", None),
            P("tensor", None),
            P(),
            P(),
            P("dp", "tensor", None, None),
        ),
        out_specs=(P("dp", None, "tensor"), P("tensor", None), P(), P()),
        check_vma=False,
    )
```

```python
import functools

import jax
import jax.numpy as jnp
from jax import lax
from jax.experimental import pallas as pl
from jax.experimental.pallas import tpu as pltpu
from jax.sharding import PartitionSpec as P

MESH = pl.DeviceIdType.MESH
F32 = jnp.float32
BF16 = jnp.bfloat16
L, HD, DD, STEPS, FR = 192, 128, 1024, 17, 6
HALF = L // 2
LO, HI = pl.ds(0, HALF), pl.ds(HALF, HALF)
ROWS = FR * (DD // HD)
PIECE = 64
N_SEM = 200


def nt(a, b):
    return lax.dot_general(a, b, (((1,), (1,)), ((), ())), preferred_element_type=F32)


def nn(a, b):
    return lax.dot_general(a, b, (((1,), (0,)), ((), ())), preferred_element_type=F32)


def tn(a, b):
    return lax.dot_general(a, b, (((0,), (0,)), ((), ())), preferred_element_type=F32)


def around(v):
    return (v + 1) % 4, (v + 3) % 4, (v + 2) % 4


class Net:
    def __init__(self, send_sems, recv_sems):
        self.send_sems, self.recv_sems = send_sems, recv_sems
        self.count = 0
        self.open = []
        dp, t = lax.axis_index("dp"), lax.axis_index("tensor")
        self.dp, self.t = dp, t
        self.x, self.zl = dp // 4, dp % 4
        self.z, self.y, self.c = t // 8, (t // 2) % 4, t % 2

    def go(self, z=0, y=0, c=0, x=0, zl=0):
        dp, t = self.dp, self.t
        if x or zl:
            dp = ((self.x + x) % 4) * 4 + (self.zl + zl) % 4
        if z or y or c:
            cc = (self.c + c) % 2
            t = ((self.z + z) % 4) * 8 + ((self.y + y) % 4) * 2 + cc
        return (dp, t)

    def peers(self):
        found = [self.go(c=1)]
        for d in (1, 2, 3):
            found += [self.go(y=d), self.go(z=d), self.go(x=d), self.go(zl=d)]
        return found

    def make(self, src, dst, peer):
        i = self.count
        self.count += 1
        return pltpu.make_async_remote_copy(
            src_ref=src,
            dst_ref=dst,
            send_sem=self.send_sems.at[i],
            recv_sem=self.recv_sems.at[i],
            device_id=peer,
            device_id_type=MESH,
        )

    def send(self, src, dst, peer):
        copy = self.make(src, dst, peer)
        copy.start()
        self.open.append(copy)
        return copy

    def drain(self, keep=0):
        done = self.open[: len(self.open) - keep]
        for copy in done:
            copy.wait_send()
        self.open = self.open[len(done) :]


class Gather:
    def __init__(self, net, g):
        self.net, self.g = net, g
        self.planes = (net.z, around(net.z)[1], around(net.z)[0], around(net.z)[2])
        self.along, self.forward, self.across = {}, {}, {}
        self.to_yp, self.to_ym, self.to_c = net.go(y=1), net.go(y=3), net.go(c=1)

    def whole(self, zz, yy, peer):
        at = self.g.at[zz, yy, self.net.c]
        return self.net.send(at, at, peer)

    def part(self, zz, yy, rows, peer):
        at = self.g.at[zz, yy, self.net.c, rows]
        return self.net.send(at, at, peer)

    def begin(self):
        z, y = self.net.z, self.net.y
        to_zp, to_zm = self.net.go(z=1), self.net.go(z=3)
        self.up_lo = self.part(z, y, LO, to_zp)
        self.dn_hi = self.part(z, y, HI, to_zm)
        self.up_hi = self.part(z, y, HI, to_zp)
        self.dn_lo = self.part(z, y, LO, to_zm)
        self.spread(0)

    def along_z(self):
        y = self.net.y
        to_zp, to_zm = self.net.go(z=1), self.net.go(z=3)
        self.up_lo.wait_recv()
        self.on = self.part(self.planes[1], y, LO, to_zp)
        self.dn_hi.wait_recv()
        self.back = self.part(self.planes[2], y, HI, to_zm)
        self.up_hi.wait_recv()
        self.spread(1)
        self.dn_lo.wait_recv()
        self.spread(2)

    def far_z(self):
        self.on.wait_recv()
        self.back.wait_recv()
        self.spread(3)

    def spread(self, i):
        zz, y = self.planes[i], self.net.y
        if i == 3:
            self.along[i] = (
                self.part(zz, y, LO, self.to_yp),
                self.part(zz, y, HI, self.to_ym),
                self.part(zz, y, HI, self.to_yp),
                self.part(zz, y, LO, self.to_ym),
            )
        else:
            self.along[i] = (self.whole(zz, y, self.to_yp), self.whole(zz, y, self.to_ym))
        self.across[i] = []
        self.over(i, zz, y)

    def over(self, i, zz, yy):
        if i == 3:
            self.across[i].append(self.whole(zz, yy, self.to_c))

    def turn(self, i):
        zz = self.planes[i]
        yp, ym, _ = around(self.net.y)
        self.along[i][0].wait_recv()
        first = self.part(zz, ym, LO, self.to_yp)
        self.along[i][1].wait_recv()
        second = self.part(zz, yp, HI, self.to_ym)
        self.forward[i] = (first, second)
        for copy in self.along[i][2:]:
            copy.wait_recv()
        self.over(i, zz, ym)
        self.over(i, zz, yp)

    def land(self, i):
        for copy in self.forward[i]:
            copy.wait_recv()
        self.over(i, self.planes[i], around(self.net.y)[2])
        if i < 3:
            at = self.g.at[self.planes[i], pl.ds(0, 4), self.net.c]
            self.across[i].append(self.net.send(at, at, self.to_c))

    def here(self, i):
        for copy in self.across[i]:
            copy.wait_recv()


def scatter_ring(net, p, fill, bufs, done, ahead=False):
    ya, yb, yup, ydn, q, za, zb, zup, zdn = bufs
    z, y = net.z, net.y
    zp, zm, z2 = around(z)
    yp, ym, y2 = around(y)
    to_zp, to_zm, to_yp, to_ym = net.go(z=1), net.go(z=3), net.go(y=1), net.go(y=3)
    order = (z2, zp, zm, z)

    def fill_rows(first, step, count):
        @pl.loop(0, 2 * count)
        def _(k):
            j = k % 2
            yy = (y + first + step * (k // 2)) % 4
            fill(yy, ((z + 2 + j) % 4, (z + 5 - j) % 4))

    far, near = [], [[], [], [], []]
    if ahead:
        fill_rows(0, 1, 4)
        yield
    else:
        fill_rows(2, 0, 1)
    for zz in order:
        a = net.send(p.at[zz, y2, LO], ya.at[zz], to_yp)
        far.append((a, net.send(p.at[zz, y2, HI], yb.at[zz], to_ym)))

    def at_once(i):
        zz = order[i]
        near[i].append(net.send(p.at[zz, yp, HI], yup.at[zz, HI], to_yp))
        near[i].append(net.send(p.at[zz, ym, LO], ydn.at[zz, LO], to_ym))

    if not ahead:
        fill_rows(1, 2, 2)
    for i in range(4):
        at_once(i)
    yield
    for i, zz in enumerate(order):
        far[i][0].wait_recv()
        p[zz, yp, LO] = (p[zz, yp, LO].astype(F32) + ya[zz].astype(F32)).astype(BF16)
        near[i].append(net.send(p.at[zz, yp, LO], yup.at[zz, LO], to_yp))
        far[i][1].wait_recv()
        p[zz, ym, HI] = (p[zz, ym, HI].astype(F32) + yb[zz].astype(F32)).astype(BF16)
        near[i].append(net.send(p.at[zz, ym, HI], ydn.at[zz, HI], to_ym))
    if not ahead:
        fill_rows(0, 0, 1)
    yield

    def mine(i):
        for copy in near[i]:
            copy.wait_recv()
        zz = order[i]
        return p[zz, y].astype(F32) + yup[zz].astype(F32) + ydn[zz].astype(F32)

    q[0] = mine(0).astype(BF16)
    a = net.send(q.at[0, LO], za, to_zp)
    b = net.send(q.at[0, HI], zb, to_zm)
    yield
    q[1] = mine(1).astype(BF16)
    last = [net.send(q.at[1, HI], zup.at[HI], to_zp)]
    q[2] = mine(2).astype(BF16)
    last.append(net.send(q.at[2, LO], zdn.at[LO], to_zm))
    yield
    a.wait_recv()
    q[1, LO] = (q[1, LO].astype(F32) + za[...].astype(F32)).astype(BF16)
    last.append(net.send(q.at[1, LO], zup.at[LO], to_zp))
    b.wait_recv()
    q[2, HI] = (q[2, HI].astype(F32) + zb[...].astype(F32)).astype(BF16)
    last.append(net.send(q.at[2, HI], zdn.at[HI], to_zm))
    yield
    total = mine(3)
    yield
    for copy in last:
        copy.wait_recv()
    done(total + zup[...].astype(F32) + zdn[...].astype(F32))


def kernel(
    x_hbm, mask_hbm, step_hbm, gain_hbm, wqkv_hbm, wout_hbm, win_hbm, cot_hbm,
    gx_ref, gw_ref, gs_ref, gg_ref,
    xg, maskv, stepv, gainv, wq, wqp, wo, wop, wi, wit, witp, cot,
    gm, mt, mtp,
    acc, qs, ks, vs, probs_s, hp, p1, hid, pf, p2, pyb, pq, pzb, pr, gpf,
    gpg, gpr, gpn, ghs, p3, gr, rows_s,
    wst, wxb, wsm, wzb, wfin,
    sst, syb, sm1, sxb, szb, slb, scb, sfin,
    *rest,
):
    bufs1, bufs2 = rest[:9], rest[9:18]
    send_sems, recv_sems, local_sems = rest[18:]
    net = Net(send_sems, recv_sems)
    x, zl, z, y, c = net.x, net.zl, net.z, net.y, net.c
    to_c = net.go(c=1)
    scale = HD ** (-0.5)

    barrier = pltpu.get_barrier_semaphore()
    peers = net.peers()
    for peer in peers:
        pl.semaphore_signal(barrier, inc=1, device_id=peer, device_id_type=MESH)
    loads = {}
    for i, (name, src, dst) in enumerate(
        (
            ("w_in", win_hbm, wi),
            ("x", x_hbm, xg.at[z, y, c]),
            ("w_out", wout_hbm, wo),
            ("w_qkv", wqkv_hbm, wq),
            ("mask", mask_hbm, maskv),
            ("step", step_hbm, stepv),
            ("gain", gain_hbm, gainv),
            ("cot", cot_hbm, cot),
        )
    ):
        loads[name] = pltpu.make_async_copy(src, dst, local_sems.at[i])
        loads[name].start()
    loads["w_in"].wait()
    for k in range(8):
        wit[k * HD : (k + 1) * HD, :] = wi[:, k * HD : (k + 1) * HD].T
    gm[z, y, c] = wit[pl.ds(pl.multiple_of(PIECE * net.dp, PIECE), PIECE), :]
    loads["x"].wait()
    pl.semaphore_wait(barrier, len(peers))

    every = pl.ds(0, 4)

    def weight_product():
        sent = [net.send(gm.at[z, y, c], gm.at[z, y, c], net.go(z=d)) for d in (1, 2, 3)]
        yield
        for copy in sent:
            copy.wait_recv()
        sent = [net.send(gm.at[every, y, c], gm.at[every, y, c], net.go(y=d)) for d in (1, 2, 3)]
        yield
        for copy in sent:
            copy.wait_recv()
        other = net.send(gm.at[every, every, c], gm.at[every, every, c], to_c)
        yield
        other.wait_recv()
        loads["w_out"].wait()
        left = jnp.concatenate(
            [gm[i, j, k] for i in range(4) for j in range(4) for k in range(2)], axis=1
        )
        mt[x, zl] = nt(left, wo[...]).astype(BF16)
        sent = [net.send(mt.at[x, zl], mt.at[x, zl], net.go(zl=d)) for d in (1, 2, 3)]
        yield
        for copy in sent:
            copy.wait_recv()
        sent = [net.send(mt.at[x], mt.at[x], net.go(x=d)) for d in (1, 2, 3)]
        last = [net.send(mt.at[x], mtp.at[x], to_c)]
        yield
        for d in (1, 2, 3):
            sent[d - 1].wait_recv()
            spot = (x + 4 - d) % 4
            last.append(net.send(mt.at[spot], mtp.at[spot], to_c))
        yield
        for copy in last:
            copy.wait_recv()

    def plane(i):
        zz = gather.planes[i]
        gather.here(i)
        left = jnp.concatenate([xg[zz, j, k] for j in range(4) for k in range(2)], axis=1)
        right = jnp.concatenate([wq[j, zz].reshape(DD, HD) for j in range(3)], axis=1)
        term = nn(left, right)
        acc[...] = term if i == 0 else acc[...] + term

    product = weight_product()
    gather = Gather(net, xg)
    next(product)
    gather.begin()
    partner_in = net.send(wit, witp, to_c)
    spot = net.count
    partner_out = net.make(wop, wop, to_c)
    for i in range(16):
        cols = pl.ds(pl.multiple_of((2 * i + 1 - c) * HD, HD), HD)
        pltpu.make_async_remote_copy(
            src_ref=wout_hbm.at[:, cols],
            dst_ref=wop.at[i],
            send_sem=send_sems.at[spot],
            recv_sem=recv_sems.at[spot],
            device_id=to_c,
            device_id_type=MESH,
        ).start()
    net.open.append(partner_out)

    next(product)
    gather.along_z()
    next(product)
    gather.turn(0)
    gather.far_z()
    gather.turn(1)
    gather.turn(2)
    gather.land(0)
    next(product)
    gather.turn(3)
    gather.land(1)
    gather.land(2)
    loads["w_qkv"].wait()
    plane(0)
    next(product)
    plane(1)
    gather.land(3)
    plane(2)
    plane(3)

    partner_qkv = []

    def swap_qkv(j):
        partner_qkv.append(net.send(wqkv_hbm.at[j, every, every, 1 - c], wqp.at[j], to_c))

    query = acc[:, :HD].astype(BF16)
    key_rows = acc[:, HD : 2 * HD].astype(BF16)
    value = acc[:, 2 * HD :].astype(BF16)
    qs[...] = query
    ks[...] = key_rows
    vs[...] = value
    loads["mask"].wait()
    row = lax.broadcasted_iota(jnp.int32, (L, L), 0)
    col = lax.broadcasted_iota(jnp.int32, (L, L), 1)
    allowed = (col <= row) & ((maskv[...] == 1) | (col == row))
    scores = jnp.where(allowed, nt(query, key_rows) * scale, -1e30)
    next(product)
    raised = jnp.exp(scores - jnp.max(scores, axis=-1, keepdims=True))
    probs = raised / jnp.sum(raised, axis=-1, keepdims=True)
    probs_s[...] = probs
    hp[0] = nn(probs.astype(BF16), value).astype(BF16)
    heads_copy = net.send(hp.at[0], hp.at[1], to_c)
    partner_in.wait_recv()
    heads_copy.wait_recv()

    next(product, None)

    left = jnp.concatenate([hp[0], hp[1], xg[z, y, c], xg[z, y, 1 - c]], axis=1)
    right = jnp.concatenate(
        [mt[...].reshape(DD, HD), mtp[...].reshape(DD, HD), wit[...], witp[...]], axis=1
    )
    term = nt(left, right)
    for k in range(8):
        pf[pl.ds(k, L, stride=8), :] = term[:, k * HD : (k + 1) * HD]
    for i in range(4):
        for j in range(4):
            rows = pl.ds(pl.multiple_of((8 * i + 2 * j + c) * ROWS, 8), ROWS)
            p2[j, i] = pf[rows, :].astype(BF16)
    sent = [net.send(p2.at[(y + d) % 4], pyb.at[d - 1], net.go(y=d)) for d in (1, 2, 3)]
    swap_qkv(0)

    def fill_out(yy, pair):
        left = jnp.concatenate([hp[0], hp[1]], axis=1)
        right = []
        for zz in pair:
            col0 = pl.multiple_of((zz * 8 + yy * 2 + c) * HD, HD)
            right.append(jnp.concatenate([wo[:, pl.ds(col0, HD)], wop[zz * 4 + yy]], axis=0))
        term = nn(left, jnp.concatenate(right, axis=1)).astype(BF16)
        p1[pair[0], yy] = term[:, :HD]
        p1[pair[1], yy] = term[:, HD:]

    def keep_hidden(summed):
        hid[...] = (xg[z, y, c].astype(F32) + summed).astype(BF16)

    outward = scatter_ring(net, p1, fill_out, bufs1, keep_hidden, ahead=True)
    partner_out.wait_recv()
    next(outward)
    total = p2[y].astype(F32)
    for d in range(3):
        sent[d].wait_recv()
        total += pyb[d].astype(F32)
    pq[...] = total.astype(BF16)
    sent = [net.send(pq.at[(z + d) % 4], pzb.at[d - 1], net.go(z=d)) for d in (1, 2, 3)]
    swap_qkv(1)
    net.drain(8)

    next(outward)
    total = pq[z].astype(F32)
    for d in range(3):
        sent[d].wait_recv()
        total += pzb[d].astype(F32)
    pr[...] = total
    swap_qkv(2)

    for name in ("step", "gain", "cot"):
        loads[name].wait()
    gains = gainv[...].astype(F32)[None]
    proj = jnp.concatenate([pr[pl.ds(k, FR, stride=8), :] for k in range(8)], axis=1)
    grad_rows = jnp.zeros((FR, DD), F32)
    gain_rows = jnp.zeros((FR, DD), F32)
    for s in range(STEPS):
        inner = proj + stepv[s : s + 1, :].astype(F32)
        inverse = lax.rsqrt(jnp.mean(inner * inner, axis=-1, keepdims=True) + 1e-06)
        arriving = cot[s].astype(F32)
        gain_rows += arriving * inner * inverse
        scaled = arriving * gains
        mixed = jnp.mean(inner * scaled, axis=-1, keepdims=True)
        grad_inner = inverse * scaled - inverse * inverse * inverse * inner * mixed
        grad_rows += grad_inner
        rows_s[s : s + 1, :] = jnp.sum(grad_inner, axis=0, keepdims=True)
    for k in range(8):
        gpf[pl.ds(k, FR, stride=8), :] = grad_rows[:, k * HD : (k + 1) * HD]
    gpg[z, y, c] = gpf[...].astype(BF16)

    sent = [net.send(gpg.at[z, y, c], gpg.at[z, y, c], net.go(z=d)) for d in (1, 2, 3)]
    next(outward)
    net.drain(20)
    rows_s[STEPS : STEPS + 1, :] = jnp.sum(gain_rows, axis=0, keepdims=True)
    for k in range(8):
        cols = slice(k * HD, (k + 1) * HD)
        j, i = k // 2, 2 * (k % 2)
        sst[j, i] = rows_s[:16, cols]
        sst[j, i + 1] = jnp.zeros((16, HD), F32)
        sst[j, i + 1, 0:2] = rows_s[16:18, cols]

    def small_sums():
        sent = [net.send(sst.at[(y + d) % 4], syb.at[d - 1], net.go(y=d)) for d in (1, 2, 3)]
        yield
        total = sst[y]
        for d in range(3):
            sent[d].wait_recv()
            total += syb[d]
        sm1[...] = total
        sent = [net.send(sm1.at[(x + d) % 4], sxb.at[d - 1], net.go(x=d)) for d in (1, 2, 3)]
        yield
        total = sm1[x]
        for d in range(3):
            sent[d].wait_recv()
            total += sxb[d]
        szb[z] = total
        sent = [net.send(szb.at[z], szb.at[z], net.go(z=d)) for d in (1, 2, 3)]
        yield
        for copy in sent:
            copy.wait_recv()
        slb[zl] = szb[0] + szb[1] + szb[2] + szb[3]
        sent = [net.send(slb.at[zl], slb.at[zl], net.go(zl=d)) for d in (1, 2, 3)]
        yield
        for copy in sent:
            copy.wait_recv()
        scb[c] = slb[0] + slb[1] + slb[2] + slb[3]
        other = net.send(scb.at[c], scb.at[c], to_c)
        yield
        other.wait_recv()
        sfin[y, x] = scb[0] + scb[1]
        sent = [net.send(sfin.at[y, x], sfin.at[y, x], net.go(x=d)) for d in (1, 2, 3)]
        yield
        for copy in sent:
            copy.wait_recv()
        sent = [net.send(sfin.at[y], sfin.at[y], net.go(y=d)) for d in (1, 2, 3)]
        yield
        for copy in sent:
            copy.wait_recv()
        for k in range(8):
            cols = slice(k * HD, (k + 1) * HD)
            j, i = k // 2, 2 * (k % 2)
            gs_ref[0:16, cols] = sfin[j, i]
            gs_ref[16:17, cols] = sfin[j, i + 1, 0:1]
            gg_ref[0:1, cols] = sfin[j, i + 1, 1:2]

    def weight_sums():
        grads = tn(hid[...], gpn[...]).astype(BF16)
        for k in range(8):
            cols = slice(k * HD, (k + 1) * HD)
            wst[2 * k] = grads[:64, cols]
            wst[2 * k + 1] = grads[64:, cols]
        sent = []
        for d in (1, 2, 3):
            rows = pl.ds(4 * ((x + d) % 4), 4)
            sent.append(net.send(wst.at[rows], wxb.at[d - 1], net.go(x=d)))
        yield
        total = wst[pl.ds(4 * x, 4)].astype(F32)
        for d in range(3):
            sent[d].wait_recv()
            total += wxb[d].astype(F32)
        wsm[...] = total.astype(BF16)
        sent = [net.send(wsm.at[(zl + d) % 4], wzb.at[d - 1], net.go(zl=d)) for d in (1, 2, 3)]
        yield
        total = wsm[zl].astype(F32)
        for d in range(3):
            sent[d].wait_recv()
            total += wzb[d].astype(F32)
        spot = 4 * x + zl
        wfin[spot] = total.astype(BF16)
        sent = [net.send(wfin.at[spot], wfin.at[spot], net.go(zl=d)) for d in (1, 2, 3)]
        yield
        for copy in sent:
            copy.wait_recv()
        rows = pl.ds(4 * x, 4)
        sent = [net.send(wfin.at[rows], wfin.at[rows], net.go(x=d)) for d in (1, 2, 3)]
        yield
        for copy in sent:
            copy.wait_recv()
        for k in range(8):
            cols = slice(k * HD, (k + 1) * HD)
            gw_ref[0:64, cols] = wfin[2 * k]
            gw_ref[64:128, cols] = wfin[2 * k + 1]

    for copy in sent:
        copy.wait_recv()
    sent = [net.send(gpg.at[every, y, c], gpg.at[every, y, c], net.go(y=d)) for d in (1, 2, 3)]
    next(outward)
    net.drain(16)
    for copy in sent:
        copy.wait_recv()
    other = net.send(gpg.at[every, every, c], gpg.at[every, every, c], to_c)
    small = small_sums()
    next(small)
    next(outward)
    net.drain(12)
    other.wait_recv()
    gpr[...] = gpg[...].reshape(32 * ROWS, HD).astype(F32)
    for k in range(8):
        gpn[:, k * HD : (k + 1) * HD] = gpr[pl.ds(k, L, stride=8), :].astype(BF16)
    back = nn(gpn[...], jnp.concatenate([mt[...].reshape(DD, HD), wit[...]], axis=1))
    ghs[...] = back[:, HD:].astype(BF16)
    next(outward)

    grad_heads = back[:, :HD].astype(BF16)
    probs = probs_s[...]
    grad_probs = nt(grad_heads, vs[...])
    inside = jnp.sum(probs * grad_probs, axis=-1, keepdims=True)
    grad_scores = (probs * (grad_probs - inside) * scale).astype(BF16)
    gr[0, 0] = nn(grad_scores, ks[...]).astype(BF16)
    gr[0, 1] = tn(grad_scores, qs[...]).astype(BF16)
    gr[0, 2] = tn(probs.astype(BF16), grad_heads).astype(BF16)
    grads_copy = net.send(gr.at[0], gr.at[1], to_c)
    next(outward)
    next(small)
    next(outward, None)
    sums = weight_sums()
    next(sums)
    for copy in partner_qkv:
        copy.wait_recv()
    grads_copy.wait_recv()

    def fill_in(yy, pair):
        left = jnp.concatenate([gr[i, j] for i in range(2) for j in range(3)], axis=1)
        right = []
        for zz in pair:
            right.append(
                jnp.concatenate(
                    [wq[j, zz, yy, c] for j in range(3)] + [wqp[j, zz, yy] for j in range(3)],
                    axis=1,
                )
            )
        term = nt(left, jnp.concatenate(right, axis=0)).astype(BF16)
        p3[pair[0], yy] = term[:, :HD]
        p3[pair[1], yy] = term[:, HD:]

    def keep_grad(summed):
        gx_ref[...] = (ghs[...].astype(F32) + summed).astype(BF16)

    for i, _ in enumerate(scatter_ring(net, p3, fill_in, bufs2, keep_grad)):
        if 1 <= i < 4:
            next(sums)
        next(small, None)
        net.drain(24)
    for _ in small:
        pass
    for _ in sums:
        pass
    net.drain()


def hand_out(*refs):
    sems = refs[8]
    copies = [pltpu.make_async_copy(refs[i], refs[4 + i], sems.at[i]) for i in range(4)]
    for copy in copies:
        copy.start()
    for copy in copies:
        copy.wait()


def ring_buffers():
    return [
        pltpu.VMEM((4, HALF, HD), BF16),
        pltpu.VMEM((4, HALF, HD), BF16),
        pltpu.VMEM((4, L, HD), BF16),
        pltpu.VMEM((4, L, HD), BF16),
        pltpu.VMEM((3, L, HD), BF16),
        pltpu.VMEM((HALF, HD), BF16),
        pltpu.VMEM((HALF, HD), BF16),
        pltpu.VMEM((L, HD), BF16),
        pltpu.VMEM((L, HD), BF16),
    ]


def shards(layer_input, frame_mask, w_qkv, w_out, w_in, step_embed, depth_gain, cotangent):
    def v(*shape, kind=BF16):
        return pltpu.VMEM(shape, kind)

    vmem = pl.BlockSpec(memory_space=pltpu.VMEM)
    hbm = pl.BlockSpec(memory_space=pltpu.HBM)
    scratch = [
        v(4, 4, 2, L, HD),
        v(1, L, kind=jnp.int32),
        v(STEPS, DD),
        v(DD),
        v(3, 4, 4, 2, HD, HD),
        v(3, 4, 4, HD, HD),
        v(HD, 32 * HD),
        v(16, HD, HD),
        v(HD, DD),
        v(DD, HD),
        v(DD, HD),
        v(STEPS, FR, DD),
        v(4, 4, 2, PIECE, HD),
        v(4, 4, PIECE, HD),
        v(4, 4, PIECE, HD),
        v(L, 3 * HD, kind=F32),
        v(L, HD),
        v(L, HD),
        v(L, HD),
        v(L, L, kind=F32),
        v(2, L, HD),
        v(4, 4, L, HD),
        v(L, HD),
        v(32 * ROWS, HD, kind=F32),
        v(4, 4, ROWS, HD),
        v(3, 4, ROWS, HD),
        v(4, ROWS, HD),
        v(3, ROWS, HD),
        v(ROWS, HD, kind=F32),
        v(ROWS, HD, kind=F32),
        v(4, 4, 2, ROWS, HD),
        v(32 * ROWS, HD, kind=F32),
        v(L, DD),
        v(L, HD),
        v(4, 4, L, HD),
        v(2, 3, L, HD),
        v(24, DD, kind=F32),
        v(16, 64, HD),
        v(3, 4, 64, HD),
        v(4, 64, HD),
        v(3, 64, HD),
        v(16, 64, HD),
        v(4, 4, 16, HD, kind=F32),
        v(3, 4, 16, HD, kind=F32),
        v(4, 16, HD, kind=F32),
        v(3, 16, HD, kind=F32),
        v(4, 16, HD, kind=F32),
        v(4, 16, HD, kind=F32),
        v(2, 16, HD, kind=F32),
        v(4, 4, 16, HD, kind=F32),
        *ring_buffers(),
        *ring_buffers(),
        pltpu.SemaphoreType.DMA((N_SEM,)),
        pltpu.SemaphoreType.DMA((N_SEM,)),
        pltpu.SemaphoreType.DMA((8,)),
    ]
    grad_x, grad_in, grad_step, grad_gain = pl.pallas_call(
        kernel,
        out_shape=(
            pltpu.VMEM((L, HD), BF16),
            pltpu.VMEM((HD, DD), BF16),
            pltpu.VMEM((STEPS, DD), F32),
            pltpu.VMEM((1, DD), F32),
        ),
        in_specs=[hbm] * 8,
        out_specs=(vmem,) * 4,
        scratch_shapes=scratch,
        compiler_params=pltpu.CompilerParams(
            collective_id=0, has_side_effects=True, vmem_limit_bytes=60 * 1024 * 1024
        ),
    )(
        layer_input[0],
        frame_mask,
        step_embed,
        depth_gain,
        w_qkv.reshape(3, 4, 4, 2, HD, HD),
        w_out,
        w_in,
        jnp.transpose(cotangent[0], (1, 0, 2)),
    )
    grad_x, grad_in, grad_step, grad_gain = pl.pallas_call(
        hand_out,
        out_shape=(
            jax.ShapeDtypeStruct((L, HD), BF16),
            jax.ShapeDtypeStruct((HD, DD), BF16),
            jax.ShapeDtypeStruct((STEPS, DD), F32),
            jax.ShapeDtypeStruct((1, DD), F32),
        ),
        in_specs=[vmem] * 4,
        out_specs=(hbm,) * 4,
        scratch_shapes=[pltpu.SemaphoreType.DMA((4,))],
        compiler_params=pltpu.CompilerParams(vmem_limit_bytes=2 * 1024 * 1024),
    )(grad_x, grad_in, grad_step, grad_gain)
    return (grad_x[None], grad_in, grad_step, grad_gain[0])


def solution(mesh):
    return jax.shard_map(
        shards,
        mesh=mesh,
        in_specs=(
            P("dp", None, "tensor"),
            P("dp", None),
            P(None, None, "tensor"),
            P("tensor", None),
            P("tensor", None),
            P(),
            P(),
            P("dp", "tensor", None, None),
        ),
        out_specs=(P("dp", None, "tensor"), P("tensor", None), P(), P()),
        check_vma=False,
    )
```
